32 devices in a mesh: seq: 8 (over y, x, core), section: 4 (over z).
Axes of the slice: x: 2, y: 2, z: 4, core: 2. Of those that a mesh axis runs over, the one named last changes fastest.
Arguments:
- queries: bfloat16 [4, 1024, 2048], P('section', 'seq'), may hold values from -60 to 60
- keys_in: bfloat16 [4, 1024, 2048], P('section', 'seq'), may hold values from -15 to 15
- values: bfloat16 [4, 1024, 2048], P('section', 'seq'), may hold values from -6 to 6
- out_grads: bfloat16 [4, 1024, 2048], P('section', 'seq'), may hold values from -6 to 6
- offsets: int32 [3, 16], replicated, may hold values from 0 to 7
Outputs:
- grad_queries: bfloat16 [4, 1024, 2048], P('section', 'seq')
- grad_keys: bfloat16 [4, 1024, 2048], P('section', 'seq')
- grad_values: bfloat16 [4, 1024, 2048], P('section', 'seq')
The draws below stay inside these ranges and needn't reach their ends.
Inputs may be any that keep to these rules, and one draw needn't show every extreme that they name: Level l uses offsets[l - 1, h] modulo 2^l.
All inputs are finite; a program needn't handle non-finite values.
Results may differ from the reference program's by a relative error of at most 0.029.
Values may be sent and summed in bfloat16 or wider, within the bound.
No kernel may reach another device: no remote copies, remote signals or barrier semaphores. Data moves between devices by JAX's collectives and lax.ppermute only.
A program may use at most 64 MiB of HBM per device.

```python
import jax
import jax.numpy as jnp
from jax import lax

TOK_DEV = 128
HEADS = 16
HEAD_DIM = 128
LEVELS = 3
SECTIONS = 4
TOKENS = 1024
WIDTH = 2048
N_SEQ = 8


def pair_draw(key):
    shape = (SECTIONS, TOKENS, HEADS * HEAD_DIM)
    base_keys = jnp.clip(jax.random.normal(jax.random.fold_in(key, 101), shape, jnp.float32), -6.0, 6.0)
    base_queries = jnp.clip(jax.random.normal(jax.random.fold_in(key, 102), shape, jnp.float32), -6.0, 6.0)
    keys_out = base_keys
    queries_out = base_queries
    return (queries_out, keys_out)


def draw_queries(key, part):
    return pair_draw(key)[0].astype(jnp.bfloat16)


def draw_keys_in(key, part):
    return pair_draw(key)[1].astype(jnp.bfloat16)


def plant(result, key, low, high):
    longest = result.shape.index(max(result.shape))
    spots = []
    for shift in (0, 1):
        where = [jax.random.randint(jax.random.fold_in(key, axis), (), 0, length) for axis, length in enumerate(result.shape)]
        where[longest] = (where[longest] + shift) % result.shape[longest]
        spots.append(tuple(where))
    return result.at[spots[0]].set(low).at[spots[1]].set(high)


def block_scale(stream_key, dims, split, low, top_value):
    gain, own = 1.0, jax.random.fold_in(stream_key, 6)
    for dim, parts in split:
        draws = jnp.exp(jax.random.uniform(jax.random.fold_in(own, dim), (parts,), jnp.float32, low / len(split), top_value / len(split)))
        gain = gain * jnp.repeat(draws, dims[dim] // parts).reshape([-1 if axis == dim else 1 for axis in range(len(dims))])
    return gain


def normal_values(own_key, dims, scale, bound, cuts=(), kind=jnp.bfloat16):
    level = block_scale(own_key, dims, cuts, -0.22, 0.18) if cuts else 1.0
    result = jax.random.normal(own_key, dims, jnp.float32) * scale * level
    return jnp.minimum(jnp.maximum(result, -bound), bound).astype(kind)


def setup_inputs(seed: int = 0) -> dict:
    seeds = jax.random.split(jax.random.key(seed), 6)
    return {
        "queries": draw_queries(jax.random.fold_in(seeds[5], 71), 0),
        "keys_in": draw_keys_in(jax.random.fold_in(seeds[5], 71), 0),
        "values": normal_values(seeds[2], (SECTIONS, TOKENS, WIDTH), 1.0, 6.0, ((0, 4), (1, 8))),
        "out_grads": normal_values(seeds[3], (SECTIONS, TOKENS, WIDTH), 1.0, 6.0, ((0, 4), (1, 8))),
        "offsets": plant(jax.random.randint(seeds[4], (LEVELS, HEADS), 0, 2 ** LEVELS), jax.random.fold_in(seeds[4], 1), 0, (2 ** LEVELS) - 1).astype(jnp.int32),
    }


def pick_rows(tile_rows, dilation, chosen):
    row_count, head_count, head_dim = tile_rows.shape
    shaped = tile_rows.reshape(row_count // dilation, dilation, head_count, head_dim)
    keep_mask = jnp.arange(dilation, dtype=jnp.int32)[None, :, None, None] == (chosen % dilation)[None, None, :, None]
    return jnp.sum(jnp.where(keep_mask, shaped, jnp.zeros((), tile_rows.dtype)), axis=1).astype(tile_rows.dtype)


def spread_rows(row_values, dilation, chosen):
    row_count, head_count, head_dim = row_values.shape
    keep_mask = jnp.arange(dilation, dtype=jnp.int32)[None, :, None, None] == (chosen % dilation)[None, None, :, None]
    spread = jnp.where(keep_mask, row_values[:, None], jnp.zeros((), row_values.dtype))
    return spread.reshape(row_count * dilation, head_count, head_dim)


def pick_stat(row_stat, dilation, chosen):
    head_count, row_count = row_stat.shape
    shaped = row_stat.reshape(head_count, row_count // dilation, dilation)
    keep_mask = jnp.arange(dilation, dtype=jnp.int32)[None, None, :] == (chosen % dilation)[:, None, None]
    return jnp.sum(jnp.where(keep_mask, shaped, 0.0), axis=2)


def spread_stat(row_stat, dilation, chosen, fill_value):
    head_count, row_count = row_stat.shape
    keep_mask = jnp.arange(dilation, dtype=jnp.int32)[None, None, :] == (chosen % dilation)[:, None, None]
    return jnp.where(keep_mask, row_stat[:, :, None], fill_value).reshape(head_count, row_count * dilation)


def block_pass(query_rows, key_rows, value_rows, grad_rows, group_keys, group_values, offsets):
    score_scale = HEAD_DIM ** -0.5
    sel_q = [query_rows]
    sel_g = [grad_rows]
    key_sets = [key_rows]
    value_sets = [value_rows]
    for bit_level in range(LEVELS):
        dilation = 2 ** (bit_level + 1)
        chosen = offsets[bit_level]
        sel_q.append(pick_rows(query_rows, dilation, chosen))
        sel_g.append(pick_rows(grad_rows, dilation, chosen))
        key_sets.append(group_keys[bit_level])
        value_sets.append(group_values[bit_level])
    scores = [jnp.einsum("qhe,khe->hqk", sel_q[i].astype(jnp.float32), key_sets[i].astype(jnp.float32)) * score_scale for i in range(LEVELS + 1)]
    part_lse = [jax.nn.logsumexp(level_scores, axis=-1) for level_scores in scores]
    total_lse = part_lse[0]
    for bit_level in range(LEVELS):
        total_lse = jnp.logaddexp(total_lse, spread_stat(part_lse[bit_level + 1], 2 ** (bit_level + 1), offsets[bit_level], -jnp.inf))
    row_lse = [total_lse] + [pick_stat(total_lse, 2 ** (b + 1), offsets[b]) for b in range(LEVELS)]
    weights = [jnp.exp(scores[i] - row_lse[i][:, :, None]) for i in range(LEVELS + 1)]
    rounded = [w.astype(jnp.bfloat16) for w in weights]
    output = jnp.einsum("hqk,khe->qhe", rounded[0].astype(jnp.float32), value_sets[0].astype(jnp.float32))
    for bit_level in range(LEVELS):
        level_out = jnp.einsum("hqk,khe->qhe", rounded[bit_level + 1].astype(jnp.float32), value_sets[bit_level + 1].astype(jnp.float32))
        output = output + spread_rows(level_out, 2 ** (bit_level + 1), offsets[bit_level])
    delta_rows = jnp.sum(grad_rows.astype(jnp.float32) * output, axis=2).T
    row_delta = [delta_rows] + [pick_stat(delta_rows, 2 ** (b + 1), offsets[b]) for b in range(LEVELS)]
    grad_q = jnp.zeros(query_rows.shape, jnp.float32)
    grad_k = jnp.zeros(query_rows.shape, jnp.float32)
    grad_v = jnp.zeros(query_rows.shape, jnp.float32)
    level_keys = []
    level_values = []
    for level_index in range(LEVELS + 1):
        pgrad = jnp.einsum("qhe,khe->hqk", sel_g[level_index].astype(jnp.float32), value_sets[level_index].astype(jnp.float32))
        dscore = weights[level_index] * (pgrad - row_delta[level_index][:, :, None])
        dround = dscore.astype(jnp.bfloat16).astype(jnp.float32)
        q_part = jnp.einsum("hqk,khe->qhe", dround, key_sets[level_index].astype(jnp.float32)) * score_scale
        key_part = jnp.einsum("hqk,qhe->khe", dround, sel_q[level_index].astype(jnp.float32)) * score_scale
        value_part = jnp.einsum("hqk,qhe->khe", rounded[level_index].astype(jnp.float32), sel_g[level_index].astype(jnp.float32))
        if level_index == 0:
            grad_q = grad_q + q_part
            grad_k = grad_k + key_part
            grad_v = grad_v + value_part
        else:
            grad_q = grad_q + spread_rows(q_part, 2 ** level_index, offsets[level_index - 1])
            level_keys.append(key_part)
            level_values.append(value_part)
    return grad_q, grad_k, grad_v, tuple(level_keys), tuple(level_values)


def reference(queries, keys_in, values, out_grads, offsets):
    tile_shape = (N_SEQ, TOK_DEV, HEADS, HEAD_DIM)
    outs_q = []
    outs_k = []
    outs_v = []
    for section_index in range(SECTIONS):
        query_all = queries[section_index].reshape(tile_shape)
        key_all = keys_in[section_index].reshape(tile_shape)
        value_all = values[section_index].reshape(tile_shape)
        grad_all = out_grads[(section_index + 1) % SECTIONS].reshape(tile_shape)
        group_k = []
        group_v = []
        for bit_level in range(LEVELS):
            dilation = 2 ** (bit_level + 1)
            chosen = offsets[bit_level]
            picker = jax.vmap(lambda tile, dilation=dilation, chosen=chosen: pick_rows(tile, dilation, chosen))
            group_k.append(picker(key_all).reshape(N_SEQ // dilation, TOK_DEV, HEADS, HEAD_DIM))
            group_v.append(picker(value_all).reshape(N_SEQ // dilation, TOK_DEV, HEADS, HEAD_DIM))

        def one_block(block_index, query_all=query_all, key_all=key_all, value_all=value_all, grad_all=grad_all, group_k=group_k, group_v=group_v):
            return block_pass(query_all[block_index], key_all[block_index], value_all[block_index], grad_all[block_index],
                              [group_k[b][block_index // (2 ** (b + 1))] for b in range(LEVELS)],
                              [group_v[b][block_index // (2 ** (b + 1))] for b in range(LEVELS)], offsets)

        grad_q, grad_k, grad_v, level_keys, level_values = lax.map(one_block, jnp.arange(N_SEQ, dtype=jnp.int32))
        for bit_level in range(LEVELS):
            dilation = 2 ** (bit_level + 1)
            chosen = offsets[bit_level]
            placer = jax.vmap(lambda rows, dilation=dilation, chosen=chosen: spread_rows(rows, dilation, chosen))
            summed_k = level_keys[bit_level].reshape(N_SEQ // dilation, dilation, TOK_DEV, HEADS, HEAD_DIM).sum(axis=1)
            summed_v = level_values[bit_level].reshape(N_SEQ // dilation, dilation, TOK_DEV, HEADS, HEAD_DIM).sum(axis=1)
            grad_k = grad_k + placer(summed_k.reshape(N_SEQ, TOK_DEV // dilation, HEADS, HEAD_DIM))
            grad_v = grad_v + placer(summed_v.reshape(N_SEQ, TOK_DEV // dilation, HEADS, HEAD_DIM))
        outs_q.append(grad_q.astype(jnp.bfloat16).reshape(TOKENS, WIDTH))
        outs_k.append(grad_k.astype(jnp.bfloat16).reshape(TOKENS, WIDTH))
        outs_v.append(grad_v.astype(jnp.bfloat16).reshape(TOKENS, WIDTH))
    return jnp.stack(outs_q), jnp.stack(outs_k), jnp.stack(outs_v)
```

```python
import functools

import jax
import jax.numpy as jnp
from jax import lax
from jax.experimental import pallas as pl
from jax.experimental.pallas import tpu as pltpu
from jax.sharding import PartitionSpec as P

F32 = jnp.float32
BF16 = jnp.bfloat16
NEG = -1e30
VMEM_LIMIT = 48 * 1024 * 1024


def exchange(value, bits):
    count = lax.axis_size("seq")
    return lax.ppermute(value, "seq", [(i, i ^ bits) for i in range(count)])


def dot(a, b):
    return jnp.dot(a, b, preferred_element_type=F32)


def dot_nt(a, b):
    return lax.dot_general(a, b, (((1,), (1,)), ((), ())), preferred_element_type=F32)


def pick_matrix(offs_ref, head, first, levels, tok):
    parts = []
    for level in range(first, levels + 1):
        rate = 2**level
        rows = tok // rate
        kept = lax.rem(offs_ref[level - 1, head], rate)
        row = lax.broadcasted_iota(jnp.int32, (rows, tok), 0)
        col = lax.broadcasted_iota(jnp.int32, (rows, tok), 1)
        parts.append((col == row * rate + kept).astype(F32))
    return jnp.concatenate(parts, axis=0).astype(BF16)


def place_matrix(offs_ref, head, first, levels, tok):
    parts = []
    for level in range(first, levels + 1):
        rate = 2**level
        rows = tok // rate
        kept = lax.rem(offs_ref[level - 1, head], rate)
        row = lax.broadcasted_iota(jnp.int32, (tok, rows), 0)
        col = lax.broadcasted_iota(jnp.int32, (tok, rows), 1)
        parts.append((row == col * rate + kept).astype(F32))
    return jnp.concatenate(parts, axis=1).astype(BF16)


def pick_kernel(levels, heads, dim, offs_ref, k_ref, v_ref, two_ref, three_ref):
    tok = k_ref.shape[0]
    n2, n3 = tok // 4, tok // 8
    for h in range(heads):
        head = pl.program_id(0) * heads + h
        pick = pick_matrix(offs_ref, head, 2, levels, tok)
        cols = slice(h * dim, (h + 1) * dim)
        kv = jnp.concatenate([k_ref[:, cols], v_ref[:, cols]], axis=1)
        got = dot(pick, kv).astype(BF16)
        out = slice(2 * h * dim, 2 * (h + 1) * dim)
        two_ref[:, out] = got[:n2]
        three_ref[:, out] = got[n2 : n2 + n3]


def pick_call(offsets, keys, values, dim):
    tok, width = keys.shape
    levels, heads = offsets.shape
    steps = 2
    per = heads // steps
    block = pl.BlockSpec((tok, per * dim), lambda i, o: (0, i))
    return pl.pallas_call(
        functools.partial(pick_kernel, levels, per, dim),
        grid_spec=pltpu.PrefetchScalarGridSpec(
            num_scalar_prefetch=1,
            grid=(steps,),
            in_specs=[block, block],
            out_specs=[
                pl.BlockSpec((tok // 4, 2 * per * dim), lambda i, o: (0, i)),
                pl.BlockSpec((tok // 8, 2 * per * dim), lambda i, o: (0, i)),
            ],
        ),
        out_shape=[
            jax.ShapeDtypeStruct((tok // 4, 2 * width), BF16),
            jax.ShapeDtypeStruct((tok // 8, 2 * width), BF16),
        ],
        compiler_params=pltpu.CompilerParams(vmem_limit_bytes=VMEM_LIMIT),
        name="pick_rows",
    )(offsets, keys, values)


def main_kernel(
    levels, per, dim, offs_ref, core_ref,
    q0, q1, k0, k1, v0, v1, g0, g1, x2, xx2, x3, xx3, y3, yy3, d3, dd3,
    dq_own, dq_oth, base_own, base_oth, xa, xb, ya, yb, da, db,
):
    tok = q0.shape[0]
    n1, n2, n3 = tok // 2, tok // 4, tok // 8
    scale = dim**-0.5
    heads = per * pl.num_programs(0)
    for h in range(per):
        head = core_ref[0] * heads + pl.program_id(0) * per + h
        pick = pick_matrix(offs_ref, head, 1, levels, tok)
        place = place_matrix(offs_ref, head, 1, levels, tok)
        cols = slice(h * dim, (h + 1) * dim)
        kc = slice(2 * h * dim, (2 * h + 1) * dim)
        vc = slice((2 * h + 1) * dim, (2 * h + 2) * dim)
        out = slice(2 * h * dim, 2 * (h + 1) * dim)
        key0, key1, val0, val1 = k0[:, cols], k1[:, cols], v0[:, cols], v1[:, cols]
        que0, que1, gra0, gra1 = q0[:, cols], q1[:, cols], g0[:, cols], g1[:, cols]
        own = dot(pick, jnp.concatenate([key0, val0], axis=1)).astype(BF16)
        oth = dot(pick, jnp.concatenate([key1, val1], axis=1)).astype(BF16)

        def rows(mine, far):
            a, b = own[:, mine], oth[:, mine]
            e = n1 + n2
            return jnp.concatenate(
                [a[:n1], b[:n1], a[n1:e], b[n1:e], x2[:, far], xx2[:, far], a[e:], b[e:]]
                + [ref[:, far] for ref in (x3, xx3, y3, yy3, d3, dd3)],
                axis=0,
            )

        keys = rows(slice(0, dim), kc)
        vals = rows(slice(dim, 2 * dim), vc)
        que = jnp.concatenate([que0, que1], axis=0)
        gra = jnp.concatenate([gra0, gra1], axis=0)
        pos = lax.broadcasted_iota(jnp.int32, (1, 2 * tok), 1)
        s0 = jnp.concatenate([dot_nt(key0, que0), dot_nt(key1, que1)], axis=1) * scale
        sc = dot_nt(keys, que) * scale
        parts = [s0]
        for level in range(1, levels + 1):
            rate = 2**level
            kept = lax.rem(offs_ref[level - 1, head], rate)
            bias = jnp.where(lax.rem(pos, rate) == kept, 0.0, NEG).astype(F32)
            parts.append(sc[(level - 1) * tok : level * tok] + bias)
        s = jnp.concatenate(parts, axis=0)
        top = jnp.max(s, axis=0, keepdims=True)
        e = jnp.exp(s - top)
        w = e * (1.0 / jnp.sum(e, axis=0, keepdims=True))
        wb = w.astype(BF16)
        p0 = jnp.concatenate([dot_nt(val0, gra0), dot_nt(val1, gra1)], axis=1)
        p = jnp.concatenate([p0, dot_nt(vals, gra)], axis=0)
        delta = jnp.sum(wb.astype(F32) * p, axis=0, keepdims=True)
        ds = (w * (p - delta)).astype(BF16)
        dsl, wl = ds[tok:], wb[tok:]
        dk = dot(dsl, que) * scale
        dv = dot(wl, gra)
        dkv = jnp.concatenate([dk, dv], axis=1).astype(BF16)
        dk00 = dot(ds[:tok, :tok], que0) * scale
        dk01 = dot(ds[:tok, tok:], que1) * scale
        dv00 = dot(wb[:tok, :tok], gra0)
        dv01 = dot(wb[:tok, tok:], gra1)
        l2, l3 = tok, 2 * tok
        mine = jnp.concatenate([dkv[:n1], dkv[l2 : l2 + n2], dkv[l3 : l3 + n3]], axis=0)
        other = jnp.concatenate(
            [dkv[n1:tok], dkv[l2 + n2 : l2 + 2 * n2], dkv[l3 + n3 : l3 + 2 * n3]], axis=0
        )
        base_own[:, out] = (jnp.concatenate([dk00, dv00], axis=1) + dot(place, mine)).astype(BF16)
        base_oth[:, out] = (jnp.concatenate([dk01, dv01], axis=1) + dot(place, other)).astype(BF16)
        xa[:n2, out] = dkv[l2 + 2 * n2 : l2 + 3 * n2]
        xb[:n2, out] = dkv[l2 + 3 * n2 : l2 + 4 * n2]
        for i, (ref, lo) in enumerate(((xa, n2), (xb, n2), (ya, 0), (yb, 0), (da, 0), (db, 0))):
            ref[lo : lo + n3, out] = dkv[l3 + (2 + i) * n3 : l3 + (3 + i) * n3]
        dqt = dot(keys.T, dsl)
        dqt0 = dot(key0.T, ds[:tok, :tok])
        dqt1 = dot(key1.T, ds[:tok, tok:])
        dq_own[:, cols] = ((dqt[:, :tok] + dqt0) * scale).T.astype(BF16)
        dq_oth[:, cols] = ((dqt[:, tok:] + dqt1) * scale).T.astype(BF16)


def main_call(offsets, core, raw, far, dim):
    tok, width = raw[0].shape
    levels, heads = offsets.shape
    half = heads // 2
    per = 2
    steps = half // per
    n2, n3 = tok // 4, tok // 8
    raw_spec = pl.BlockSpec((tok, per * dim), lambda i, o, c: (0, c[0] * steps + i))

    def far_spec(rows):
        return pl.BlockSpec((rows, 2 * per * dim), lambda i, o, c: (0, c[0] * steps + i))

    def out(rows, mult):
        return (
            pl.BlockSpec((rows, mult * per * dim), lambda i, o, c: (0, i)),
            jax.ShapeDtypeStruct((rows, mult * half * dim), BF16),
        )

    outs = [out(tok, 1), out(tok, 1), out(tok, 2), out(tok, 2)]
    outs += [out(n2 + n3, 2)] * 2 + [out(n3, 2)] * 4
    return pl.pallas_call(
        functools.partial(main_kernel, levels, per, dim),
        grid_spec=pltpu.PrefetchScalarGridSpec(
            num_scalar_prefetch=2,
            grid=(steps,),
            in_specs=[raw_spec] * 8 + [far_spec(n2)] * 2 + [far_spec(n3)] * 6,
            out_specs=[o[0] for o in outs],
        ),
        out_shape=[o[1] for o in outs],
        compiler_params=pltpu.CompilerParams(vmem_limit_bytes=VMEM_LIMIT),
        name="attention_backward",
    )(offsets, core, *raw, *far)


def final_kernel(
    levels, per, dim, offs_ref, core_ref, dqa, dqb, ba, bb, xa, xb, ya, yb, da, db, dq, dk, dv
):
    tok = dq.shape[0]
    n2 = tok // 4
    heads = per * pl.num_programs(0)
    swap = pl.program_id(0) * 2 // pl.num_programs(0) != core_ref[0]

    def work(dq_in, base, x, y, d):
        dq[...] = dq_in[...]
        for h in range(per):
            head = pl.program_id(0) * per + h
            place = place_matrix(offs_ref, head, 2, levels, tok)
            cols = slice(h * dim, (h + 1) * dim)
            src = slice(2 * h * dim, 2 * (h + 1) * dim)
            third = x[n2:, src].astype(F32) + y[:, src].astype(F32) + d[:, src].astype(F32)
            part = jnp.concatenate([x[:n2, src], third.astype(BF16)], axis=0)
            total = (base[:, src].astype(F32) + dot(place, part)).astype(BF16)
            dk[:, cols] = total[:, :dim]
            dv[:, cols] = total[:, dim:]

    @pl.when(jnp.logical_not(swap))
    def _():
        work(dqa, ba, xa, ya, da)

    @pl.when(swap)
    def _():
        work(dqb, bb, xb, yb, db)


def final_call(offsets, core, parts, dim):
    levels, heads = offsets.shape
    tok = parts[0].shape[0]
    steps = 4
    per = heads // steps

    def spec(a):
        cols = a.shape[1] * 2 // steps
        return pl.BlockSpec((a.shape[0], cols), lambda i, o, c: (0, lax.rem(i, steps // 2)))

    out = pl.BlockSpec((tok, per * dim), lambda i, o, c: (0, i))
    return pl.pallas_call(
        functools.partial(final_kernel, levels, per, dim),
        grid_spec=pltpu.PrefetchScalarGridSpec(
            num_scalar_prefetch=2,
            grid=(steps,),
            in_specs=[spec(a) for a in parts],
            out_specs=[out] * 3,
        ),
        out_shape=[jax.ShapeDtypeStruct((tok, heads * dim), BF16)] * 3,
        compiler_params=pltpu.CompilerParams(vmem_limit_bytes=VMEM_LIMIT),
        name="add_pieces",
    )(offsets, core, *parts)


def per_device(queries, keys_in, values, out_grads, offsets):
    heads = offsets.shape[1]
    dim = queries.shape[2] // heads
    sections = lax.axis_size("section")
    core = lax.rem(lax.axis_index("seq"), 2).astype(jnp.int32).reshape(1)
    grads = lax.ppermute(
        out_grads[0], "section", [(i, (i - 1) % sections) for i in range(sections)]
    )
    q, k, v = queries[0], keys_in[0], values[0]
    q_oth, k_oth, v_oth = exchange(q, 1), exchange(k, 1), exchange(v, 1)
    two, three = pick_call(offsets, k, v, dim)
    x3 = exchange(three, 2)
    y3 = exchange(three, 4)
    x2 = exchange(two, 2)
    d3 = exchange(x3, 4)
    far = []
    for piece in (x2, x3, y3, d3):
        far += [piece, exchange(piece, 1)]
    g_oth = exchange(grads, 1)
    outs = main_call(offsets, core, [q, q_oth, k, k_oth, v, v_oth, grads, g_oth], far, dim)
    dq_own, dq_oth, base_own, base_oth, xa, xb, ya, yb, da, db = outs
    parts = [dq_own, exchange(dq_oth, 1), base_own, exchange(base_oth, 1)]
    parts += [exchange(xa, 2), exchange(xb, 3), exchange(ya, 4), exchange(yb, 5)]
    parts += [exchange(da, 6), exchange(db, 7)]
    dq, dk, dv = final_call(offsets, core, parts, dim)
    return dq[None], dk[None], dv[None]


def solution(mesh):
    spec = P("section", "seq", None)
    return jax.shard_map(
        per_device,
        mesh=mesh,
        in_specs=(spec, spec, spec, spec, P()),
        out_specs=(spec, spec, spec),
        check_vma=False,
    )
```

```python
import functools

import jax
import jax.numpy as jnp
from jax import lax
from jax.experimental import pallas as pl
from jax.experimental.pallas import tpu as pltpu
from jax.sharding import PartitionSpec as P

F32 = jnp.float32
BF16 = jnp.bfloat16
NEG = -1e30
VMEM_LIMIT = 48 * 1024 * 1024


def params():
    return pltpu.CompilerParams(vmem_limit_bytes=VMEM_LIMIT)


def cost(micros):
    return pl.CostEstimate(flops=0, bytes_accessed=int(micros * 3.69e6), transcendentals=0)


def exchange(value, bits):
    count = lax.axis_size("seq")
    return lax.ppermute(value, "seq", [(i, i ^ bits) for i in range(count)])


def dot(a, b):
    return jnp.dot(a, b, preferred_element_type=F32)


def dot_nt(a, b):
    return lax.dot_general(a, b, (((1,), (1,)), ((), ())), preferred_element_type=F32)


def pick_matrix(offs_ref, head, first, levels, tok):
    parts = []
    for level in range(first, levels + 1):
        rate = 2**level
        rows = tok // rate
        kept = lax.rem(offs_ref[level - 1, head], rate)
        row = lax.broadcasted_iota(jnp.int32, (rows, tok), 0)
        col = lax.broadcasted_iota(jnp.int32, (rows, tok), 1)
        parts.append((col == row * rate + kept).astype(F32))
    return jnp.concatenate(parts, axis=0).astype(BF16)


def place_matrix(offs_ref, head, first, levels, tok):
    parts = []
    for level in range(first, levels + 1):
        rate = 2**level
        rows = tok // rate
        kept = lax.rem(offs_ref[level - 1, head], rate)
        row = lax.broadcasted_iota(jnp.int32, (tok, rows), 0)
        col = lax.broadcasted_iota(jnp.int32, (tok, rows), 1)
        parts.append((row == col * rate + kept).astype(F32))
    return jnp.concatenate(parts, axis=1).astype(BF16)


def pick_kernel(levels, heads, dim, offs_ref, k_ref, v_ref, two_ref, three_ref):
    tok = k_ref.shape[0]
    n2, n3 = tok // 4, tok // 8
    for h in range(heads):
        head = pl.program_id(0) * heads + h
        pick = pick_matrix(offs_ref, head, 2, levels, tok)
        cols = slice(h * dim, (h + 1) * dim)
        kv = jnp.concatenate([k_ref[:, cols], v_ref[:, cols]], axis=1)
        got = dot(pick, kv).astype(BF16)
        out = slice(2 * h * dim, 2 * (h + 1) * dim)
        two_ref[:, out] = got[:n2]
        three_ref[:, out] = got[n2 : n2 + n3]


def pick_call(offsets, keys, values, dim):
    tok, width = keys.shape
    levels, heads = offsets.shape
    steps = 2
    per = heads // steps
    block = pl.BlockSpec((tok, per * dim), lambda i, o: (0, i))
    return pl.pallas_call(
        functools.partial(pick_kernel, levels, per, dim),
        grid_spec=pltpu.PrefetchScalarGridSpec(
            num_scalar_prefetch=1,
            grid=(steps,),
            in_specs=[block, block],
            out_specs=[
                pl.BlockSpec((tok // 4, 2 * per * dim), lambda i, o: (0, i)),
                pl.BlockSpec((tok // 8, 2 * per * dim), lambda i, o: (0, i)),
            ],
        ),
        out_shape=[
            jax.ShapeDtypeStruct((tok // 4, 2 * width), BF16),
            jax.ShapeDtypeStruct((tok // 8, 2 * width), BF16),
        ],
        compiler_params=params(),
        cost_estimate=cost(2),
        name="pick_rows",
    )(offsets, keys, values)


def side(*values):
    return jnp.concatenate(values, axis=1)


def stack(*values):
    return jnp.concatenate(values, axis=0)


def split(value, terms):
    parts = []
    for _ in range(terms):
        part = value.astype(BF16)
        parts.append(part)
        value = value - part.astype(F32)
    return parts


def local_scores(pick, levels, offs_ref, head, key0, key1, ones, que0, que1):
    tok, dim = key0.shape
    pos = lax.broadcasted_iota(jnp.int32, (1, 2 * tok), 1)
    bias = jnp.where(lax.rem(pos, 2) == lax.rem(offs_ref[0, head], 2), 0.0, NEG).astype(F32)
    s0 = side(dot_nt(key0, que0), dot_nt(key1, que1)) * dim**-0.5
    s1 = dot_nt(ones, stack(que0, que1)) * dim**-0.5 + bias
    return stack(s0, s1)


def pre_kernel(
    levels, per, dim, offs_ref, core_ref, q0, q1, k0, k1, v0, v1, exps, stats, near, selq
):
    tok = q0.shape[0]
    n1 = tok // 2
    heads = per * pl.num_programs(0)
    for h in range(per):
        head = core_ref[0] * heads + pl.program_id(0) * per + h
        pick = pick_matrix(offs_ref, head, 1, levels, tok)
        cols = slice(h * dim, (h + 1) * dim)
        wide = slice(2 * h * dim, 2 * (h + 1) * dim)
        lanes = slice(2 * h * tok, 2 * (h + 1) * tok)
        own = dot(pick, side(k0[:, cols], v0[:, cols])).astype(BF16)
        oth = dot(pick, side(k1[:, cols], v1[:, cols])).astype(BF16)
        ones = stack(own[:n1], oth[:n1])
        near[:, wide] = stack(ones, own[n1:], oth[n1:])
        que0, que1 = q0[:, cols], q1[:, cols]
        far_pick = pick[n1:]
        selq[:, cols] = stack(dot(far_pick, que0), dot(far_pick, que1)).astype(BF16)
        s = local_scores(
            pick, levels, offs_ref, head, k0[:, cols], k1[:, cols], ones[:, :dim], que0, que1
        )
        top = jnp.max(s, axis=0, keepdims=True)
        e = jnp.exp(s - top)
        exps[:, lanes] = e.astype(BF16)
        stats[0:1, lanes] = top
        stats[1:2, lanes] = jnp.sum(e, axis=0, keepdims=True)


def pre_call(offsets, core, raw, dim):
    tok, width = raw[0].shape
    levels, heads = offsets.shape
    half = heads // 2
    per = 2
    steps = half // per
    raw_spec = pl.BlockSpec((tok, per * dim), lambda i, o, c: (0, c[0] * steps + i))
    sel = 2 * (tok // 4 + tok // 8)

    def out(rows, lanes, kind=BF16):
        return (
            pl.BlockSpec((rows, per * lanes), lambda i, o, c: (0, i)),
            jax.ShapeDtypeStruct((rows, half * lanes), kind),
        )

    outs = [out(2 * tok, 2 * tok), out(8, 2 * tok, F32), out(tok + sel, 2 * dim), out(sel, dim)]
    return pl.pallas_call(
        functools.partial(pre_kernel, levels, per, dim),
        grid_spec=pltpu.PrefetchScalarGridSpec(
            num_scalar_prefetch=2,
            grid=(steps,),
            in_specs=[raw_spec] * 6,
            out_specs=[o[0] for o in outs],
        ),
        out_shape=[o[1] for o in outs],
        compiler_params=params(),
        cost_estimate=cost(5),
        name="local_scores",
    )(offsets, core, *raw)


def far_kernel(
    levels, per, dim, offs_ref, core_ref, exps, stats, near, selq, v0, v1, g0, g1,
    x2, xx2, x3, xx3, y3, yy3, d3, dd3,
    xa, xb, yab, da, db, ngrad, dqt, stats2,
):
    tok = g0.shape[0]
    n1, n2, n3 = tok // 2, tok // 4, tok // 8
    sel = n2 + n3
    scale = dim**-0.5
    heads = per * pl.num_programs(0)
    lane = lax.broadcasted_iota(jnp.int32, (1, 2 * sel), 1)
    is2 = lax.rem(lane, sel) < n2
    pos = lax.broadcasted_iota(jnp.int32, (1, 2 * tok), 1)
    for h in range(per):
        head = core_ref[0] * heads + pl.program_id(0) * per + h
        pick = pick_matrix(offs_ref, head, 2, levels, tok)
        none = jnp.zeros_like(pick)
        both = stack(side(pick, none), side(none, pick))
        cols = slice(h * dim, (h + 1) * dim)
        kc = slice(2 * h * dim, (2 * h + 1) * dim)
        vc = slice((2 * h + 1) * dim, (2 * h + 2) * dim)
        wide = slice(2 * h * dim, 2 * (h + 1) * dim)
        lanes = slice(2 * h * tok, 2 * (h + 1) * tok)
        gra0, gra1 = g0[:, cols], g1[:, cols]
        gsel = stack(dot(pick, gra0), dot(pick, gra1)).astype(BF16)
        qsel = selq[:, cols]

        def rows(c):
            a, b = near[tok : tok + sel, c], near[tok + sel :, c]
            return stack(
                a[:n2], b[:n2], x2[:, c], xx2[:, c], a[n2:], b[n2:],
                *(ref[:, c] for ref in (x3, xx3, y3, yy3, d3, dd3)),
            )

        keys, vals = rows(kc), rows(vc)
        st = dot_nt(keys, qsel)
        s = jnp.where(is2, st[:tok], st[tok:]) * scale
        top = jnp.max(s, axis=0, keepdims=True)
        e = jnp.exp(s - top)
        size = jnp.sum(e, axis=0, keepdims=True)
        pt = dot_nt(vals, gsel)
        p = jnp.where(is2, pt[:tok], pt[tok:])
        dhat = jnp.sum(e * p, axis=0, keepdims=True)
        p0 = side(dot_nt(v0[:, cols], gra0), dot_nt(v1[:, cols], gra1))
        p1 = dot_nt(near[:tok, vc], stack(gra0, gra1))
        ex = exps[:, lanes]
        dloc = jnp.sum(ex[:tok].astype(F32) * p0 + ex[tok:].astype(F32) * p1, axis=0, keepdims=True)
        terms = split(top, 3) + split(size, 2) + split(dhat, 2)
        terms = stack(*terms)
        zero = jnp.zeros_like(terms)
        spread = dot(stack(jnp.where(is2, terms, zero), jnp.where(is2, zero, terms)), both)

        def level_stats(level, lo):
            rate = 2**level
            on = lax.rem(pos, rate) == lax.rem(offs_ref[level - 1, head], rate)
            t = spread[lo : lo + 1] + spread[lo + 1 : lo + 2] + spread[lo + 2 : lo + 3]
            return (
                jnp.where(on, t, NEG),
                spread[lo + 3 : lo + 4] + spread[lo + 4 : lo + 5],
                spread[lo + 5 : lo + 6] + spread[lo + 6 : lo + 7],
            )

        t1, z1 = stats[0:1, lanes], stats[1:2, lanes]
        t2, z2, d2 = level_stats(2, 0)
        t3, z3, d3v = level_stats(3, 7)
        high = jnp.maximum(t1, jnp.maximum(t2, t3))
        a1, a2, a3 = jnp.exp(t1 - high), jnp.exp(t2 - high), jnp.exp(t3 - high)
        inv = 1.0 / (a1 * z1 + a2 * z2 + a3 * z3)
        f1, f2, f3 = a1 * inv, a2 * inv, a3 * inv
        delta = f1 * dloc + f2 * d2 + f3 * d3v
        stats2[0:1, lanes] = f1
        stats2[1:2, lanes] = delta
        back = dot_nt(stack(*split(f2, 2), *split(f3, 2), *split(delta, 2)), both)
        f = jnp.where(is2, back[0:1] + back[1:2], back[2:3] + back[3:4])
        dl = back[4:5] + back[5:6]
        w = e * f
        ds = w * (p - dl)
        zero = jnp.zeros_like(w)

        def apart(value):
            return stack(jnp.where(is2, value, zero), jnp.where(is2, zero, value)).astype(BF16)

        dsm = apart(ds)
        dkv = side(dot(dsm, qsel) * scale, dot(apart(w), gsel)).astype(BF16)
        xa[:n2, wide] = dkv[2 * n2 : 3 * n2]
        xb[:n2, wide] = dkv[3 * n2 : 4 * n2]
        third = [dkv[tok + i * n3 : tok + (i + 1) * n3] for i in range(8)]
        xa[n2:, wide] = third[2]
        xb[n2:, wide] = third[3]
        yab[:, wide] = stack(third[4], third[5])
        da[:, wide] = third[6]
        db[:, wide] = third[7]
        ngrad[:, wide] = stack(dkv[:n2], third[0], dkv[n2 : 2 * n2], third[1])
        dqt[:, h * dim : h * dim + 2 * sel] = dot(keys.T, dsm).astype(BF16)


def far_call(offsets, core, pre, raw, far, dim):
    tok, width = raw[0].shape
    levels, heads = offsets.shape
    half = heads // 2
    per = 2
    steps = half // per
    n2, n3 = tok // 4, tok // 8
    raw_spec = pl.BlockSpec((tok, per * dim), lambda i, o, c: (0, c[0] * steps + i))

    def near_spec(a):
        return pl.BlockSpec((a.shape[0], a.shape[1] // steps), lambda i, o, c: (0, i))

    def far_spec(a):
        return pl.BlockSpec((a.shape[0], 2 * per * dim), lambda i, o, c: (0, c[0] * steps + i))

    def out(rows, lanes, kind=BF16):
        return (
            pl.BlockSpec((rows, per * lanes), lambda i, o, c: (0, i)),
            jax.ShapeDtypeStruct((rows, half * lanes), kind),
        )

    outs = [out(n2 + n3, 2 * dim)] * 2 + [out(2 * n3, 2 * dim)] + [out(n3, 2 * dim)] * 2
    outs += [out(2 * (n2 + n3), 2 * dim), out(dim, dim), out(8, 2 * tok, F32)]
    return pl.pallas_call(
        functools.partial(far_kernel, levels, per, dim),
        grid_spec=pltpu.PrefetchScalarGridSpec(
            num_scalar_prefetch=2,
            grid=(steps,),
            in_specs=[near_spec(a) for a in pre] + [raw_spec] * 4 + [far_spec(a) for a in far],
            out_specs=[o[0] for o in outs],
        ),
        out_shape=[o[1] for o in outs],
        compiler_params=params(),
        cost_estimate=cost(4),
        name="far_levels",
    )(offsets, core, *pre, *raw, *far)


def near_kernel(
    levels, per, dim, offs_ref, core_ref, exps, stats2, near, ngrad, dqt,
    q0, q1, k0, k1, v0, v1, g0, g1, mine, other,
):
    tok = q0.shape[0]
    n1 = tok // 2
    sel = tok // 4 + tok // 8
    scale = dim**-0.5
    heads = per * pl.num_programs(0)
    for h in range(per):
        head = core_ref[0] * heads + pl.program_id(0) * per + h
        pick = pick_matrix(offs_ref, head, 2, levels, tok)
        place = place_matrix(offs_ref, head, 1, levels, tok)
        cols = slice(h * dim, (h + 1) * dim)
        kc = slice(2 * h * dim, (2 * h + 1) * dim)
        vc = slice((2 * h + 1) * dim, (2 * h + 2) * dim)
        wide = slice(2 * h * dim, 2 * (h + 1) * dim)
        lanes = slice(2 * h * tok, 2 * (h + 1) * tok)
        que0, que1, gra0, gra1 = q0[:, cols], q1[:, cols], g0[:, cols], g1[:, cols]
        que, gra = stack(que0, que1), stack(gra0, gra1)
        p0 = side(dot_nt(v0[:, cols], gra0), dot_nt(v1[:, cols], gra1))
        p = stack(p0, dot_nt(near[:tok, vc], gra))
        w = exps[:, lanes].astype(F32) * stats2[0:1, lanes]
        wb = w.astype(BF16)
        ds = (w * (p - stats2[1:2, lanes])).astype(BF16)
        dkv1 = side(dot(ds[tok:], que) * scale, dot(wb[tok:], gra)).astype(BF16)
        ds0, ds1 = ds[:tok, :tok], ds[:tok, tok:]
        kv0 = side(dot(ds0, que0) * scale, dot(wb[:tok, :tok], gra0))
        kv1 = side(dot(ds1, que1) * scale, dot(wb[:tok, tok:], gra1))
        kv0 += dot(place, stack(dkv1[:n1], ngrad[:sel, wide]))
        kv1 += dot(place, stack(dkv1[n1:], ngrad[sel:, wide]))
        dqa = dot(near[:tok, kc].T, ds[tok:])
        dq0 = dqa[:, :tok] + dot(k0[:, cols].T, ds0)
        dq1 = dqa[:, tok:] + dot(k1[:, cols].T, ds1)
        dq0 += dot(dqt[:, h * dim : h * dim + sel], pick)
        dq1 += dot(dqt[:, h * dim + sel : h * dim + 2 * sel], pick)
        for ref, dq, kv in ((mine, dq0, kv0), (other, dq1, kv1)):
            lo = 3 * h * dim
            ref[:, lo : lo + dim] = (dq * scale).T.astype(BF16)
            ref[:, lo + dim : lo + 3 * dim] = kv.astype(BF16)


def near_call(offsets, core, mid, raw, dim):
    tok, width = raw[0].shape
    levels, heads = offsets.shape
    half = heads // 2
    per = 2
    steps = half // per
    raw_spec = pl.BlockSpec((tok, per * dim), lambda i, o, c: (0, c[0] * steps + i))

    def mid_spec(a):
        return pl.BlockSpec((a.shape[0], a.shape[1] // steps), lambda i, o, c: (0, i))

    out_spec = pl.BlockSpec((tok, 3 * per * dim), lambda i, o, c: (0, i))
    return pl.pallas_call(
        functools.partial(near_kernel, levels, per, dim),
        grid_spec=pltpu.PrefetchScalarGridSpec(
            num_scalar_prefetch=2,
            grid=(steps,),
            in_specs=[mid_spec(a) for a in mid] + [raw_spec] * 8,
            out_specs=[out_spec] * 2,
        ),
        out_shape=[jax.ShapeDtypeStruct((tok, 3 * half * dim), BF16)] * 2,
        compiler_params=params(),
        cost_estimate=cost(7),
        name="near_levels",
    )(offsets, core, *mid, *raw)


def final_kernel(
    levels, per, dim, offs_ref, core_ref, ba, bb, xa, xb, ya, yb, da, db, dq, dk, dv
):
    tok = dq.shape[0]
    n2, n3 = tok // 4, tok // 8
    heads = per * pl.num_programs(0)
    swap = pl.program_id(0) * 2 // pl.num_programs(0) != core_ref[0]

    def work(base, x, y, d):
        for h in range(per):
            head = pl.program_id(0) * per + h
            place = place_matrix(offs_ref, head, 2, levels, tok)
            cols = slice(h * dim, (h + 1) * dim)
            src = slice(2 * h * dim, 2 * (h + 1) * dim)
            lo = 3 * h * dim
            third = x[n2:, src].astype(F32) + y[:, src].astype(F32) + d[:, src].astype(F32)
            part = stack(x[:n2, src], third.astype(BF16))
            total = base[:, lo + dim : lo + 3 * dim].astype(F32) + dot(place, part)
            dq[:, cols] = base[:, lo : lo + dim]
            dk[:, cols] = total[:, :dim].astype(BF16)
            dv[:, cols] = total[:, dim:].astype(BF16)

    @pl.when(jnp.logical_not(swap))
    def _():
        work(ba, xa, ya, da)

    @pl.when(swap)
    def _():
        work(bb, xb, yb, db)


def final_call(offsets, core, parts, dim):
    levels, heads = offsets.shape
    tok = parts[0].shape[0]
    steps = 4
    per = heads // steps
    third = tok // 8

    def spec(a, far, row, rows):
        cols = a.shape[1] * 2 // steps

        def where(i, o, c):
            turn = 1 - c[0] if far else c[0]
            return row, jnp.clip(i - turn * (steps // 2), 0, steps // 2 - 1)

        return pl.BlockSpec((rows, cols), where)

    specs = []
    for i, a in enumerate(parts):
        far = i % 2 == 1
        if i in (4, 5):
            specs.append(spec(a, far, 1 if far else 0, third))
        else:
            specs.append(spec(a, far, 0, a.shape[0]))
    out = pl.BlockSpec((tok, per * dim), lambda i, o, c: (0, i))
    return pl.pallas_call(
        functools.partial(final_kernel, levels, per, dim),
        grid_spec=pltpu.PrefetchScalarGridSpec(
            num_scalar_prefetch=2,
            grid=(steps,),
            in_specs=specs,
            out_specs=[out] * 3,
        ),
        out_shape=[jax.ShapeDtypeStruct((tok, heads * dim), BF16)] * 3,
        compiler_params=params(),
        cost_estimate=cost(3),
        name="add_pieces",
    )(offsets, core, *parts)


def per_device(queries, keys_in, values, out_grads, offsets):
    heads = offsets.shape[1]
    dim = queries.shape[2] // heads
    sections = lax.axis_size("section")
    core = lax.rem(lax.axis_index("seq"), 2).astype(jnp.int32).reshape(1)
    grads = lax.ppermute(
        out_grads[0], "section", [(i, (i - 1) % sections) for i in range(sections)]
    )
    q, k, v = queries[0], keys_in[0], values[0]
    q_oth, k_oth, v_oth = exchange(q, 1), exchange(k, 1), exchange(v, 1)
    two, three = pick_call(offsets, k, v, dim)
    x3 = exchange(three, 2)
    y3 = exchange(three, 4)
    x2 = exchange(two, 2)
    d3 = exchange(x3, 4)
    exps, stats, near, selq = pre_call(offsets, core, [q, q_oth, k, k_oth, v, v_oth], dim)
    far = []
    for piece in (x2, x3, y3, d3):
        far += [piece, exchange(piece, 1)]
    g_oth = exchange(grads, 1)
    xa, xb, yab, da, db, ngrad, dqt, stats2 = far_call(
        offsets, core, [exps, stats, near, selq], [v, v_oth, grads, g_oth], far, dim
    )
    xa, xb, da, db = exchange(xa, 2), exchange(xb, 3), exchange(da, 6), exchange(db, 7)
    y = exchange(yab, 4)
    yy = exchange(y, 1)
    mine, other = near_call(
        offsets, core, [exps, stats2, near, ngrad, dqt],
        [q, q_oth, k, k_oth, v, v_oth, grads, g_oth], dim,
    )
    parts = [mine, exchange(other, 1), xa, xb, y, yy, da, db]
    dq, dk, dv = final_call(offsets, core, parts, dim)
    return dq[None], dk[None], dv[None]


def solution(mesh):
    spec = P("section", "seq", None)
    return jax.shard_map(
        per_device,
        mesh=mesh,
        in_specs=(spec, spec, spec, spec, P()),
        out_specs=(spec, spec, spec),
        check_vma=False,
    )
```

```python
import functools

import jax
import jax.numpy as jnp
from jax import lax
from jax.experimental import pallas as pl
from jax.experimental.pallas import tpu as pltpu
from jax.sharding import PartitionSpec as P

F32 = jnp.float32
BF16 = jnp.bfloat16
NEG = -1e30
VMEM_LIMIT = 48 * 1024 * 1024


def params():
    return pltpu.CompilerParams(vmem_limit_bytes=VMEM_LIMIT)


def exchange(value, bits):
    count = lax.axis_size("seq")
    return lax.ppermute(value, "seq", [(i, i ^ bits) for i in range(count)])


def dot(a, b):
    return jnp.dot(a, b, preferred_element_type=F32)


def dot_nt(a, b):
    return lax.dot_general(a, b, (((1,), (1,)), ((), ())), preferred_element_type=F32)


def pick_matrix(offs_ref, head, first, levels, tok):
    parts = []
    for level in range(first, levels + 1):
        rate = 2**level
        rows = tok // rate
        kept = lax.rem(offs_ref[level - 1, head], rate)
        row = lax.broadcasted_iota(jnp.int32, (rows, tok), 0)
        col = lax.broadcasted_iota(jnp.int32, (rows, tok), 1)
        parts.append((col == row * rate + kept).astype(F32))
    return jnp.concatenate(parts, axis=0).astype(BF16)


def place_matrix(offs_ref, head, first, levels, tok):
    parts = []
    for level in range(first, levels + 1):
        rate = 2**level
        rows = tok // rate
        kept = lax.rem(offs_ref[level - 1, head], rate)
        row = lax.broadcasted_iota(jnp.int32, (tok, rows), 0)
        col = lax.broadcasted_iota(jnp.int32, (tok, rows), 1)
        parts.append((row == col * rate + kept).astype(F32))
    return jnp.concatenate(parts, axis=1).astype(BF16)


def pick_kernel(levels, heads, dim, offs_ref, core_ref, k_ref, v_ref, q_half, k_half, v_half,
                both_ref, three_ref, swap_ref):
    tok = k_ref.shape[0]
    n2, n3 = tok // 4, tok // 8
    for h in range(heads):
        head = pl.program_id(0) * heads + h
        pick = pick_matrix(offs_ref, head, 2, levels, tok)
        cols = slice(h * dim, (h + 1) * dim)
        kv = jnp.concatenate([k_ref[:, cols], v_ref[:, cols]], axis=1)
        got = dot(pick, kv).astype(BF16)
        out = slice(2 * h * dim, 2 * (h + 1) * dim)
        both_ref[:, out] = got
        three_ref[:, out] = got[n2 : n2 + n3]

    @pl.when(pl.program_id(0) == 0)
    def _():
        half = q_half.shape[1]
        for i, ref in enumerate((q_half, k_half, v_half)):
            swap_ref[:, i * half : (i + 1) * half] = ref[...]


def pick_call(offsets, core, queries, keys, values, dim):
    tok, width = keys.shape
    levels, heads = offsets.shape
    steps = 2
    per = heads // steps
    block = pl.BlockSpec((tok, per * dim), lambda i, o, c: (0, i))
    half = pl.BlockSpec((tok, width // 2), lambda i, o, c: (0, 1 - c[0]))
    return pl.pallas_call(
        functools.partial(pick_kernel, levels, per, dim),
        grid_spec=pltpu.PrefetchScalarGridSpec(
            num_scalar_prefetch=2,
            grid=(steps,),
            in_specs=[block, block, half, half, half],
            out_specs=[
                pl.BlockSpec((tok // 4 + tok // 8, 2 * per * dim), lambda i, o, c: (0, i)),
                pl.BlockSpec((tok // 8, 2 * per * dim), lambda i, o, c: (0, i)),
                pl.BlockSpec((tok, 3 * width // 2), lambda i, o, c: (0, 0)),
            ],
        ),
        out_shape=[
            jax.ShapeDtypeStruct((tok // 4 + tok // 8, 2 * width), BF16),
            jax.ShapeDtypeStruct((tok // 8, 2 * width), BF16),
            jax.ShapeDtypeStruct((tok, 3 * width // 2), BF16),
        ],
        compiler_params=params(),
        name="pick_rows",
    )(offsets, core, keys, values, queries, keys, values)


def own_spec(tok, cols, steps):
    return pl.BlockSpec((tok, cols), lambda i, o, c: (0, c[0] * steps + i))


def swap_spec(tok, cols, steps, part):
    return pl.BlockSpec((tok, cols), lambda i, o, c: (0, part * steps + i))


def side(*values):
    return jnp.concatenate(values, axis=1)


def stack(*values):
    return jnp.concatenate(values, axis=0)


def split(value, terms):
    parts = []
    for _ in range(terms):
        part = value.astype(BF16)
        parts.append(part)
        value = value - part.astype(F32)
    return parts


def local_scores(pick, levels, offs_ref, head, key0, key1, ones, que0, que1):
    tok, dim = key0.shape
    pos = lax.broadcasted_iota(jnp.int32, (1, 2 * tok), 1)
    bias = jnp.where(lax.rem(pos, 2) == lax.rem(offs_ref[0, head], 2), 0.0, NEG).astype(F32)
    s0 = side(dot_nt(key0, que0), dot_nt(key1, que1)) * dim**-0.5
    s1 = dot_nt(ones, stack(que0, que1)) * dim**-0.5 + bias
    return stack(s0, s1)


def pre_kernel(
    levels, per, dim, offs_ref, core_ref, q0, q1, k0, k1, v0, v1, exps, stats, near, selq
):
    tok = q0.shape[0]
    n1 = tok // 2
    heads = per * pl.num_programs(0)
    for h in range(per):
        head = core_ref[0] * heads + pl.program_id(0) * per + h
        pick = pick_matrix(offs_ref, head, 1, levels, tok)
        cols = slice(h * dim, (h + 1) * dim)
        wide = slice(2 * h * dim, 2 * (h + 1) * dim)
        lanes = slice(2 * h * tok, 2 * (h + 1) * tok)
        own = dot(pick, side(k0[:, cols], v0[:, cols])).astype(BF16)
        oth = dot(pick, side(k1[:, cols], v1[:, cols])).astype(BF16)
        ones = stack(own[:n1], oth[:n1])
        near[:, wide] = stack(ones, own[n1:], oth[n1:])
        que0, que1 = q0[:, cols], q1[:, cols]
        far_pick = pick[n1:]
        selq[:, cols] = stack(dot(far_pick, que0), dot(far_pick, que1)).astype(BF16)
        s = local_scores(
            pick, levels, offs_ref, head, k0[:, cols], k1[:, cols], ones[:, :dim], que0, que1
        )
        top = jnp.max(s, axis=0, keepdims=True)
        e = jnp.exp(s - top)
        exps[:, lanes] = e.astype(BF16)
        stats[0:1, lanes] = top
        stats[1:2, lanes] = jnp.sum(e, axis=0, keepdims=True)


def pre_call(offsets, core, raw, dim):
    tok, width = raw[0].shape
    levels, heads = offsets.shape
    half = heads // 2
    per = 2
    steps = half // per
    raw_spec = own_spec(tok, per * dim, steps)
    swapped = [swap_spec(tok, per * dim, steps, i) for i in range(3)]
    sel = 2 * (tok // 4 + tok // 8)

    def out(rows, lanes, kind=BF16):
        return (
            pl.BlockSpec((rows, per * lanes), lambda i, o, c: (0, i)),
            jax.ShapeDtypeStruct((rows, half * lanes), kind),
        )

    outs = [out(2 * tok, 2 * tok), out(8, 2 * tok, F32), out(tok + sel, 2 * dim), out(sel, dim)]
    return pl.pallas_call(
        functools.partial(pre_kernel, levels, per, dim),
        grid_spec=pltpu.PrefetchScalarGridSpec(
            num_scalar_prefetch=2,
            grid=(steps,),
            in_specs=[raw_spec, swapped[0], raw_spec, swapped[1], raw_spec, swapped[2]],
            out_specs=[o[0] for o in outs],
        ),
        out_shape=[o[1] for o in outs],
        compiler_params=params(),
        name="local_scores",
    )(offsets, core, *raw)


def far_kernel(
    levels, per, dim, offs_ref, core_ref, exps, stats, near, selq, v0, v1, g0, g1,
    x, xx, y3, yy3, d3, dd3,
    xa, xb, yab, da, db, ngrad, dqt, stats2,
):
    tok = g0.shape[0]
    n1, n2, n3 = tok // 2, tok // 4, tok // 8
    sel = n2 + n3
    scale = dim**-0.5
    heads = per * pl.num_programs(0)
    lane = lax.broadcasted_iota(jnp.int32, (1, 2 * sel), 1)
    is2 = lax.rem(lane, sel) < n2
    pos = lax.broadcasted_iota(jnp.int32, (1, 2 * tok), 1)
    for h in range(per):
        head = core_ref[0] * heads + pl.program_id(0) * per + h
        pick = pick_matrix(offs_ref, head, 2, levels, tok)
        none = jnp.zeros_like(pick)
        both = stack(side(pick, none), side(none, pick))
        cols = slice(h * dim, (h + 1) * dim)
        kc = slice(2 * h * dim, (2 * h + 1) * dim)
        vc = slice((2 * h + 1) * dim, (2 * h + 2) * dim)
        wide = slice(2 * h * dim, 2 * (h + 1) * dim)
        lanes = slice(2 * h * tok, 2 * (h + 1) * tok)
        gra0, gra1 = g0[:, cols], g1[:, cols]
        gsel = stack(dot(pick, gra0), dot(pick, gra1)).astype(BF16)
        qsel = selq[:, cols]

        def rows(c):
            a, b = near[tok : tok + sel, c], near[tok + sel :, c]
            return stack(
                a[:n2], b[:n2], x[:n2, c], xx[:n2, c], a[n2:], b[n2:], x[n2:, c], xx[n2:, c],
                *(ref[:, c] for ref in (y3, yy3, d3, dd3)),
            )

        keys, vals = rows(kc), rows(vc)
        st = dot_nt(keys, qsel)
        s = jnp.where(is2, st[:tok], st[tok:]) * scale
        top = jnp.max(s, axis=0, keepdims=True)
        e = jnp.exp(s - top)
        size = jnp.sum(e, axis=0, keepdims=True)
        pt = dot_nt(vals, gsel)
        p = jnp.where(is2, pt[:tok], pt[tok:])
        dhat = jnp.sum(e * p, axis=0, keepdims=True)
        p0 = side(dot_nt(v0[:, cols], gra0), dot_nt(v1[:, cols], gra1))
        p1 = dot_nt(near[:tok, vc], stack(gra0, gra1))
        ex = exps[:, lanes]
        dloc = jnp.sum(ex[:tok].astype(F32) * p0 + ex[tok:].astype(F32) * p1, axis=0, keepdims=True)
        terms = split(top, 3) + split(size, 2) + split(dhat, 2)
        terms = stack(*terms)
        zero = jnp.zeros_like(terms)
        spread = dot(stack(jnp.where(is2, terms, zero), jnp.where(is2, zero, terms)), both)

        def level_stats(level, lo):
            rate = 2**level
            on = lax.rem(pos, rate) == lax.rem(offs_ref[level - 1, head], rate)
            t = spread[lo : lo + 1] + spread[lo + 1 : lo + 2] + spread[lo + 2 : lo + 3]
            return (
                jnp.where(on, t, NEG),
                spread[lo + 3 : lo + 4] + spread[lo + 4 : lo + 5],
                spread[lo + 5 : lo + 6] + spread[lo + 6 : lo + 7],
            )

        t1, z1 = stats[0:1, lanes], stats[1:2, lanes]
        t2, z2, d2 = level_stats(2, 0)
        t3, z3, d3v = level_stats(3, 7)
        high = jnp.maximum(t1, jnp.maximum(t2, t3))
        a1, a2, a3 = jnp.exp(t1 - high), jnp.exp(t2 - high), jnp.exp(t3 - high)
        inv = 1.0 / (a1 * z1 + a2 * z2 + a3 * z3)
        f1, f2, f3 = a1 * inv, a2 * inv, a3 * inv
        delta = f1 * dloc + f2 * d2 + f3 * d3v
        stats2[0:1, lanes] = f1
        stats2[1:2, lanes] = delta
        back = dot_nt(stack(*split(f2, 2), *split(f3, 2), *split(delta, 2)), both)
        f = jnp.where(is2, back[0:1] + back[1:2], back[2:3] + back[3:4])
        dl = back[4:5] + back[5:6]
        w = e * f
        ds = w * (p - dl)
        zero = jnp.zeros_like(w)

        def apart(value):
            return stack(jnp.where(is2, value, zero), jnp.where(is2, zero, value)).astype(BF16)

        dsm = apart(ds)
        dkv = side(dot(dsm, qsel) * scale, dot(apart(w), gsel)).astype(BF16)
        xa[:n2, wide] = dkv[2 * n2 : 3 * n2]
        xb[:n2, wide] = dkv[3 * n2 : 4 * n2]
        third = [dkv[tok + i * n3 : tok + (i + 1) * n3] for i in range(8)]
        xa[n2:, wide] = third[2]
        xb[n2:, wide] = third[3]
        yab[:, wide] = stack(third[4], third[5])
        da[:, wide] = third[6]
        db[:, wide] = third[7]
        ngrad[:, wide] = stack(dkv[:n2], third[0], dkv[n2 : 2 * n2], third[1])
        dqt[:, h * dim : h * dim + 2 * sel] = dot(keys.T, dsm).astype(BF16)


def far_call(offsets, core, pre, raw, far, dim):
    tok, width = raw[0].shape
    levels, heads = offsets.shape
    half = heads // 2
    per = 2
    steps = half // per
    n2, n3 = tok // 4, tok // 8
    raw_spec = own_spec(tok, per * dim, steps)
    swapped = [swap_spec(tok, per * dim, steps, i) for i in range(3)]

    def near_spec(a):
        return pl.BlockSpec((a.shape[0], a.shape[1] // steps), lambda i, o, c: (0, i))

    def far_spec(a):
        return pl.BlockSpec((a.shape[0], 2 * per * dim), lambda i, o, c: (0, c[0] * steps + i))

    def out(rows, lanes, kind=BF16):
        return (
            pl.BlockSpec((rows, per * lanes), lambda i, o, c: (0, i)),
            jax.ShapeDtypeStruct((rows, half * lanes), kind),
        )

    outs = [out(n2 + n3, 2 * dim)] * 2 + [out(2 * n3, 2 * dim)] + [out(n3, 2 * dim)] * 2
    outs += [out(2 * (n2 + n3), 2 * dim), out(dim, dim), out(8, 2 * tok, F32)]
    return pl.pallas_call(
        functools.partial(far_kernel, levels, per, dim),
        grid_spec=pltpu.PrefetchScalarGridSpec(
            num_scalar_prefetch=2,
            grid=(steps,),
            in_specs=[near_spec(a) for a in pre] + [raw_spec, swapped[2], raw_spec, raw_spec]
            + [far_spec(a) for a in far],
            out_specs=[o[0] for o in outs],
        ),
        out_shape=[o[1] for o in outs],
        compiler_params=params(),
        name="far_levels",
    )(offsets, core, *pre, *raw, *far)


def near_kernel(
    levels, per, dim, offs_ref, core_ref, exps, stats2, near, ngrad, dqt,
    q0, q1, k0, k1, v0, v1, g0, g1, mine, other,
):
    tok = q0.shape[0]
    n1 = tok // 2
    sel = tok // 4 + tok // 8
    scale = dim**-0.5
    heads = per * pl.num_programs(0)
    for h in range(per):
        head = core_ref[0] * heads + pl.program_id(0) * per + h
        pick = pick_matrix(offs_ref, head, 2, levels, tok)
        place = place_matrix(offs_ref, head, 1, levels, tok)
        cols = slice(h * dim, (h + 1) * dim)
        kc = slice(2 * h * dim, (2 * h + 1) * dim)
        vc = slice((2 * h + 1) * dim, (2 * h + 2) * dim)
        wide = slice(2 * h * dim, 2 * (h + 1) * dim)
        lanes = slice(2 * h * tok, 2 * (h + 1) * tok)
        que0, que1, gra0, gra1 = q0[:, cols], q1[:, cols], g0[:, cols], g1[:, cols]
        que, gra = stack(que0, que1), stack(gra0, gra1)
        p0 = side(dot_nt(v0[:, cols], gra0), dot_nt(v1[:, cols], gra1))
        p = stack(p0, dot_nt(near[:tok, vc], gra))
        w = exps[:, lanes].astype(F32) * stats2[0:1, lanes]
        wb = w.astype(BF16)
        ds = (w * (p - stats2[1:2, lanes])).astype(BF16)
        dkv1 = side(dot(ds[tok:], que) * scale, dot(wb[tok:], gra)).astype(BF16)
        ds0, ds1 = ds[:tok, :tok], ds[:tok, tok:]
        kv0 = side(dot(ds0, que0) * scale, dot(wb[:tok, :tok], gra0))
        kv1 = side(dot(ds1, que1) * scale, dot(wb[:tok, tok:], gra1))
        kv0 += dot(place, stack(dkv1[:n1], ngrad[:sel, wide]))
        kv1 += dot(place, stack(dkv1[n1:], ngrad[sel:, wide]))
        dqa = dot(near[:tok, kc].T, ds[tok:])
        dq0 = dqa[:, :tok] + dot(k0[:, cols].T, ds0)
        dq1 = dqa[:, tok:] + dot(k1[:, cols].T, ds1)
        dq0 += dot(dqt[:, h * dim : h * dim + sel], pick)
        dq1 += dot(dqt[:, h * dim + sel : h * dim + 2 * sel], pick)
        for ref, dq, kv in ((mine, dq0, kv0), (other, dq1, kv1)):
            lo = 3 * h * dim
            ref[:, lo : lo + dim] = (dq * scale).T.astype(BF16)
            ref[:, lo + dim : lo + 3 * dim] = kv.astype(BF16)


def near_call(offsets, core, mid, raw, dim):
    tok, width = raw[0].shape
    levels, heads = offsets.shape
    half = heads // 2
    per = 2
    steps = half // per
    raw_spec = own_spec(tok, per * dim, steps)
    swapped = [swap_spec(tok, per * dim, steps, i) for i in range(3)]

    def mid_spec(a):
        return pl.BlockSpec((a.shape[0], a.shape[1] // steps), lambda i, o, c: (0, i))

    out_spec = pl.BlockSpec((tok, 3 * per * dim), lambda i, o, c: (0, i))
    return pl.pallas_call(
        functools.partial(near_kernel, levels, per, dim),
        grid_spec=pltpu.PrefetchScalarGridSpec(
            num_scalar_prefetch=2,
            grid=(steps,),
            in_specs=[mid_spec(a) for a in mid]
            + [raw_spec, swapped[0], raw_spec, swapped[1], raw_spec, swapped[2], raw_spec, raw_spec],
            out_specs=[out_spec] * 2,
        ),
        out_shape=[jax.ShapeDtypeStruct((tok, 3 * half * dim), BF16)] * 2,
        compiler_params=params(),
        name="near_levels",
    )(offsets, core, *mid, *raw)


def final_kernel(
    levels, per, dim, offs_ref, core_ref, ba, bb, xa, xb, ya, yb, da, db, dq, dk, dv
):
    tok = dq.shape[0]
    n2, n3 = tok // 4, tok // 8
    heads = per * pl.num_programs(0)
    swap = pl.program_id(0) * 2 // pl.num_programs(0) != core_ref[0]

    def work(base, x, y, d):
        for h in range(per):
            head = pl.program_id(0) * per + h
            place = place_matrix(offs_ref, head, 2, levels, tok)
            cols = slice(h * dim, (h + 1) * dim)
            src = slice(2 * h * dim, 2 * (h + 1) * dim)
            lo = 3 * h * dim
            third = x[n2:, src].astype(F32) + y[:, src].astype(F32) + d[:, src].astype(F32)
            part = stack(x[:n2, src], third.astype(BF16))
            total = base[:, lo + dim : lo + 3 * dim].astype(F32) + dot(place, part)
            dq[:, cols] = base[:, lo : lo + dim]
            dk[:, cols] = total[:, :dim].astype(BF16)
            dv[:, cols] = total[:, dim:].astype(BF16)

    @pl.when(jnp.logical_not(swap))
    def _():
        work(ba, xa, ya, da)

    @pl.when(swap)
    def _():
        work(bb, xb, yb, db)


def final_call(offsets, core, parts, dim):
    levels, heads = offsets.shape
    tok = parts[0].shape[0]
    steps = 4
    per = heads // steps
    third = tok // 8

    def spec(a, far, row, rows):
        cols = a.shape[1] * 2 // steps

        def where(i, o, c):
            turn = 1 - c[0] if far else c[0]
            return row, jnp.clip(i - turn * (steps // 2), 0, steps // 2 - 1)

        return pl.BlockSpec((rows, cols), where)

    specs = []
    for i, a in enumerate(parts):
        far = i % 2 == 1
        if i in (4, 5):
            specs.append(spec(a, far, 1 if far else 0, third))
        else:
            specs.append(spec(a, far, 0, a.shape[0]))
    out = pl.BlockSpec((tok, per * dim), lambda i, o, c: (0, i))
    return pl.pallas_call(
        functools.partial(final_kernel, levels, per, dim),
        grid_spec=pltpu.PrefetchScalarGridSpec(
            num_scalar_prefetch=2,
            grid=(steps,),
            in_specs=specs,
            out_specs=[out] * 3,
        ),
        out_shape=[jax.ShapeDtypeStruct((tok, heads * dim), BF16)] * 3,
        compiler_params=params(),
        name="add_pieces",
    )(offsets, core, *parts)


def per_device(queries, keys_in, values, out_grads, offsets):
    heads = offsets.shape[1]
    dim = queries.shape[2] // heads
    sections = lax.axis_size("section")
    core = lax.rem(lax.axis_index("seq"), 2).astype(jnp.int32).reshape(1)
    grads = lax.ppermute(
        out_grads[0], "section", [(i, (i - 1) % sections) for i in range(sections)]
    )
    q, k, v = (pltpu.with_memory_space_constraint(a[0], pltpu.HBM) for a in (queries, keys_in, values))
    both, three, swap = pick_call(offsets, core, q, k, v, dim)
    swap = exchange(swap, 1)
    x, y, d = exchange(both, 2), exchange(three, 4), exchange(three, 6)
    pre = pre_call(offsets, core, [q, swap, k, swap, v, swap], dim)
    x, y, d, grads = lax.optimization_barrier((x, y, d, grads, pre[1]))[:4]
    far = []
    for piece in (x, y, d):
        far += [piece, exchange(piece, 1)]
    g_oth = exchange(grads, 1)
    xa, xb, yab, da, db, ngrad, dqt, stats2 = far_call(
        offsets, core, pre, [v, swap, grads, g_oth], far, dim
    )
    xa, xb, da, db = exchange(xa, 2), exchange(xb, 3), exchange(da, 6), exchange(db, 7)
    y = exchange(yab, 4)
    yy = exchange(y, 1)
    mine, other = near_call(
        offsets, core, [pre[0], stats2, pre[2], ngrad, dqt],
        [q, swap, k, swap, v, swap, grads, g_oth], dim,
    )
    other, xa, xb, da, db, y = lax.optimization_barrier((other, xa, xb, da, db, y))
    parts = [mine, exchange(other, 1), xa, xb, y, yy, da, db]
    dq, dk, dv = final_call(offsets, core, parts, dim)
    return dq[None], dk[None], dv[None]


def solution(mesh):
    spec = P("section", "seq", None)
    return jax.shard_map(
        per_device,
        mesh=mesh,
        in_specs=(spec, spec, spec, spec, P()),
        out_specs=(spec, spec, spec),
        check_vma=False,
    )
```

```python
import functools

import jax
import jax.numpy as jnp
from jax import lax
from jax.experimental import pallas as pl
from jax.experimental.pallas import tpu as pltpu
from jax.sharding import PartitionSpec as P

F32 = jnp.float32
BF16 = jnp.bfloat16
NEG = -1e30
VMEM_LIMIT = 48 * 1024 * 1024


def params():
    return pltpu.CompilerParams(vmem_limit_bytes=VMEM_LIMIT)


def exchange(value, bits):
    count = lax.axis_size("seq")
    return lax.ppermute(value, "seq", [(i, i ^ bits) for i in range(count)])


def dot(a, b):
    return jnp.dot(a, b, preferred_element_type=F32)


def dot_nt(a, b):
    return lax.dot_general(a, b, (((1,), (1,)), ((), ())), preferred_element_type=F32)


def pick_matrix(offs_ref, head, first, levels, tok):
    parts = []
    for level in range(first, levels + 1):
        rate = 2**level
        rows = tok // rate
        kept = lax.rem(offs_ref[level - 1, head], rate)
        row = lax.broadcasted_iota(jnp.int32, (rows, tok), 0)
        col = lax.broadcasted_iota(jnp.int32, (rows, tok), 1)
        parts.append((col == row * rate + kept).astype(F32))
    return jnp.concatenate(parts, axis=0).astype(BF16)


def place_matrix(offs_ref, head, first, levels, tok):
    parts = []
    for level in range(first, levels + 1):
        rate = 2**level
        rows = tok // rate
        kept = lax.rem(offs_ref[level - 1, head], rate)
        row = lax.broadcasted_iota(jnp.int32, (tok, rows), 0)
        col = lax.broadcasted_iota(jnp.int32, (tok, rows), 1)
        parts.append((row == col * rate + kept).astype(F32))
    return jnp.concatenate(parts, axis=1).astype(BF16)


def pick_kernel(levels, heads, dim, offs_ref, core_ref, k_ref, v_ref, q_half, k_half, v_half,
                both_ref, three_ref, swap_ref):
    tok = k_ref.shape[0]
    n2, n3 = tok // 4, tok // 8
    for h in range(heads):
        head = pl.program_id(0) * heads + h
        pick = pick_matrix(offs_ref, head, 2, levels, tok)
        cols = slice(h * dim, (h + 1) * dim)
        kv = jnp.concatenate([k_ref[:, cols], v_ref[:, cols]], axis=1)
        got = dot(pick, kv).astype(BF16)
        out = slice(2 * h * dim, 2 * (h + 1) * dim)
        both_ref[:, out] = got
        three_ref[:, out] = got[n2 : n2 + n3]

    @pl.when(pl.program_id(0) == 0)
    def _():
        half = q_half.shape[1]
        for i, ref in enumerate((q_half, k_half, v_half)):
            swap_ref[:, i * half : (i + 1) * half] = ref[...]


def pick_call(offsets, core, queries, keys, values, dim):
    tok, width = keys.shape
    levels, heads = offsets.shape
    steps = 2
    per = heads // steps
    block = pl.BlockSpec((tok, per * dim), lambda i, o, c: (0, i))
    half = pl.BlockSpec((tok, width // 2), lambda i, o, c: (0, 1 - c[0]))
    return pl.pallas_call(
        functools.partial(pick_kernel, levels, per, dim),
        grid_spec=pltpu.PrefetchScalarGridSpec(
            num_scalar_prefetch=2,
            grid=(steps,),
            in_specs=[block, block, half, half, half],
            out_specs=[
                pl.BlockSpec((tok // 4 + tok // 8, 2 * per * dim), lambda i, o, c: (0, i)),
                pl.BlockSpec((tok // 8, 2 * per * dim), lambda i, o, c: (0, i)),
                pl.BlockSpec((tok, 3 * width // 2), lambda i, o, c: (0, 0)),
            ],
        ),
        out_shape=[
            jax.ShapeDtypeStruct((tok // 4 + tok // 8, 2 * width), BF16),
            jax.ShapeDtypeStruct((tok // 8, 2 * width), BF16),
            jax.ShapeDtypeStruct((tok, 3 * width // 2), BF16),
        ],
        compiler_params=params(),
        name="pick_rows",
    )(offsets, core, keys, values, queries, keys, values)


def own_spec(tok, cols, steps):
    return pl.BlockSpec((tok, cols), lambda i, o, c: (0, c[0] * steps + i))


def swap_spec(tok, cols, steps, part):
    return pl.BlockSpec((tok, cols), lambda i, o, c: (0, part * steps + i))


def side(*values):
    return jnp.concatenate(values, axis=1)


def stack(*values):
    return jnp.concatenate(values, axis=0)


def split(value, terms):
    parts = []
    for _ in range(terms):
        part = value.astype(BF16)
        parts.append(part)
        value = value - part.astype(F32)
    return parts


def local_scores(pick, levels, offs_ref, head, key0, key1, ones, que0, que1):
    tok, dim = key0.shape
    pos = lax.broadcasted_iota(jnp.int32, (1, 2 * tok), 1)
    bias = jnp.where(lax.rem(pos, 2) == lax.rem(offs_ref[0, head], 2), 0.0, NEG).astype(F32)
    s0 = side(dot_nt(key0, que0), dot_nt(key1, que1)) * dim**-0.5
    s1 = dot_nt(ones, stack(que0, que1)) * dim**-0.5 + bias
    return stack(s0, s1)


def pre_kernel(
    levels, per, dim, offs_ref, core_ref, q0, q1, k0, k1, v0, v1, exps, stats, near, selq
):
    tok = q0.shape[0]
    n1 = tok // 2
    heads = per * pl.num_programs(0)
    for h in range(per):
        head = core_ref[0] * heads + pl.program_id(0) * per + h
        pick = pick_matrix(offs_ref, head, 1, levels, tok)
        cols = slice(h * dim, (h + 1) * dim)
        wide = slice(2 * h * dim, 2 * (h + 1) * dim)
        lanes = slice(2 * h * tok, 2 * (h + 1) * tok)
        own = dot(pick, side(k0[:, cols], v0[:, cols])).astype(BF16)
        oth = dot(pick, side(k1[:, cols], v1[:, cols])).astype(BF16)
        ones = stack(own[:n1], oth[:n1])
        near[:, wide] = stack(ones, own[n1:], oth[n1:])
        que0, que1 = q0[:, cols], q1[:, cols]
        far_pick = pick[n1:]
        selq[:, cols] = stack(dot(far_pick, que0), dot(far_pick, que1)).astype(BF16)
        s = local_scores(
            pick, levels, offs_ref, head, k0[:, cols], k1[:, cols], ones[:, :dim], que0, que1
        )
        top = jnp.max(s, axis=0, keepdims=True)
        e = jnp.exp(s - top)
        exps[:, lanes] = e.astype(BF16)
        stats[0:1, lanes] = top
        stats[1:2, lanes] = jnp.sum(e, axis=0, keepdims=True)


def pre_call(offsets, core, raw, dim):
    tok, width = raw[0].shape
    levels, heads = offsets.shape
    half = heads // 2
    per = 8
    steps = half // per
    raw_spec = own_spec(tok, per * dim, steps)
    swapped = [swap_spec(tok, per * dim, steps, i) for i in range(3)]
    sel = 2 * (tok // 4 + tok // 8)

    def out(rows, lanes, kind=BF16):
        return (
            pl.BlockSpec((rows, per * lanes), lambda i, o, c: (0, i)),
            jax.ShapeDtypeStruct((rows, half * lanes), kind),
        )

    outs = [out(2 * tok, 2 * tok), out(8, 2 * tok, F32), out(tok + sel, 2 * dim), out(sel, dim)]
    return pl.pallas_call(
        functools.partial(pre_kernel, levels, per, dim),
        grid_spec=pltpu.PrefetchScalarGridSpec(
            num_scalar_prefetch=2,
            grid=(steps,),
            in_specs=[raw_spec, swapped[0], raw_spec, swapped[1], raw_spec, swapped[2]],
            out_specs=[o[0] for o in outs],
        ),
        out_shape=[o[1] for o in outs],
        compiler_params=params(),
        name="local_scores",
    )(offsets, core, *raw)


def far_kernel(
    levels, per, dim, offs_ref, core_ref, exps, stats, near, selq, v0, v1, g0, g1,
    x, xx, y3, yy3, d3, dd3,
    xa, xb, yab, da, db, ngrad, dqt, stats2,
):
    tok = g0.shape[0]
    n1, n2, n3 = tok // 2, tok // 4, tok // 8
    sel = n2 + n3
    scale = dim**-0.5
    heads = per * pl.num_programs(0)
    lane = lax.broadcasted_iota(jnp.int32, (1, 2 * sel), 1)
    is2 = lax.rem(lane, sel) < n2
    pos = lax.broadcasted_iota(jnp.int32, (1, 2 * tok), 1)
    first = core_ref[0] * heads + pl.program_id(0) * per
    each = range(per)
    cols = [slice(h * dim, (h + 1) * dim) for h in each]
    kc = [slice(2 * h * dim, (2 * h + 1) * dim) for h in each]
    vc = [slice((2 * h + 1) * dim, (2 * h + 2) * dim) for h in each]
    wide = [slice(2 * h * dim, 2 * (h + 1) * dim) for h in each]
    lanes = [slice(2 * h * tok, 2 * (h + 1) * tok) for h in each]

    def rows(c):
        a, b = near[tok : tok + sel, c], near[tok + sel :, c]
        return stack(
            a[:n2], b[:n2], x[:n2, c], xx[:n2, c], a[n2:], b[n2:], x[n2:, c], xx[n2:, c],
            *(ref[:, c] for ref in (y3, yy3, d3, dd3)),
        )

    def level_pick(value):
        return jnp.where(is2, value[:tok], value[tok:])

    picks = [pick_matrix(offs_ref, first + h, 2, levels, tok) for h in each]
    gsel = [
        stack(dot(picks[h], g0[:, cols[h]]), dot(picks[h], g1[:, cols[h]])).astype(BF16)
        for h in each
    ]
    keys = [rows(kc[h]) for h in each]
    s = [level_pick(dot_nt(keys[h], selq[:, cols[h]])) * scale for h in each]
    p = [level_pick(dot_nt(rows(vc[h]), gsel[h])) for h in each]
    dloc = []
    for h in each:
        gra0, gra1 = g0[:, cols[h]], g1[:, cols[h]]
        p0 = side(dot_nt(v0[:, cols[h]], gra0), dot_nt(v1[:, cols[h]], gra1))
        p1 = dot_nt(near[:tok, vc[h]], stack(gra0, gra1))
        ex = exps[:, lanes[h]]
        both = ex[:tok].astype(F32) * p0 + ex[tok:].astype(F32) * p1
        dloc.append(jnp.sum(both, axis=0, keepdims=True))
    top = [jnp.max(a, axis=0, keepdims=True) for a in s]
    e = [jnp.exp(a - b) for a, b in zip(s, top)]
    size = [jnp.sum(a, axis=0, keepdims=True) for a in e]
    dhat = [jnp.sum(a * b, axis=0, keepdims=True) for a, b in zip(e, p)]
    none = jnp.zeros_like(picks[0])
    spots = [stack(side(a, none), side(none, a)) for a in picks]
    spread = []
    for h in each:
        terms = stack(*split(top[h], 3), *split(size[h], 2), *split(dhat[h], 2))
        zero = jnp.zeros_like(terms)
        apart = stack(jnp.where(is2, terms, zero), jnp.where(is2, zero, terms))
        spread.append(dot(apart, spots[h]))
    back = []
    for h in each:

        def level_stats(level, lo):
            rate = 2**level
            on = lax.rem(pos, rate) == lax.rem(offs_ref[level - 1, first + h], rate)
            t = [spread[h][lo + i : lo + i + 1] for i in range(7)]
            return jnp.where(on, t[0] + t[1] + t[2], NEG), t[3] + t[4], t[5] + t[6]

        t1, z1 = stats[0:1, lanes[h]], stats[1:2, lanes[h]]
        t2, z2, dot2 = level_stats(2, 0)
        t3, z3, dot3 = level_stats(3, 7)
        high = jnp.maximum(t1, jnp.maximum(t2, t3))
        a1, a2, a3 = jnp.exp(t1 - high), jnp.exp(t2 - high), jnp.exp(t3 - high)
        inv = 1.0 / (a1 * z1 + a2 * z2 + a3 * z3)
        f1, f2, f3 = a1 * inv, a2 * inv, a3 * inv
        delta = f1 * dloc[h] + f2 * dot2 + f3 * dot3
        stats2[0:1, lanes[h]] = f1
        stats2[1:2, lanes[h]] = delta
        terms = stack(*split(f2, 2), *split(f3, 2), *split(delta, 2))
        back.append(dot_nt(terms, spots[h]))

    def apart(value):
        zero = jnp.zeros_like(value)
        return stack(jnp.where(is2, value, zero), jnp.where(is2, zero, value)).astype(BF16)

    dsm, wm = [], []
    for h in each:
        b = back[h]
        w = e[h] * jnp.where(is2, b[0:1] + b[1:2], b[2:3] + b[3:4])
        dsm.append(apart(w * (p[h] - (b[4:5] + b[5:6]))))
        wm.append(apart(w))
    dk = [dot(dsm[h], selq[:, cols[h]]) * scale for h in each]
    dv = [dot(wm[h], gsel[h]) for h in each]
    for h in each:
        dkv = side(dk[h], dv[h]).astype(BF16)
        xa[:n2, wide[h]] = dkv[2 * n2 : 3 * n2]
        xb[:n2, wide[h]] = dkv[3 * n2 : 4 * n2]
        third = [dkv[tok + i * n3 : tok + (i + 1) * n3] for i in range(8)]
        xa[n2:, wide[h]] = third[2]
        xb[n2:, wide[h]] = third[3]
        yab[:, wide[h]] = stack(third[4], third[5])
        da[:, wide[h]] = third[6]
        db[:, wide[h]] = third[7]
        ngrad[:, wide[h]] = stack(dkv[:n2], third[0], dkv[n2 : 2 * n2], third[1])
        dqt[:, h * dim : h * dim + 2 * sel] = dot(keys[h].T, dsm[h]).astype(BF16)


def far_call(offsets, core, pre, raw, far, dim):
    tok, width = raw[0].shape
    levels, heads = offsets.shape
    half = heads // 2
    per = 8
    steps = half // per
    n2, n3 = tok // 4, tok // 8
    raw_spec = own_spec(tok, per * dim, steps)
    swapped = [swap_spec(tok, per * dim, steps, i) for i in range(3)]

    def near_spec(a):
        return pl.BlockSpec((a.shape[0], a.shape[1] // steps), lambda i, o, c: (0, i))

    def far_spec(a):
        return pl.BlockSpec((a.shape[0], 2 * per * dim), lambda i, o, c: (0, c[0] * steps + i))

    def out(rows, lanes, kind=BF16):
        return (
            pl.BlockSpec((rows, per * lanes), lambda i, o, c: (0, i)),
            jax.ShapeDtypeStruct((rows, half * lanes), kind),
        )

    outs = [out(n2 + n3, 2 * dim)] * 2 + [out(2 * n3, 2 * dim)] + [out(n3, 2 * dim)] * 2
    outs += [out(2 * (n2 + n3), 2 * dim), out(dim, dim), out(8, 2 * tok, F32)]
    return pl.pallas_call(
        functools.partial(far_kernel, levels, per, dim),
        grid_spec=pltpu.PrefetchScalarGridSpec(
            num_scalar_prefetch=2,
            grid=(steps,),
            in_specs=[near_spec(a) for a in pre] + [raw_spec, swapped[2], raw_spec, raw_spec]
            + [far_spec(a) for a in far],
            out_specs=[o[0] for o in outs],
        ),
        out_shape=[o[1] for o in outs],
        compiler_params=params(),
        name="far_levels",
    )(offsets, core, *pre, *raw, *far)


def near_kernel(
    levels, per, dim, offs_ref, core_ref, exps, stats2, near, ngrad, dqt,
    q0, q1, k0, k1, v0, v1, g0, g1, mine, other,
):
    tok = q0.shape[0]
    n1 = tok // 2
    sel = tok // 4 + tok // 8
    scale = dim**-0.5
    heads = per * pl.num_programs(0)
    for h in range(per):
        head = core_ref[0] * heads + pl.program_id(0) * per + h
        pick = pick_matrix(offs_ref, head, 2, levels, tok)
        place = place_matrix(offs_ref, head, 1, levels, tok)
        cols = slice(h * dim, (h + 1) * dim)
        kc = slice(2 * h * dim, (2 * h + 1) * dim)
        vc = slice((2 * h + 1) * dim, (2 * h + 2) * dim)
        wide = slice(2 * h * dim, 2 * (h + 1) * dim)
        lanes = slice(2 * h * tok, 2 * (h + 1) * tok)
        que0, que1, gra0, gra1 = q0[:, cols], q1[:, cols], g0[:, cols], g1[:, cols]
        que, gra = stack(que0, que1), stack(gra0, gra1)
        p0 = side(dot_nt(v0[:, cols], gra0), dot_nt(v1[:, cols], gra1))
        p = stack(p0, dot_nt(near[:tok, vc], gra))
        w = exps[:, lanes].astype(F32) * stats2[0:1, lanes]
        wb = w.astype(BF16)
        ds = (w * (p - stats2[1:2, lanes])).astype(BF16)
        dkv1 = side(dot(ds[tok:], que) * scale, dot(wb[tok:], gra)).astype(BF16)
        ds0, ds1 = ds[:tok, :tok], ds[:tok, tok:]
        kv0 = side(dot(ds0, que0) * scale, dot(wb[:tok, :tok], gra0))
        kv1 = side(dot(ds1, que1) * scale, dot(wb[:tok, tok:], gra1))
        kv0 += dot(place, stack(dkv1[:n1], ngrad[:sel, wide]))
        kv1 += dot(place, stack(dkv1[n1:], ngrad[sel:, wide]))
        dqa = dot(near[:tok, kc].T, ds[tok:])
        dq0 = dqa[:, :tok] + dot(k0[:, cols].T, ds0)
        dq1 = dqa[:, tok:] + dot(k1[:, cols].T, ds1)
        dq0 += dot(dqt[:, h * dim : h * dim + sel], pick)
        dq1 += dot(dqt[:, h * dim + sel : h * dim + 2 * sel], pick)
        for ref, dq, kv in ((mine, dq0, kv0), (other, dq1, kv1)):
            lo = 3 * h * dim
            ref[:, lo : lo + dim] = (dq * scale).T.astype(BF16)
            ref[:, lo + dim : lo + 3 * dim] = kv.astype(BF16)


def near_call(offsets, core, mid, raw, dim):
    tok, width = raw[0].shape
    levels, heads = offsets.shape
    half = heads // 2
    per = 8
    steps = half // per
    raw_spec = own_spec(tok, per * dim, steps)
    swapped = [swap_spec(tok, per * dim, steps, i) for i in range(3)]

    def mid_spec(a):
        return pl.BlockSpec((a.shape[0], a.shape[1] // steps), lambda i, o, c: (0, i))

    out_spec = pl.BlockSpec((tok, 3 * per * dim), lambda i, o, c: (0, i))
    return pl.pallas_call(
        functools.partial(near_kernel, levels, per, dim),
        grid_spec=pltpu.PrefetchScalarGridSpec(
            num_scalar_prefetch=2,
            grid=(steps,),
            in_specs=[mid_spec(a) for a in mid]
            + [raw_spec, swapped[0], raw_spec, swapped[1], raw_spec, swapped[2], raw_spec, raw_spec],
            out_specs=[out_spec] * 2,
        ),
        out_shape=[jax.ShapeDtypeStruct((tok, 3 * half * dim), BF16)] * 2,
        compiler_params=params(),
        name="near_levels",
    )(offsets, core, *mid, *raw)


def final_kernel(
    levels, per, dim, offs_ref, core_ref, ba, bb, xa, xb, ya, yb, da, db, dq, dk, dv
):
    tok = dq.shape[0]
    n2, n3 = tok // 4, tok // 8
    heads = per * pl.num_programs(0)
    swap = pl.program_id(0) * 2 // pl.num_programs(0) != core_ref[0]

    def work(base, x, y, d):
        each = range(per)
        place = [
            place_matrix(offs_ref, pl.program_id(0) * per + h, 2, levels, tok) for h in each
        ]
        third = (x[n2:].astype(F32) + y[...].astype(F32) + d[...].astype(F32)).astype(BF16)
        src = [slice(2 * h * dim, 2 * (h + 1) * dim) for h in each]
        more = [dot(place[h], stack(x[:n2, src[h]], third[:, src[h]])) for h in each]
        for h in each:
            cols = slice(h * dim, (h + 1) * dim)
            lo = 3 * h * dim
            total = base[:, lo + dim : lo + 3 * dim].astype(F32) + more[h]
            dq[:, cols] = base[:, lo : lo + dim]
            dk[:, cols] = total[:, :dim].astype(BF16)
            dv[:, cols] = total[:, dim:].astype(BF16)

    @pl.when(jnp.logical_not(swap))
    def _():
        work(ba, xa, ya, da)

    @pl.when(swap)
    def _():
        work(bb, xb, yb, db)


def final_call(offsets, core, parts, dim):
    levels, heads = offsets.shape
    tok = parts[0].shape[0]
    steps = 2
    per = heads // steps
    third = tok // 8

    def spec(a, far, row, rows):
        cols = a.shape[1] * 2 // steps

        def where(i, o, c):
            turn = 1 - c[0] if far else c[0]
            return row, jnp.clip(i - turn * (steps // 2), 0, steps // 2 - 1)

        return pl.BlockSpec((rows, cols), where)

    specs = []
    for i, a in enumerate(parts):
        far = i % 2 == 1
        if i in (4, 5):
            specs.append(spec(a, far, 1 if far else 0, third))
        else:
            specs.append(spec(a, far, 0, a.shape[0]))
    out = pl.BlockSpec((tok, per * dim), lambda i, o, c: (0, i))
    return pl.pallas_call(
        functools.partial(final_kernel, levels, per, dim),
        grid_spec=pltpu.PrefetchScalarGridSpec(
            num_scalar_prefetch=2,
            grid=(steps,),
            in_specs=specs,
            out_specs=[out] * 3,
        ),
        out_shape=[jax.ShapeDtypeStruct((tok, heads * dim), BF16)] * 3,
        compiler_params=params(),
        name="add_pieces",
    )(offsets, core, *parts)


def per_device(queries, keys_in, values, out_grads, offsets):
    heads = offsets.shape[1]
    dim = queries.shape[2] // heads
    sections = lax.axis_size("section")
    core = lax.rem(lax.axis_index("seq"), 2).astype(jnp.int32).reshape(1)
    grads = lax.ppermute(
        out_grads[0], "section", [(i, (i - 1) % sections) for i in range(sections)]
    )
    q, k, v = (pltpu.with_memory_space_constraint(a[0], pltpu.HBM) for a in (queries, keys_in, values))
    both, three, swap = pick_call(offsets, core, q, k, v, dim)
    swap = exchange(swap, 1)
    x, y, d = exchange(both, 2), exchange(three, 4), exchange(three, 6)
    pre = pre_call(offsets, core, [q, swap, k, swap, v, swap], dim)
    x, y, d, grads = lax.optimization_barrier((x, y, d, grads, pre[1]))[:4]
    far = []
    for piece in (x, y, d):
        far += [piece, exchange(piece, 1)]
    g_oth = exchange(grads, 1)
    xa, xb, yab, da, db, ngrad, dqt, stats2 = far_call(
        offsets, core, pre, [v, swap, grads, g_oth], far, dim
    )
    xa, xb, da, db = exchange(xa, 2), exchange(xb, 3), exchange(da, 6), exchange(db, 7)
    y = exchange(yab, 4)
    yy = exchange(y, 1)
    mine, other = near_call(
        offsets, core, [pre[0], stats2, pre[2], ngrad, dqt],
        [q, swap, k, swap, v, swap, grads, g_oth], dim,
    )
    other, xa, xb, da, db, y = lax.optimization_barrier((other, xa, xb, da, db, y))
    parts = [mine, exchange(other, 1), xa, xb, y, yy, da, db]
    dq, dk, dv = final_call(offsets, core, parts, dim)
    return dq[None], dk[None], dv[None]


def solution(mesh):
    spec = P("section", "seq", None)
    return jax.shard_map(
        per_device,
        mesh=mesh,
        in_specs=(spec, spec, spec, spec, P()),
        out_specs=(spec, spec, spec),
        check_vma=False,
    )
```

```python
import functools

import jax
import jax.numpy as jnp
from jax import lax
from jax.experimental import pallas as pl
from jax.experimental.pallas import tpu as pltpu
from jax.sharding import PartitionSpec as P

F32 = jnp.float32
BF16 = jnp.bfloat16
NEG = -1e30
VMEM_LIMIT = 48 * 1024 * 1024


def params():
    return pltpu.CompilerParams(vmem_limit_bytes=VMEM_LIMIT)


def exchange(value, bits):
    count = lax.axis_size("seq")
    return lax.ppermute(value, "seq", [(i, i ^ bits) for i in range(count)])


def dot(a, b):
    return jnp.dot(a, b, preferred_element_type=F32)


def dot_nt(a, b):
    return lax.dot_general(a, b, (((1,), (1,)), ((), ())), preferred_element_type=F32)


def pick_matrix(offs_ref, head, first, levels, tok):
    parts = []
    for level in range(first, levels + 1):
        rate = 2**level
        rows = tok // rate
        kept = lax.rem(offs_ref[level - 1, head], rate)
        row = lax.broadcasted_iota(jnp.int32, (rows, tok), 0)
        col = lax.broadcasted_iota(jnp.int32, (rows, tok), 1)
        parts.append((col == row * rate + kept).astype(F32))
    return jnp.concatenate(parts, axis=0).astype(BF16)


def place_matrix(offs_ref, head, first, levels, tok):
    parts = []
    for level in range(first, levels + 1):
        rate = 2**level
        rows = tok // rate
        kept = lax.rem(offs_ref[level - 1, head], rate)
        row = lax.broadcasted_iota(jnp.int32, (tok, rows), 0)
        col = lax.broadcasted_iota(jnp.int32, (tok, rows), 1)
        parts.append((row == col * rate + kept).astype(F32))
    return jnp.concatenate(parts, axis=1).astype(BF16)


def pack_kernel(core_ref, rows, out):
    out[...] = rows[...]


def pack_call(core, rows):
    tok, width = rows.shape
    half = width // 2
    return pl.pallas_call(
        pack_kernel,
        grid_spec=pltpu.PrefetchScalarGridSpec(
            num_scalar_prefetch=1,
            grid=(1,),
            in_specs=[pl.BlockSpec((tok, half), lambda i, c: (0, 1 - c[0]))],
            out_specs=pl.BlockSpec((tok, half), lambda i, c: (0, 0)),
        ),
        out_shape=jax.ShapeDtypeStruct((tok, half), BF16),
        compiler_params=params(),
        name="pack_half",
    )(core, rows)


def pick_kernel(levels, per, dim, offs_ref, core_ref, k0, k1, v0, v1, both_ref, three_ref):
    tok = k0.shape[0]
    n2, n3 = tok // 4, tok // 8
    each = range(per)
    picks = [pick_matrix(offs_ref, core_ref[0] * per + h, 2, levels, tok) for h in each]
    cols = [slice(h * dim, (h + 1) * dim) for h in each]
    own = [dot(picks[h], side(k0[:, cols[h]], v0[:, cols[h]])).astype(BF16) for h in each]
    oth = [dot(picks[h], side(k1[:, cols[h]], v1[:, cols[h]])).astype(BF16) for h in each]
    for h in each:
        out = slice(2 * h * dim, 2 * (h + 1) * dim)
        third = stack(own[h][n2:], oth[h][n2:])
        both_ref[:, out] = stack(own[h][:n2], oth[h][:n2], third)
        three_ref[:, out] = third


def pick_call(offsets, core, raw, dim):
    tok, width = raw[0].shape
    levels, heads = offsets.shape
    per = heads // 2
    spec = own_spec(tok, per * dim, 1)

    def out(rows):
        return pl.BlockSpec((rows, 2 * per * dim), lambda i, o, c: (0, 0))

    return pl.pallas_call(
        functools.partial(pick_kernel, levels, per, dim),
        grid_spec=pltpu.PrefetchScalarGridSpec(
            num_scalar_prefetch=2,
            grid=(1,),
            in_specs=[spec] * 4,
            out_specs=[out(tok // 2 + tok // 4), out(tok // 4)],
        ),
        out_shape=[
            jax.ShapeDtypeStruct((tok // 2 + tok // 4, width), BF16),
            jax.ShapeDtypeStruct((tok // 4, width), BF16),
        ],
        compiler_params=params(),
        name="pick_rows",
    )(offsets, core, *raw)


def own_spec(tok, cols, steps):
    return pl.BlockSpec((tok, cols), lambda i, o, c: (0, c[0] * steps + i))


def side(*values):
    return jnp.concatenate(values, axis=1)


def stack(*values):
    return jnp.concatenate(values, axis=0)


def split(value, terms):
    parts = []
    for _ in range(terms):
        part = value.astype(BF16)
        parts.append(part)
        value = value - part.astype(F32)
    return parts


def local_scores(pick, levels, offs_ref, head, key0, key1, ones, que0, que1):
    tok, dim = key0.shape
    pos = lax.broadcasted_iota(jnp.int32, (1, 2 * tok), 1)
    bias = jnp.where(lax.rem(pos, 2) == lax.rem(offs_ref[0, head], 2), 0.0, NEG).astype(F32)
    s0 = side(dot_nt(key0, que0), dot_nt(key1, que1)) * dim**-0.5
    s1 = dot_nt(ones, stack(que0, que1)) * dim**-0.5 + bias
    return stack(s0, s1)


def pre_kernel(
    levels, per, dim, offs_ref, core_ref, q0, q1, k0, k1, v0, v1, exps, stats, near, selq
):
    tok = q0.shape[0]
    n1 = tok // 2
    heads = per * pl.num_programs(0)
    for h in range(per):
        head = core_ref[0] * heads + pl.program_id(0) * per + h
        pick = pick_matrix(offs_ref, head, 1, levels, tok)
        cols = slice(h * dim, (h + 1) * dim)
        wide = slice(2 * h * dim, 2 * (h + 1) * dim)
        lanes = slice(2 * h * tok, 2 * (h + 1) * tok)
        own = dot(pick[:n1], side(k0[:, cols], v0[:, cols])).astype(BF16)
        oth = dot(pick[:n1], side(k1[:, cols], v1[:, cols])).astype(BF16)
        ones = stack(own, oth)
        near[:, wide] = ones
        que0, que1 = q0[:, cols], q1[:, cols]
        far_pick = pick[n1:]
        selq[:, cols] = stack(dot(far_pick, que0), dot(far_pick, que1)).astype(BF16)
        s = local_scores(
            pick, levels, offs_ref, head, k0[:, cols], k1[:, cols], ones[:, :dim], que0, que1
        )
        top = jnp.max(s, axis=0, keepdims=True)
        e = jnp.exp(s - top)
        exps[:, lanes] = e.astype(BF16)
        stats[0:1, lanes] = top
        stats[1:2, lanes] = jnp.sum(e, axis=0, keepdims=True)


def pre_call(offsets, core, raw, dim):
    tok, width = raw[0].shape
    levels, heads = offsets.shape
    half = heads // 2
    per = 8
    steps = half // per
    raw_spec = own_spec(tok, per * dim, steps)
    sel = 2 * (tok // 4 + tok // 8)

    def out(rows, lanes, kind=BF16):
        return (
            pl.BlockSpec((rows, per * lanes), lambda i, o, c: (0, i)),
            jax.ShapeDtypeStruct((rows, half * lanes), kind),
        )

    outs = [out(2 * tok, 2 * tok), out(8, 2 * tok, F32), out(tok, 2 * dim), out(sel, dim)]
    return pl.pallas_call(
        functools.partial(pre_kernel, levels, per, dim),
        grid_spec=pltpu.PrefetchScalarGridSpec(
            num_scalar_prefetch=2,
            grid=(steps,),
            in_specs=[raw_spec] * 6,
            out_specs=[o[0] for o in outs],
        ),
        out_shape=[o[1] for o in outs],
        compiler_params=params(),
        name="local_scores",
    )(offsets, core, *raw)


def far_kernel(
    levels, per, dim, offs_ref, core_ref, exps, stats, near, selq, v0, v1, g0, g1,
    own, x, y, d,
    xa, xb, yab, da, db, ngrad, dqt, stats2,
):
    tok = g0.shape[0]
    n1, n2, n3 = tok // 2, tok // 4, tok // 8
    sel = n2 + n3
    scale = dim**-0.5
    heads = per * pl.num_programs(0)
    lane = lax.broadcasted_iota(jnp.int32, (1, 2 * sel), 1)
    is2 = lax.rem(lane, sel) < n2
    pos = lax.broadcasted_iota(jnp.int32, (1, 2 * tok), 1)
    first = core_ref[0] * heads + pl.program_id(0) * per
    each = range(per)
    cols = [slice(h * dim, (h + 1) * dim) for h in each]
    kc = [slice(2 * h * dim, (2 * h + 1) * dim) for h in each]
    vc = [slice((2 * h + 1) * dim, (2 * h + 2) * dim) for h in each]
    wide = [slice(2 * h * dim, 2 * (h + 1) * dim) for h in each]
    lanes = [slice(2 * h * tok, 2 * (h + 1) * tok) for h in each]

    def rows(c):
        lo = 2 * n2
        parts = own[:lo, c], x[:lo, c], own[lo:, c], x[lo:, c], y[:, c], d[:, c]
        return stack(*parts)

    def level_pick(value):
        return jnp.where(is2, value[:tok], value[tok:])

    picks = [pick_matrix(offs_ref, first + h, 2, levels, tok) for h in each]
    gsel = [
        stack(dot(picks[h], g0[:, cols[h]]), dot(picks[h], g1[:, cols[h]])).astype(BF16)
        for h in each
    ]
    keys = [rows(kc[h]) for h in each]
    s = [level_pick(dot_nt(keys[h], selq[:, cols[h]])) * scale for h in each]
    p = [level_pick(dot_nt(rows(vc[h]), gsel[h])) for h in each]
    dloc = []
    for h in each:
        gra0, gra1 = g0[:, cols[h]], g1[:, cols[h]]
        p0 = side(dot_nt(v0[:, cols[h]], gra0), dot_nt(v1[:, cols[h]], gra1))
        p1 = dot_nt(near[:tok, vc[h]], stack(gra0, gra1))
        ex = exps[:, lanes[h]]
        both = ex[:tok].astype(F32) * p0 + ex[tok:].astype(F32) * p1
        dloc.append(jnp.sum(both, axis=0, keepdims=True))
    top = [jnp.max(a, axis=0, keepdims=True) for a in s]
    e = [jnp.exp(a - b) for a, b in zip(s, top)]
    size = [jnp.sum(a, axis=0, keepdims=True) for a in e]
    dhat = [jnp.sum(a * b, axis=0, keepdims=True) for a, b in zip(e, p)]
    none = jnp.zeros_like(picks[0])
    spots = [stack(side(a, none), side(none, a)) for a in picks]
    spread = []
    for h in each:
        terms = stack(*split(top[h], 3), *split(size[h], 2), *split(dhat[h], 2))
        zero = jnp.zeros_like(terms)
        apart = stack(jnp.where(is2, terms, zero), jnp.where(is2, zero, terms))
        spread.append(dot(apart, spots[h]))
    back = []
    for h in each:

        def level_stats(level, lo):
            rate = 2**level
            on = lax.rem(pos, rate) == lax.rem(offs_ref[level - 1, first + h], rate)
            t = [spread[h][lo + i : lo + i + 1] for i in range(7)]
            return jnp.where(on, t[0] + t[1] + t[2], NEG), t[3] + t[4], t[5] + t[6]

        t1, z1 = stats[0:1, lanes[h]], stats[1:2, lanes[h]]
        t2, z2, dot2 = level_stats(2, 0)
        t3, z3, dot3 = level_stats(3, 7)
        high = jnp.maximum(t1, jnp.maximum(t2, t3))
        a1, a2, a3 = jnp.exp(t1 - high), jnp.exp(t2 - high), jnp.exp(t3 - high)
        inv = 1.0 / (a1 * z1 + a2 * z2 + a3 * z3)
        f1, f2, f3 = a1 * inv, a2 * inv, a3 * inv
        delta = f1 * dloc[h] + f2 * dot2 + f3 * dot3
        stats2[0:1, lanes[h]] = f1
        stats2[1:2, lanes[h]] = delta
        terms = stack(*split(f2, 2), *split(f3, 2), *split(delta, 2))
        back.append(dot_nt(terms, spots[h]))

    def apart(value):
        zero = jnp.zeros_like(value)
        return stack(jnp.where(is2, value, zero), jnp.where(is2, zero, value)).astype(BF16)

    dsm, wm = [], []
    for h in each:
        b = back[h]
        w = e[h] * jnp.where(is2, b[0:1] + b[1:2], b[2:3] + b[3:4])
        dsm.append(apart(w * (p[h] - (b[4:5] + b[5:6]))))
        wm.append(apart(w))
    dk = [dot(dsm[h], selq[:, cols[h]]) * scale for h in each]
    dv = [dot(wm[h], gsel[h]) for h in each]
    for h in each:
        dkv = side(dk[h], dv[h]).astype(BF16)
        xa[:n2, wide[h]] = dkv[2 * n2 : 3 * n2]
        xb[:n2, wide[h]] = dkv[3 * n2 : 4 * n2]
        third = [dkv[tok + i * n3 : tok + (i + 1) * n3] for i in range(8)]
        xa[n2:, wide[h]] = third[2]
        xb[n2:, wide[h]] = third[3]
        yab[:, wide[h]] = stack(third[4], third[5])
        da[:, wide[h]] = third[6]
        db[:, wide[h]] = third[7]
        ngrad[:, wide[h]] = stack(dkv[:n2], third[0], dkv[n2 : 2 * n2], third[1])
        dqt[:, h * dim : h * dim + 2 * sel] = dot(keys[h].T, dsm[h]).astype(BF16)


def far_call(offsets, core, pre, raw, grads, far, dim):
    tok, width = raw[0].shape
    levels, heads = offsets.shape
    half = heads // 2
    per = 8
    steps = half // per
    n2, n3 = tok // 4, tok // 8
    raw_spec = own_spec(tok, per * dim, steps)

    def mid_spec(a):
        return pl.BlockSpec((a.shape[0], a.shape[1] // steps), lambda i, o, c: (0, i))

    def out(rows, lanes, kind=BF16):
        return (
            pl.BlockSpec((rows, per * lanes), lambda i, o, c: (0, i)),
            jax.ShapeDtypeStruct((rows, half * lanes), kind),
        )

    outs = [out(n2 + n3, 2 * dim)] * 2 + [out(2 * n3, 2 * dim)] + [out(n3, 2 * dim)] * 2
    outs += [out(2 * (n2 + n3), 2 * dim), out(dim, dim), out(8, 2 * tok, F32)]
    return pl.pallas_call(
        functools.partial(far_kernel, levels, per, dim),
        grid_spec=pltpu.PrefetchScalarGridSpec(
            num_scalar_prefetch=2,
            grid=(steps,),
            in_specs=[mid_spec(a) for a in pre] + [raw_spec] * 2
            + [raw_spec] + [mid_spec(a) for a in grads[1:] + far],
            out_specs=[o[0] for o in outs],
        ),
        out_shape=[o[1] for o in outs],
        compiler_params=params(),
        name="far_levels",
    )(offsets, core, *pre, *raw, *grads, *far)


def near_kernel(
    levels, per, dim, offs_ref, core_ref, exps, stats2, near, ngrad, dqt,
    q0, q1, k0, k1, v0, v1, g0, g1, mine, other,
):
    tok = q0.shape[0]
    n1 = tok // 2
    sel = tok // 4 + tok // 8
    scale = dim**-0.5
    heads = per * pl.num_programs(0)
    for h in range(per):
        head = core_ref[0] * heads + pl.program_id(0) * per + h
        pick = pick_matrix(offs_ref, head, 2, levels, tok)
        place = place_matrix(offs_ref, head, 1, levels, tok)
        cols = slice(h * dim, (h + 1) * dim)
        kc = slice(2 * h * dim, (2 * h + 1) * dim)
        vc = slice((2 * h + 1) * dim, (2 * h + 2) * dim)
        wide = slice(2 * h * dim, 2 * (h + 1) * dim)
        lanes = slice(2 * h * tok, 2 * (h + 1) * tok)
        que0, que1, gra0, gra1 = q0[:, cols], q1[:, cols], g0[:, cols], g1[:, cols]
        que, gra = stack(que0, que1), stack(gra0, gra1)
        p0 = side(dot_nt(v0[:, cols], gra0), dot_nt(v1[:, cols], gra1))
        p = stack(p0, dot_nt(near[:tok, vc], gra))
        w = exps[:, lanes].astype(F32) * stats2[0:1, lanes]
        wb = w.astype(BF16)
        ds = (w * (p - stats2[1:2, lanes])).astype(BF16)
        dkv1 = side(dot(ds[tok:], que) * scale, dot(wb[tok:], gra)).astype(BF16)
        ds0, ds1 = ds[:tok, :tok], ds[:tok, tok:]
        kv0 = side(dot(ds0, que0) * scale, dot(wb[:tok, :tok], gra0))
        kv1 = side(dot(ds1, que1) * scale, dot(wb[:tok, tok:], gra1))
        kv0 += dot(place, stack(dkv1[:n1], ngrad[:sel, wide]))
        kv1 += dot(place, stack(dkv1[n1:], ngrad[sel:, wide]))
        dqa = dot(near[:tok, kc].T, ds[tok:])
        dq0 = dqa[:, :tok] + dot(k0[:, cols].T, ds0)
        dq1 = dqa[:, tok:] + dot(k1[:, cols].T, ds1)
        dq0 += dot(dqt[:, h * dim : h * dim + sel], pick)
        dq1 += dot(dqt[:, h * dim + sel : h * dim + 2 * sel], pick)
        for ref, dq, kv in ((mine, dq0, kv0), (other, dq1, kv1)):
            lo = 3 * h * dim
            ref[:, lo : lo + dim] = (dq * scale).T.astype(BF16)
            ref[:, lo + dim : lo + 3 * dim] = kv.astype(BF16)


def near_call(offsets, core, mid, raw, grads, dim):
    tok, width = raw[0].shape
    levels, heads = offsets.shape
    half = heads // 2
    per = 8
    steps = half // per
    raw_spec = own_spec(tok, per * dim, steps)

    def mid_spec(a):
        return pl.BlockSpec((a.shape[0], a.shape[1] // steps), lambda i, o, c: (0, i))

    out_spec = pl.BlockSpec((tok, 3 * per * dim), lambda i, o, c: (0, i))
    return pl.pallas_call(
        functools.partial(near_kernel, levels, per, dim),
        grid_spec=pltpu.PrefetchScalarGridSpec(
            num_scalar_prefetch=2,
            grid=(steps,),
            in_specs=[mid_spec(a) for a in mid] + [raw_spec] * 7 + [mid_spec(grads[1])],
            out_specs=[out_spec] * 2,
        ),
        out_shape=[jax.ShapeDtypeStruct((tok, 3 * half * dim), BF16)] * 2,
        compiler_params=params(),
        name="near_levels",
    )(offsets, core, *mid, *raw, *grads)


def final_kernel(
    levels, per, dim, offs_ref, core_ref, ba, bb, xa, xb, ya, yb, da, db, dq, dk, dv
):
    tok = dq.shape[0]
    n2, n3 = tok // 4, tok // 8
    heads = per * pl.num_programs(0)
    swap = pl.program_id(0) * 2 // pl.num_programs(0) != core_ref[0]

    def work(base, x, y, d):
        each = range(per)
        place = [
            place_matrix(offs_ref, pl.program_id(0) * per + h, 2, levels, tok) for h in each
        ]
        third = (x[n2:].astype(F32) + y[...].astype(F32) + d[...].astype(F32)).astype(BF16)
        src = [slice(2 * h * dim, 2 * (h + 1) * dim) for h in each]
        more = [dot(place[h], stack(x[:n2, src[h]], third[:, src[h]])) for h in each]
        for h in each:
            cols = slice(h * dim, (h + 1) * dim)
            lo = 3 * h * dim
            total = base[:, lo + dim : lo + 3 * dim].astype(F32) + more[h]
            dq[:, cols] = base[:, lo : lo + dim]
            dk[:, cols] = total[:, :dim].astype(BF16)
            dv[:, cols] = total[:, dim:].astype(BF16)

    @pl.when(jnp.logical_not(swap))
    def _():
        work(ba, xa, ya, da)

    @pl.when(swap)
    def _():
        work(bb, xb, yb, db)


def final_call(offsets, core, parts, dim):
    levels, heads = offsets.shape
    tok = parts[0].shape[0]
    steps = 2
    per = heads // steps
    third = tok // 8

    def spec(a, far, row, rows):
        cols = a.shape[1] * 2 // steps

        def where(i, o, c):
            turn = 1 - c[0] if far else c[0]
            return row, jnp.clip(i - turn * (steps // 2), 0, steps // 2 - 1)

        return pl.BlockSpec((rows, cols), where)

    specs = []
    for i, a in enumerate(parts):
        far = i % 2 == 1
        if i in (4, 5):
            specs.append(spec(a, far, 1 if far else 0, third))
        else:
            specs.append(spec(a, far, 0, a.shape[0]))
    out = pl.BlockSpec((tok, per * dim), lambda i, o, c: (0, i))
    return pl.pallas_call(
        functools.partial(final_kernel, levels, per, dim),
        grid_spec=pltpu.PrefetchScalarGridSpec(
            num_scalar_prefetch=2,
            grid=(steps,),
            in_specs=specs,
            out_specs=[out] * 3,
        ),
        out_shape=[jax.ShapeDtypeStruct((tok, heads * dim), BF16)] * 3,
        compiler_params=params(),
        name="add_pieces",
    )(offsets, core, *parts)


def per_device(queries, keys_in, values, out_grads, offsets):
    heads = offsets.shape[1]
    dim = queries.shape[2] // heads
    core = lax.rem(lax.axis_index("seq"), 2).astype(jnp.int32).reshape(1)
    q, k, v = (
        pltpu.with_memory_space_constraint(a[0], pltpu.HBM) for a in (queries, keys_in, values)
    )
    sections = lax.axis_size("section")
    grads = lax.ppermute(
        out_grads[0], "section", [(i, (i - 1) % sections) for i in range(sections)]
    )
    q_oth, k_oth, v_oth = exchange(q, 1), exchange(k, 1), exchange(v, 1)
    both, three = pick_call(offsets, core, [k, k_oth, v, v_oth], dim)
    x, y, d = exchange(both, 2), exchange(three, 4), exchange(three, 6)
    raw = [q, q_oth, k, k_oth, v, v_oth]
    pre = pre_call(offsets, core, raw, dim)
    y, d, grads = lax.optimization_barrier((y, d, grads, pre[1]))[:3]
    grads = [grads, exchange(pack_call(core, grads), 1)]
    xa, xb, yab, da, db, ngrad, dqt, stats2 = far_call(
        offsets, core, pre, [v, v_oth], grads, [both, x, y, d], dim
    )
    xa, xb, da, db = exchange(xa, 2), exchange(xb, 3), exchange(da, 6), exchange(db, 7)
    y = exchange(yab, 4)
    yy = exchange(y, 1)
    mine, other = near_call(
        offsets, core, [pre[0], stats2, pre[2], ngrad, dqt], raw, grads, dim
    )
    other, xa, xb, da, db, y = lax.optimization_barrier((other, xa, xb, da, db, y))
    parts = [mine, exchange(other, 1), xa, xb, y, yy, da, db]
    dq, dk, dv = final_call(offsets, core, parts, dim)
    return dq[None], dk[None], dv[None]


def solution(mesh):
    spec = P("section", "seq", None)
    return jax.shard_map(
        per_device,
        mesh=mesh,
        in_specs=(spec, spec, spec, spec, P()),
        out_specs=(spec, spec, spec),
        check_vma=False,
    )
```

```python
import functools

import jax
import jax.numpy as jnp
from jax import lax
from jax.experimental import pallas as pl
from jax.experimental.pallas import tpu as pltpu
from jax.sharding import PartitionSpec as P

F32 = jnp.float32
BF16 = jnp.bfloat16
NEG = -1e30
VMEM_LIMIT = 32 * 1024 * 1024


def params():
    return pltpu.CompilerParams(vmem_limit_bytes=VMEM_LIMIT)


def exchange(value, bits):
    count = lax.axis_size("seq")
    return lax.ppermute(value, "seq", [(i, i ^ bits) for i in range(count)])


def dot(a, b):
    return jnp.dot(a, b, preferred_element_type=F32)


def dot_nt(a, b):
    return lax.dot_general(a, b, (((1,), (1,)), ((), ())), preferred_element_type=F32)


def pick_matrix(offs_ref, head, first, levels, tok):
    parts = []
    for level in range(first, levels + 1):
        rate = 2**level
        rows = tok // rate
        kept = lax.rem(offs_ref[level - 1, head], rate)
        row = lax.broadcasted_iota(jnp.int32, (rows, tok), 0)
        col = lax.broadcasted_iota(jnp.int32, (rows, tok), 1)
        parts.append((col == row * rate + kept).astype(F32))
    return jnp.concatenate(parts, axis=0).astype(BF16)


def place_matrix(offs_ref, head, first, levels, tok):
    parts = []
    for level in range(first, levels + 1):
        rate = 2**level
        rows = tok // rate
        kept = lax.rem(offs_ref[level - 1, head], rate)
        row = lax.broadcasted_iota(jnp.int32, (tok, rows), 0)
        col = lax.broadcasted_iota(jnp.int32, (tok, rows), 1)
        parts.append((row == col * rate + kept).astype(F32))
    return jnp.concatenate(parts, axis=1).astype(BF16)


def pack_kernel(core_ref, rows, out):
    out[...] = rows[...]


def pack_call(core, rows):
    tok, width = rows.shape
    half = width // 2
    return pl.pallas_call(
        pack_kernel,
        grid_spec=pltpu.PrefetchScalarGridSpec(
            num_scalar_prefetch=1,
            grid=(1,),
            in_specs=[pl.BlockSpec((tok, half), lambda i, c: (0, 1 - c[0]))],
            out_specs=pl.BlockSpec((tok, half), lambda i, c: (0, 0)),
        ),
        out_shape=jax.ShapeDtypeStruct((tok, half), BF16),
        compiler_params=params(),
        name="pack_half",
    )(core, rows)


def pick_kernel(levels, per, dim, offs_ref, core_ref, k0, k1, v0, v1, both_ref, three_ref):
    tok = k0.shape[0]
    n2, n3 = tok // 4, tok // 8
    each = range(per)
    picks = [pick_matrix(offs_ref, core_ref[0] * per + h, 2, levels, tok) for h in each]
    cols = [slice(h * dim, (h + 1) * dim) for h in each]
    own = [dot(picks[h], side(k0[:, cols[h]], v0[:, cols[h]])).astype(BF16) for h in each]
    oth = [dot(picks[h], side(k1[:, cols[h]], v1[:, cols[h]])).astype(BF16) for h in each]
    for h in each:
        out = slice(2 * h * dim, 2 * (h + 1) * dim)
        third = stack(own[h][n2:], oth[h][n2:])
        both_ref[:, out] = stack(own[h][:n2], oth[h][:n2], third)
        three_ref[:, out] = third


def pick_call(offsets, core, raw, dim):
    tok, width = raw[0].shape
    levels, heads = offsets.shape
    per = heads // 2
    spec = own_spec(tok, per * dim, 1)

    def out(rows):
        return pl.BlockSpec((rows, 2 * per * dim), lambda i, o, c: (0, 0))

    return pl.pallas_call(
        functools.partial(pick_kernel, levels, per, dim),
        grid_spec=pltpu.PrefetchScalarGridSpec(
            num_scalar_prefetch=2,
            grid=(1,),
            in_specs=[spec] * 4,
            out_specs=[out(tok // 2 + tok // 4), out(tok // 4)],
        ),
        out_shape=[
            jax.ShapeDtypeStruct((tok // 2 + tok // 4, width), BF16),
            jax.ShapeDtypeStruct((tok // 4, width), BF16),
        ],
        compiler_params=params(),
        name="pick_rows",
    )(offsets, core, *raw)


def own_spec(tok, cols, steps):
    return pl.BlockSpec((tok, cols), lambda i, o, c: (0, c[0] * steps + i))


def side(*values):
    return jnp.concatenate(values, axis=1)


def stack(*values):
    return jnp.concatenate(values, axis=0)


def split(value, terms):
    parts = []
    for _ in range(terms):
        part = value.astype(BF16)
        parts.append(part)
        value = value - part.astype(F32)
    return parts


def local_scores(pick, levels, offs_ref, head, key0, key1, ones, que0, que1):
    tok, dim = key0.shape
    pos = lax.broadcasted_iota(jnp.int32, (1, 2 * tok), 1)
    bias = jnp.where(lax.rem(pos, 2) == lax.rem(offs_ref[0, head], 2), 0.0, NEG).astype(F32)
    s0 = side(dot_nt(key0, que0), dot_nt(key1, que1)) * dim**-0.5
    s1 = dot_nt(ones, stack(que0, que1)) * dim**-0.5 + bias
    return stack(s0, s1)


def pre_kernel(
    levels, per, dim, offs_ref, core_ref, q0, q1, k0, k1, v0, v1, exps, stats, near, selq
):
    tok = q0.shape[0]
    n1 = tok // 2
    heads = per * pl.num_programs(0)
    for h in range(per):
        head = core_ref[0] * heads + pl.program_id(0) * per + h
        pick = pick_matrix(offs_ref, head, 1, levels, tok)
        cols = slice(h * dim, (h + 1) * dim)
        wide = slice(2 * h * dim, 2 * (h + 1) * dim)
        lanes = slice(2 * h * tok, 2 * (h + 1) * tok)
        own = dot(pick[:n1], side(k0[:, cols], v0[:, cols])).astype(BF16)
        oth = dot(pick[:n1], side(k1[:, cols], v1[:, cols])).astype(BF16)
        ones = stack(own, oth)
        near[:, wide] = ones
        que0, que1 = q0[:, cols], q1[:, cols]
        far_pick = pick[n1:]
        selq[:, cols] = stack(dot(far_pick, que0), dot(far_pick, que1)).astype(BF16)
        s = local_scores(
            pick, levels, offs_ref, head, k0[:, cols], k1[:, cols], ones[:, :dim], que0, que1
        )
        top = jnp.max(s, axis=0, keepdims=True)
        e = jnp.exp(s - top)
        exps[:, lanes] = e.astype(BF16)
        stats[0:1, lanes] = top
        stats[1:2, lanes] = jnp.sum(e, axis=0, keepdims=True)


def pre_call(offsets, core, raw, dim):
    tok, width = raw[0].shape
    levels, heads = offsets.shape
    half = heads // 2
    per = 8
    steps = half // per
    raw_spec = own_spec(tok, per * dim, steps)
    sel = 2 * (tok // 4 + tok // 8)

    def out(rows, lanes, kind=BF16):
        return (
            pl.BlockSpec((rows, per * lanes), lambda i, o, c: (0, i)),
            jax.ShapeDtypeStruct((rows, half * lanes), kind),
        )

    outs = [out(2 * tok, 2 * tok), out(8, 2 * tok, F32), out(tok, 2 * dim), out(sel, dim)]
    return pl.pallas_call(
        functools.partial(pre_kernel, levels, per, dim),
        grid_spec=pltpu.PrefetchScalarGridSpec(
            num_scalar_prefetch=2,
            grid=(steps,),
            in_specs=[raw_spec] * 6,
            out_specs=[o[0] for o in outs],
        ),
        out_shape=[o[1] for o in outs],
        compiler_params=params(),
        name="local_scores",
    )(offsets, core, *raw)


def far_kernel(
    levels, per, dim, offs_ref, core_ref, exps, stats, near, selq, v0, v1, g0, g1,
    own, x, y, d,
    xa, xb, yab, da, db, ngrad, dqt, stats2,
):
    tok = g0.shape[0]
    n1, n2, n3 = tok // 2, tok // 4, tok // 8
    sel = n2 + n3
    scale = dim**-0.5
    heads = per * pl.num_programs(0)
    lane = lax.broadcasted_iota(jnp.int32, (1, 2 * sel), 1)
    is2 = lax.rem(lane, sel) < n2
    pos = lax.broadcasted_iota(jnp.int32, (1, 2 * tok), 1)
    first = core_ref[0] * heads + pl.program_id(0) * per
    each = range(per)
    cols = [slice(h * dim, (h + 1) * dim) for h in each]
    kc = [slice(2 * h * dim, (2 * h + 1) * dim) for h in each]
    vc = [slice((2 * h + 1) * dim, (2 * h + 2) * dim) for h in each]
    wide = [slice(2 * h * dim, 2 * (h + 1) * dim) for h in each]
    lanes = [slice(2 * h * tok, 2 * (h + 1) * tok) for h in each]

    def rows(c):
        lo = 2 * n2
        parts = own[:lo, c], x[:lo, c], own[lo:, c], x[lo:, c], y[:, c], d[:, c]
        return stack(*parts)

    def level_pick(value):
        return jnp.where(is2, value[:tok], value[tok:])

    picks = [pick_matrix(offs_ref, first + h, 2, levels, tok) for h in each]
    gsel = [
        stack(dot(picks[h], g0[:, cols[h]]), dot(picks[h], g1[:, cols[h]])).astype(BF16)
        for h in each
    ]
    keys = [rows(kc[h]) for h in each]
    s = [level_pick(dot_nt(keys[h], selq[:, cols[h]])) * scale for h in each]
    p = [level_pick(dot_nt(rows(vc[h]), gsel[h])) for h in each]
    dloc = []
    for h in each:
        gra0, gra1 = g0[:, cols[h]], g1[:, cols[h]]
        p0 = side(dot_nt(v0[:, cols[h]], gra0), dot_nt(v1[:, cols[h]], gra1))
        p1 = dot_nt(near[:tok, vc[h]], stack(gra0, gra1))
        ex = exps[:, lanes[h]]
        both = ex[:tok].astype(F32) * p0 + ex[tok:].astype(F32) * p1
        dloc.append(jnp.sum(both, axis=0, keepdims=True))
    top = [jnp.max(a, axis=0, keepdims=True) for a in s]
    e = [jnp.exp(a - b) for a, b in zip(s, top)]
    size = [jnp.sum(a, axis=0, keepdims=True) for a in e]
    dhat = [jnp.sum(a * b, axis=0, keepdims=True) for a, b in zip(e, p)]
    none = jnp.zeros_like(picks[0])
    spots = [stack(side(a, none), side(none, a)) for a in picks]
    spread = []
    for h in each:
        terms = stack(*split(top[h], 3), *split(size[h], 2), *split(dhat[h], 2))
        zero = jnp.zeros_like(terms)
        apart = stack(jnp.where(is2, terms, zero), jnp.where(is2, zero, terms))
        spread.append(dot(apart, spots[h]))
    back = []
    for h in each:

        def level_stats(level, lo):
            rate = 2**level
            on = lax.rem(pos, rate) == lax.rem(offs_ref[level - 1, first + h], rate)
            t = [spread[h][lo + i : lo + i + 1] for i in range(7)]
            return jnp.where(on, t[0] + t[1] + t[2], NEG), t[3] + t[4], t[5] + t[6]

        t1, z1 = stats[0:1, lanes[h]], stats[1:2, lanes[h]]
        t2, z2, dot2 = level_stats(2, 0)
        t3, z3, dot3 = level_stats(3, 7)
        high = jnp.maximum(t1, jnp.maximum(t2, t3))
        a1, a2, a3 = jnp.exp(t1 - high), jnp.exp(t2 - high), jnp.exp(t3 - high)
        inv = 1.0 / (a1 * z1 + a2 * z2 + a3 * z3)
        f1, f2, f3 = a1 * inv, a2 * inv, a3 * inv
        delta = f1 * dloc[h] + f2 * dot2 + f3 * dot3
        stats2[0:1, lanes[h]] = f1
        stats2[1:2, lanes[h]] = delta
        terms = stack(*split(f2, 2), *split(f3, 2), *split(delta, 2))
        back.append(dot_nt(terms, spots[h]))

    def apart(value):
        zero = jnp.zeros_like(value)
        return stack(jnp.where(is2, value, zero), jnp.where(is2, zero, value)).astype(BF16)

    dsm, wm = [], []
    for h in each:
        b = back[h]
        w = e[h] * jnp.where(is2, b[0:1] + b[1:2], b[2:3] + b[3:4])
        dsm.append(apart(w * (p[h] - (b[4:5] + b[5:6]))))
        wm.append(apart(w))
    dk = [dot(dsm[h], selq[:, cols[h]]) * scale for h in each]
    dv = [dot(wm[h], gsel[h]) for h in each]
    for h in each:
        dkv = side(dk[h], dv[h]).astype(BF16)
        xa[:n2, wide[h]] = dkv[2 * n2 : 3 * n2]
        xb[:n2, wide[h]] = dkv[3 * n2 : 4 * n2]
        third = [dkv[tok + i * n3 : tok + (i + 1) * n3] for i in range(8)]
        xa[n2:, wide[h]] = third[2]
        xb[n2:, wide[h]] = third[3]
        yab[:, wide[h]] = stack(third[4], third[5])
        da[:, wide[h]] = third[6]
        db[:, wide[h]] = third[7]
        ngrad[:, wide[h]] = stack(dkv[:n2], third[0], dkv[n2 : 2 * n2], third[1])
        dqt[:, h * dim : h * dim + 2 * sel] = dot(keys[h].T, dsm[h]).astype(BF16)


def far_call(offsets, core, pre, raw, grads, far, dim):
    tok, width = raw[0].shape
    levels, heads = offsets.shape
    half = heads // 2
    per = 8
    steps = half // per
    n2, n3 = tok // 4, tok // 8
    raw_spec = own_spec(tok, per * dim, steps)

    def mid_spec(a):
        return pl.BlockSpec((a.shape[0], a.shape[1] // steps), lambda i, o, c: (0, i))

    def out(rows, lanes, kind=BF16):
        return (
            pl.BlockSpec((rows, per * lanes), lambda i, o, c: (0, i)),
            jax.ShapeDtypeStruct((rows, half * lanes), kind),
        )

    outs = [out(n2 + n3, 2 * dim)] * 2 + [out(2 * n3, 2 * dim)] + [out(n3, 2 * dim)] * 2
    outs += [out(2 * (n2 + n3), 2 * dim), out(dim, dim), out(8, 2 * tok, F32)]
    return pl.pallas_call(
        functools.partial(far_kernel, levels, per, dim),
        grid_spec=pltpu.PrefetchScalarGridSpec(
            num_scalar_prefetch=2,
            grid=(steps,),
            in_specs=[mid_spec(a) for a in pre] + [raw_spec] * 2
            + [raw_spec] + [mid_spec(a) for a in grads[1:] + far],
            out_specs=[o[0] for o in outs],
        ),
        out_shape=[o[1] for o in outs],
        compiler_params=params(),
        name="far_levels",
    )(offsets, core, *pre, *raw, *grads, *far)


def near_kernel(
    levels, per, dim, offs_ref, core_ref, exps, stats2, near, ngrad, dqt,
    q0, q1, k0, k1, v0, v1, g0, g1, mine, other,
):
    tok = q0.shape[0]
    n1 = tok // 2
    sel = tok // 4 + tok // 8
    scale = dim**-0.5
    heads = per * pl.num_programs(0)
    for h in range(per):
        head = core_ref[0] * heads + pl.program_id(0) * per + h
        pick = pick_matrix(offs_ref, head, 2, levels, tok)
        place = place_matrix(offs_ref, head, 1, levels, tok)
        cols = slice(h * dim, (h + 1) * dim)
        kc = slice(2 * h * dim, (2 * h + 1) * dim)
        vc = slice((2 * h + 1) * dim, (2 * h + 2) * dim)
        wide = slice(2 * h * dim, 2 * (h + 1) * dim)
        lanes = slice(2 * h * tok, 2 * (h + 1) * tok)
        que0, que1, gra0, gra1 = q0[:, cols], q1[:, cols], g0[:, cols], g1[:, cols]
        que, gra = stack(que0, que1), stack(gra0, gra1)
        p0 = side(dot_nt(v0[:, cols], gra0), dot_nt(v1[:, cols], gra1))
        p = stack(p0, dot_nt(near[:tok, vc], gra))
        w = exps[:, lanes].astype(F32) * stats2[0:1, lanes]
        wb = w.astype(BF16)
        ds = (w * (p - stats2[1:2, lanes])).astype(BF16)
        dkv1 = side(dot(ds[tok:], que) * scale, dot(wb[tok:], gra)).astype(BF16)
        ds0, ds1 = ds[:tok, :tok], ds[:tok, tok:]
        kv0 = side(dot(ds0, que0) * scale, dot(wb[:tok, :tok], gra0))
        kv1 = side(dot(ds1, que1) * scale, dot(wb[:tok, tok:], gra1))
        kv0 += dot(place, stack(dkv1[:n1], ngrad[:sel, wide]))
        kv1 += dot(place, stack(dkv1[n1:], ngrad[sel:, wide]))
        dqa = dot(near[:tok, kc].T, ds[tok:])
        dq0 = dqa[:, :tok] + dot(k0[:, cols].T, ds0)
        dq1 = dqa[:, tok:] + dot(k1[:, cols].T, ds1)
        dq0 += dot(dqt[:, h * dim : h * dim + sel], pick)
        dq1 += dot(dqt[:, h * dim + sel : h * dim + 2 * sel], pick)
        for ref, dq, kv in ((mine, dq0, kv0), (other, dq1, kv1)):
            lo = 3 * h * dim
            ref[:, lo : lo + dim] = (dq * scale).T.astype(BF16)
            ref[:, lo + dim : lo + 3 * dim] = kv.astype(BF16)


def near_call(offsets, core, mid, raw, grads, dim):
    tok, width = raw[0].shape
    levels, heads = offsets.shape
    half = heads // 2
    per = 8
    steps = half // per
    raw_spec = own_spec(tok, per * dim, steps)

    def mid_spec(a):
        return pl.BlockSpec((a.shape[0], a.shape[1] // steps), lambda i, o, c: (0, i))

    out_spec = pl.BlockSpec((tok, 3 * per * dim), lambda i, o, c: (0, i))
    return pl.pallas_call(
        functools.partial(near_kernel, levels, per, dim),
        grid_spec=pltpu.PrefetchScalarGridSpec(
            num_scalar_prefetch=2,
            grid=(steps,),
            in_specs=[mid_spec(a) for a in mid] + [raw_spec] * 7 + [mid_spec(grads[1])],
            out_specs=[out_spec] * 2,
        ),
        out_shape=[jax.ShapeDtypeStruct((tok, 3 * half * dim), BF16)] * 2,
        compiler_params=params(),
        name="near_levels",
    )(offsets, core, *mid, *raw, *grads)


def half_kernel(levels, per, dim, turn, offs_ref, core_ref, base, x, y, d, *refs):
    dq, dk, dv = refs[-3:]
    tok = dq.shape[0]
    n2, n3 = tok // 4, tok // 8
    first = per * (1 - core_ref[0] if turn else core_ref[0])
    each = range(per)
    place = [place_matrix(offs_ref, first + h, 2, levels, tok) for h in each]
    mine = y[n3:] if turn else y[:n3]
    third = (x[n2:].astype(F32) + mine.astype(F32) + d[...].astype(F32)).astype(BF16)
    src = [slice(2 * h * dim, 2 * (h + 1) * dim) for h in each]
    more = [dot(place[h], stack(x[:n2, src[h]], third[:, src[h]])) for h in each]
    for h in each:
        cols = slice(h * dim, (h + 1) * dim)
        lo = 3 * h * dim
        total = base[:, lo + dim : lo + 3 * dim].astype(F32) + more[h]
        dq[:, cols] = base[:, lo : lo + dim]
        dk[:, cols] = total[:, :dim].astype(BF16)
        dv[:, cols] = total[:, dim:].astype(BF16)


def half_call(offsets, core, parts, whole, dim):
    levels, heads = offsets.shape
    tok = parts[0].shape[0]
    per = heads // 2
    turn = len(whole) > 0

    def where(i, o, c):
        return 0, (1 - c[0] if turn else c[0])

    return pl.pallas_call(
        functools.partial(half_kernel, levels, per, dim, turn),
        grid_spec=pltpu.PrefetchScalarGridSpec(
            num_scalar_prefetch=2,
            grid=(1,),
            in_specs=[pl.BlockSpec(memory_space=pltpu.VMEM)] * len(parts)
            + [pl.BlockSpec(memory_space=pl.ANY)] * len(whole),
            out_specs=[pl.BlockSpec((tok, per * dim), where)] * 3,
        ),
        out_shape=[jax.ShapeDtypeStruct((tok, heads * dim), BF16)] * 3,
        input_output_aliases={2 + len(parts) + i: i for i in range(len(whole))},
        compiler_params=params(),
        name="add_other_half" if turn else "add_own_half",
    )(offsets, core, *parts, *whole)


def per_device(queries, keys_in, values, out_grads, offsets):
    heads = offsets.shape[1]
    dim = queries.shape[2] // heads
    core = lax.rem(lax.axis_index("seq"), 2).astype(jnp.int32).reshape(1)
    q, k, v = queries[0], keys_in[0], values[0]
    sections = lax.axis_size("section")
    grads = lax.ppermute(
        out_grads[0], "section", [(i, (i - 1) % sections) for i in range(sections)]
    )
    q_oth, k_oth, v_oth = exchange(q, 1), exchange(k, 1), exchange(v, 1)
    kept = [pltpu.with_memory_space_constraint(a, pltpu.HBM) for a in (k, v)]
    both, three = pick_call(offsets, core, [kept[0], k_oth, kept[1], v_oth], dim)
    x, y, d = exchange(both, 2), exchange(three, 4), exchange(three, 6)
    raw = [q, q_oth, k, k_oth, v, v_oth]
    pre = pre_call(offsets, core, raw, dim)
    y, d, grads = lax.optimization_barrier((y, d, grads, pre[1]))[:3]
    grads = [grads, exchange(pack_call(core, grads), 1)]
    xa, xb, yab, da, db, ngrad, dqt, stats2 = far_call(
        offsets, core, pre, [v, v_oth], grads, [both, x, y, d], dim
    )
    xa, xb, da, db = exchange(xa, 2), exchange(xb, 3), exchange(da, 6), exchange(db, 7)
    y = exchange(yab, 4)
    yy = exchange(y, 1)
    mine, other = near_call(
        offsets, core, [pre[0], stats2, pre[2], ngrad, dqt], raw, grads, dim
    )
    other, xa, xb, da, db, y = lax.optimization_barrier((other, xa, xb, da, db, y))
    halves = half_call(offsets, core, [mine, xa, y, da], [], dim)
    dq, dk, dv = half_call(offsets, core, [exchange(other, 1), xb, yy, db], halves, dim)
    return dq[None], dk[None], dv[None]


def solution(mesh):
    spec = P("section", "seq", None)
    return jax.shard_map(
        per_device,
        mesh=mesh,
        in_specs=(spec, spec, spec, spec, P()),
        out_specs=(spec, spec, spec),
        check_vma=False,
    )
```

```python
import functools

import jax
import jax.numpy as jnp
from jax import lax
from jax.experimental import pallas as pl
from jax.experimental.pallas import tpu as pltpu
from jax.sharding import PartitionSpec as P

F32 = jnp.float32
BF16 = jnp.bfloat16
NEG = -1e30
VMEM_LIMIT = 32 * 1024 * 1024


def params():
    return pltpu.CompilerParams(vmem_limit_bytes=VMEM_LIMIT)


def exchange(value, bits):
    count = lax.axis_size("seq")
    return lax.ppermute(value, "seq", [(i, i ^ bits) for i in range(count)])


def dot(a, b):
    return jnp.dot(a, b, preferred_element_type=F32)


def dot_nt(a, b):
    return lax.dot_general(a, b, (((1,), (1,)), ((), ())), preferred_element_type=F32)


def pick_matrix(offs_ref, head, first, levels, tok):
    parts = []
    for level in range(first, levels + 1):
        rate = 2**level
        rows = tok // rate
        kept = lax.rem(offs_ref[level - 1, head], rate)
        row = lax.broadcasted_iota(jnp.int32, (rows, tok), 0)
        col = lax.broadcasted_iota(jnp.int32, (rows, tok), 1)
        parts.append((col == row * rate + kept).astype(F32))
    return jnp.concatenate(parts, axis=0).astype(BF16)


def place_matrix(offs_ref, head, first, levels, tok):
    parts = []
    for level in range(first, levels + 1):
        rate = 2**level
        rows = tok // rate
        kept = lax.rem(offs_ref[level - 1, head], rate)
        row = lax.broadcasted_iota(jnp.int32, (tok, rows), 0)
        col = lax.broadcasted_iota(jnp.int32, (tok, rows), 1)
        parts.append((row == col * rate + kept).astype(F32))
    return jnp.concatenate(parts, axis=1).astype(BF16)


def pack_kernel(core_ref, rows, out):
    out[...] = rows[...]


def pack_call(core, rows):
    tok, width = rows.shape
    half = width // 2
    return pl.pallas_call(
        pack_kernel,
        grid_spec=pltpu.PrefetchScalarGridSpec(
            num_scalar_prefetch=1,
            grid=(1,),
            in_specs=[pl.BlockSpec((tok, half), lambda i, c: (0, 1 - c[0]))],
            out_specs=pl.BlockSpec((tok, half), lambda i, c: (0, 0)),
        ),
        out_shape=jax.ShapeDtypeStruct((tok, half), BF16),
        compiler_params=params(),
        name="pack_half",
    )(core, rows)


def pick_kernel(
    levels, per, dim, core_ref, offs, k0, v0, k1, v1, both_ref, three_ref, offs_ref, own_k, own_v, sems
):
    tok = k1.shape[0]
    n2, n3 = tok // 4, tok // 8
    each = range(per)
    mine = pl.ds(pl.multiple_of(core_ref[0] * per * dim, per * dim), per * dim)
    copies = [
        pltpu.make_async_copy(src.at[:, mine], dst, sems.at[i])
        for i, (src, dst) in enumerate(((k0, own_k), (v0, own_v)))
    ]
    table = pltpu.make_async_copy(offs, offs_ref, sems.at[2])
    table.start()
    for copy in copies:
        copy.start()
    table.wait()
    picks = [pick_matrix(offs_ref, core_ref[0] * per + h, 2, levels, tok) for h in each]

    def work(keys, values, lo):
        for h in each:
            cols = slice(h * dim, (h + 1) * dim)
            out = slice(2 * h * dim, 2 * (h + 1) * dim)
            got = dot(picks[h], side(keys[:, cols], values[:, cols])).astype(BF16)
            both_ref[lo * n2 : (lo + 1) * n2, out] = got[:n2]
            both_ref[2 * n2 + lo * n3 : 2 * n2 + (lo + 1) * n3, out] = got[n2:]
            three_ref[lo * n3 : (lo + 1) * n3, out] = got[n2:]

    work(k1, v1, 1)
    for copy in copies:
        copy.wait()
    work(own_k, own_v, 0)


def pick_call(offsets, core, own, other, dim):
    tok, width = own[0].shape
    levels, heads = offsets.shape
    per = heads // 2
    spec = pl.BlockSpec((tok, per * dim), lambda i, c: (0, c[0]))

    def out(rows):
        return pl.BlockSpec((rows, 2 * per * dim), lambda i, c: (0, 0))

    rows = [tok // 2 + tok // 4, tok // 4]
    return pl.pallas_call(
        functools.partial(pick_kernel, levels, per, dim),
        grid_spec=pltpu.PrefetchScalarGridSpec(
            num_scalar_prefetch=1,
            grid=(1,),
            in_specs=[pl.BlockSpec(memory_space=pl.ANY)] * 3 + [spec] * 2,
            out_specs=[out(r) for r in rows],
            scratch_shapes=[pltpu.SMEM((levels, heads), jnp.int32)]
            + [pltpu.VMEM((tok, per * dim), BF16)] * 2
            + [pltpu.SemaphoreType.DMA((3,))],
        ),
        out_shape=[jax.ShapeDtypeStruct((r, width), BF16) for r in rows],
        compiler_params=params(),
        name="pick_rows",
    )(core, offsets, *own, *other)


def own_spec(tok, cols, steps):
    return pl.BlockSpec((tok, cols), lambda i, o, c: (0, c[0] * steps + i))


def side(*values):
    return jnp.concatenate(values, axis=1)


def stack(*values):
    return jnp.concatenate(values, axis=0)


def split(value, terms):
    parts = []
    for _ in range(terms):
        part = value.astype(BF16)
        parts.append(part)
        value = value - part.astype(F32)
    return parts


def local_scores(pick, levels, offs_ref, head, key0, key1, ones, que0, que1):
    tok, dim = key0.shape
    pos = lax.broadcasted_iota(jnp.int32, (1, 2 * tok), 1)
    bias = jnp.where(lax.rem(pos, 2) == lax.rem(offs_ref[0, head], 2), 0.0, NEG).astype(F32)
    s0 = side(dot_nt(key0, que0), dot_nt(key1, que1)) * dim**-0.5
    s1 = dot_nt(ones, stack(que0, que1)) * dim**-0.5 + bias
    return stack(s0, s1)


def pre_kernel(
    levels, per, dim, offs_ref, core_ref, q0, q1, k0, k1, v0, v1, exps, stats, near, selq
):
    tok = q0.shape[0]
    n1 = tok // 2
    heads = per * pl.num_programs(0)
    for h in range(per):
        head = core_ref[0] * heads + pl.program_id(0) * per + h
        pick = pick_matrix(offs_ref, head, 1, levels, tok)
        cols = slice(h * dim, (h + 1) * dim)
        wide = slice(2 * h * dim, 2 * (h + 1) * dim)
        lanes = slice(2 * h * tok, 2 * (h + 1) * tok)
        own = dot(pick[:n1], side(k0[:, cols], v0[:, cols])).astype(BF16)
        oth = dot(pick[:n1], side(k1[:, cols], v1[:, cols])).astype(BF16)
        ones = stack(own, oth)
        near[:, wide] = ones
        que0, que1 = q0[:, cols], q1[:, cols]
        far_pick = pick[n1:]
        selq[:, cols] = stack(dot(far_pick, que0), dot(far_pick, que1)).astype(BF16)
        s = local_scores(
            pick, levels, offs_ref, head, k0[:, cols], k1[:, cols], ones[:, :dim], que0, que1
        )
        top = jnp.max(s, axis=0, keepdims=True)
        e = jnp.exp(s - top)
        exps[:, lanes] = e.astype(BF16)
        stats[0:1, lanes] = top
        stats[1:2, lanes] = jnp.sum(e, axis=0, keepdims=True)


def pre_call(offsets, core, raw, dim):
    tok, width = raw[0].shape
    levels, heads = offsets.shape
    half = heads // 2
    per = 8
    steps = half // per
    raw_spec = own_spec(tok, per * dim, steps)
    sel = 2 * (tok // 4 + tok // 8)

    def out(rows, lanes, kind=BF16):
        return (
            pl.BlockSpec((rows, per * lanes), lambda i, o, c: (0, i)),
            jax.ShapeDtypeStruct((rows, half * lanes), kind),
        )

    outs = [out(2 * tok, 2 * tok), out(8, 2 * tok, F32), out(tok, 2 * dim), out(sel, dim)]
    return pl.pallas_call(
        functools.partial(pre_kernel, levels, per, dim),
        grid_spec=pltpu.PrefetchScalarGridSpec(
            num_scalar_prefetch=2,
            grid=(steps,),
            in_specs=[raw_spec] * 6,
            out_specs=[o[0] for o in outs],
        ),
        out_shape=[o[1] for o in outs],
        compiler_params=params(),
        name="local_scores",
    )(offsets, core, *raw)


def grad_kernel(levels, per, dim, offs_ref, core_ref, exps, near, v0, v1, g0, g1, selg, local):
    tok = g0.shape[0]
    first = core_ref[0] * per
    each = range(per)
    cols = [slice(h * dim, (h + 1) * dim) for h in each]
    lanes = [slice(2 * h * tok, 2 * (h + 1) * tok) for h in each]
    picks = [pick_matrix(offs_ref, first + h, 2, levels, tok) for h in each]
    for h in each:
        rows = stack(dot(picks[h], g0[:, cols[h]]), dot(picks[h], g1[:, cols[h]]))
        selg[:, cols[h]] = rows.astype(BF16)
    for h in each:
        vc = slice((2 * h + 1) * dim, (2 * h + 2) * dim)
        gra0, gra1 = g0[:, cols[h]], g1[:, cols[h]]
        p0 = side(dot_nt(v0[:, cols[h]], gra0), dot_nt(v1[:, cols[h]], gra1))
        p1 = dot_nt(near[:, vc], stack(gra0, gra1))
        ex = exps[:, lanes[h]]
        both = ex[:tok].astype(F32) * p0 + ex[tok:].astype(F32) * p1
        local[0:1, lanes[h]] = jnp.sum(both, axis=0, keepdims=True)


def grad_call(offsets, core, mid, raw, grads, dim):
    tok, width = raw[0].shape
    levels, heads = offsets.shape
    per = heads // 2
    raw_spec = own_spec(tok, per * dim, 1)
    sel = 2 * (tok // 4 + tok // 8)

    def whole(a):
        return pl.BlockSpec(a.shape, lambda i, o, c: (0, 0))

    outs = [
        jax.ShapeDtypeStruct((sel, per * dim), BF16),
        jax.ShapeDtypeStruct((8, per * 2 * tok), F32),
    ]
    return pl.pallas_call(
        functools.partial(grad_kernel, levels, per, dim),
        grid_spec=pltpu.PrefetchScalarGridSpec(
            num_scalar_prefetch=2,
            grid=(1,),
            in_specs=[whole(a) for a in mid] + [raw_spec] * 3 + [whole(grads[1])],
            out_specs=[whole(a) for a in outs],
        ),
        out_shape=outs,
        compiler_params=params(),
        name="local_delta",
    )(offsets, core, *mid, *raw, *grads)


def far_kernel(
    levels, per, dim, offs_ref, core_ref, stats, selq, selg, local, own, x, y, d,
    xa, xb, yab, da, db, ngrad, dqt, stats2,
):
    tok = dqt.shape[0]
    n1, n2, n3 = tok // 2, tok // 4, tok // 8
    sel = n2 + n3
    scale = dim**-0.5
    heads = per * pl.num_programs(0)
    lane = lax.broadcasted_iota(jnp.int32, (1, 2 * sel), 1)
    is2 = lax.rem(lane, sel) < n2
    pos = lax.broadcasted_iota(jnp.int32, (1, 2 * tok), 1)
    first = core_ref[0] * heads + pl.program_id(0) * per
    each = range(per)
    cols = [slice(h * dim, (h + 1) * dim) for h in each]
    kc = [slice(2 * h * dim, (2 * h + 1) * dim) for h in each]
    vc = [slice((2 * h + 1) * dim, (2 * h + 2) * dim) for h in each]
    wide = [slice(2 * h * dim, 2 * (h + 1) * dim) for h in each]
    lanes = [slice(2 * h * tok, 2 * (h + 1) * tok) for h in each]

    def rows(c):
        lo = 2 * n2
        parts = own[:lo, c], x[:lo, c], own[lo:, c], x[lo:, c], y[:, c], d[:, c]
        return stack(*parts)

    def level_pick(value):
        return jnp.where(is2, value[:tok], value[tok:])

    picks = [pick_matrix(offs_ref, first + h, 2, levels, tok) for h in each]
    keys = [rows(kc[h]) for h in each]
    s = [level_pick(dot_nt(keys[h], selq[:, cols[h]])) * scale for h in each]
    p = [level_pick(dot_nt(rows(vc[h]), selg[:, cols[h]])) for h in each]
    top = [jnp.max(a, axis=0, keepdims=True) for a in s]
    e = [jnp.exp(a - b) for a, b in zip(s, top)]
    size = [jnp.sum(a, axis=0, keepdims=True) for a in e]
    dhat = [jnp.sum(a * b, axis=0, keepdims=True) for a, b in zip(e, p)]
    none = jnp.zeros_like(picks[0])
    spots = [stack(side(a, none), side(none, a)) for a in picks]
    spread = []
    for h in each:
        terms = stack(*split(top[h], 3), *split(size[h], 2), *split(dhat[h], 2))
        zero = jnp.zeros_like(terms)
        apart = stack(jnp.where(is2, terms, zero), jnp.where(is2, zero, terms))
        spread.append(dot(apart, spots[h]))
    back = []
    for h in each:

        def level_stats(level, lo):
            rate = 2**level
            on = lax.rem(pos, rate) == lax.rem(offs_ref[level - 1, first + h], rate)
            t = [spread[h][lo + i : lo + i + 1] for i in range(7)]
            return jnp.where(on, t[0] + t[1] + t[2], NEG), t[3] + t[4], t[5] + t[6]

        t1, z1 = stats[0:1, lanes[h]], stats[1:2, lanes[h]]
        t2, z2, dot2 = level_stats(2, 0)
        t3, z3, dot3 = level_stats(3, 7)
        high = jnp.maximum(t1, jnp.maximum(t2, t3))
        a1, a2, a3 = jnp.exp(t1 - high), jnp.exp(t2 - high), jnp.exp(t3 - high)
        inv = 1.0 / (a1 * z1 + a2 * z2 + a3 * z3)
        f1, f2, f3 = a1 * inv, a2 * inv, a3 * inv
        delta = f1 * local[0:1, lanes[h]] + f2 * dot2 + f3 * dot3
        stats2[0:1, lanes[h]] = f1
        stats2[1:2, lanes[h]] = delta
        terms = stack(*split(f2, 2), *split(f3, 2), *split(delta, 2))
        back.append(dot_nt(terms, spots[h]))

    def apart(value):
        zero = jnp.zeros_like(value)
        return stack(jnp.where(is2, value, zero), jnp.where(is2, zero, value)).astype(BF16)

    dsm, wm = [], []
    for h in each:
        b = back[h]
        w = e[h] * jnp.where(is2, b[0:1] + b[1:2], b[2:3] + b[3:4])
        dsm.append(apart(w * (p[h] - (b[4:5] + b[5:6]))))
        wm.append(apart(w))
    dk = [dot(dsm[h], selq[:, cols[h]]) * scale for h in each]
    dv = [dot(wm[h], selg[:, cols[h]]) for h in each]
    for h in each:
        dkv = side(dk[h], dv[h]).astype(BF16)
        xa[:n2, wide[h]] = dkv[2 * n2 : 3 * n2]
        xb[:n2, wide[h]] = dkv[3 * n2 : 4 * n2]
        third = [dkv[tok + i * n3 : tok + (i + 1) * n3] for i in range(8)]
        xa[n2:, wide[h]] = third[2]
        xb[n2:, wide[h]] = third[3]
        yab[:, wide[h]] = stack(third[4], third[5])
        da[:, wide[h]] = third[6]
        db[:, wide[h]] = third[7]
        ngrad[:, wide[h]] = stack(dkv[:n2], third[0], dkv[n2 : 2 * n2], third[1])
        dqt[:, h * dim : h * dim + 2 * sel] = dot(keys[h].T, dsm[h]).astype(BF16)


def far_call(offsets, core, mid, far, tok, dim):
    levels, heads = offsets.shape
    half = heads // 2
    per = 8
    steps = half // per
    n2, n3 = tok // 4, tok // 8

    def mid_spec(a):
        return pl.BlockSpec((a.shape[0], a.shape[1] // steps), lambda i, o, c: (0, i))

    def out(rows, lanes, kind=BF16):
        return (
            pl.BlockSpec((rows, per * lanes), lambda i, o, c: (0, i)),
            jax.ShapeDtypeStruct((rows, half * lanes), kind),
        )

    outs = [out(n2 + n3, 2 * dim)] * 2 + [out(2 * n3, 2 * dim)] + [out(n3, 2 * dim)] * 2
    outs += [out(2 * (n2 + n3), 2 * dim), out(dim, dim), out(8, 2 * tok, F32)]
    return pl.pallas_call(
        functools.partial(far_kernel, levels, per, dim),
        grid_spec=pltpu.PrefetchScalarGridSpec(
            num_scalar_prefetch=2,
            grid=(steps,),
            in_specs=[mid_spec(a) for a in mid + far],
            out_specs=[o[0] for o in outs],
        ),
        out_shape=[o[1] for o in outs],
        compiler_params=params(),
        name="far_levels",
    )(offsets, core, *mid, *far)


def near_kernel(
    levels, per, dim, offs_ref, core_ref, exps, stats2, near, ngrad, dqt,
    q0, q1, k0, k1, v0, v1, g0, g1, mine, other,
):
    tok = q0.shape[0]
    n1 = tok // 2
    sel = tok // 4 + tok // 8
    scale = dim**-0.5
    heads = per * pl.num_programs(0)
    for h in range(per):
        head = core_ref[0] * heads + pl.program_id(0) * per + h
        pick = pick_matrix(offs_ref, head, 2, levels, tok)
        place = place_matrix(offs_ref, head, 1, levels, tok)
        cols = slice(h * dim, (h + 1) * dim)
        kc = slice(2 * h * dim, (2 * h + 1) * dim)
        vc = slice((2 * h + 1) * dim, (2 * h + 2) * dim)
        wide = slice(2 * h * dim, 2 * (h + 1) * dim)
        lanes = slice(2 * h * tok, 2 * (h + 1) * tok)
        que0, que1, gra0, gra1 = q0[:, cols], q1[:, cols], g0[:, cols], g1[:, cols]
        que, gra = stack(que0, que1), stack(gra0, gra1)
        p0 = side(dot_nt(v0[:, cols], gra0), dot_nt(v1[:, cols], gra1))
        p = stack(p0, dot_nt(near[:tok, vc], gra))
        w = exps[:, lanes].astype(F32) * stats2[0:1, lanes]
        wb = w.astype(BF16)
        ds = (w * (p - stats2[1:2, lanes])).astype(BF16)
        dkv1 = side(dot(ds[tok:], que) * scale, dot(wb[tok:], gra)).astype(BF16)
        ds0, ds1 = ds[:tok, :tok], ds[:tok, tok:]
        kv0 = side(dot(ds0, que0) * scale, dot(wb[:tok, :tok], gra0))
        kv1 = side(dot(ds1, que1) * scale, dot(wb[:tok, tok:], gra1))
        kv0 += dot(place, stack(dkv1[:n1], ngrad[:sel, wide]))
        kv1 += dot(place, stack(dkv1[n1:], ngrad[sel:, wide]))
        dqa = dot(near[:tok, kc].T, ds[tok:])
        dq0 = dqa[:, :tok] + dot(k0[:, cols].T, ds0)
        dq1 = dqa[:, tok:] + dot(k1[:, cols].T, ds1)
        dq0 += dot(dqt[:, h * dim : h * dim + sel], pick)
        dq1 += dot(dqt[:, h * dim + sel : h * dim + 2 * sel], pick)
        for ref, dq, kv in ((mine, dq0, kv0), (other, dq1, kv1)):
            lo = 3 * h * dim
            ref[:, lo : lo + dim] = (dq * scale).T.astype(BF16)
            ref[:, lo + dim : lo + 3 * dim] = kv.astype(BF16)


def near_call(offsets, core, mid, raw, grads, dim):
    tok, width = raw[0].shape
    levels, heads = offsets.shape
    half = heads // 2
    per = 8
    steps = half // per
    raw_spec = own_spec(tok, per * dim, steps)

    def mid_spec(a):
        return pl.BlockSpec((a.shape[0], a.shape[1] // steps), lambda i, o, c: (0, i))

    out_spec = pl.BlockSpec((tok, 3 * per * dim), lambda i, o, c: (0, i))
    return pl.pallas_call(
        functools.partial(near_kernel, levels, per, dim),
        grid_spec=pltpu.PrefetchScalarGridSpec(
            num_scalar_prefetch=2,
            grid=(steps,),
            in_specs=[mid_spec(a) for a in mid] + [raw_spec] * 7 + [mid_spec(grads[1])],
            out_specs=[out_spec] * 2,
        ),
        out_shape=[jax.ShapeDtypeStruct((tok, 3 * half * dim), BF16)] * 2,
        compiler_params=params(),
        name="near_levels",
    )(offsets, core, *mid, *raw, *grads)


def half_kernel(levels, per, dim, turn, offs_ref, core_ref, base, x, y, d, *refs):
    outs, (held, sems) = refs[-5:-2], refs[-2:]
    tok = base.shape[0]
    n2, n3 = tok // 4, tok // 8
    first = per * (1 - core_ref[0] if turn else core_ref[0])
    group = 2
    each = range(per)
    place = [place_matrix(offs_ref, first + h, 2, levels, tok) for h in each]
    mine = y[n3:] if turn else y[:n3]
    third = (x[n2:].astype(F32) + mine.astype(F32) + d[...].astype(F32)).astype(BF16)
    src = [slice(2 * h * dim, 2 * (h + 1) * dim) for h in each]
    copies = []

    def send(part, lo, n):
        cols = pl.ds(pl.multiple_of(first * dim + lo * dim, dim), n * dim)
        here = held.at[part, :, pl.ds(lo * dim, n * dim)]
        copies.append(pltpu.make_async_copy(here, outs[part].at[:, cols], sems.at[len(copies)]))
        copies[-1].start()

    for h in each:
        held[0, :, h * dim : (h + 1) * dim] = base[:, 3 * h * dim : (3 * h + 1) * dim]
    send(0, 0, per)
    for lo in range(0, per, group):
        heads = range(lo, lo + group)
        more = [dot(place[h], stack(x[:n2, src[h]], third[:, src[h]])) for h in heads]
        for h, add in zip(heads, more):
            cols = slice(h * dim, (h + 1) * dim)
            at = (3 * h + 1) * dim
            total = (base[:, at : at + 2 * dim].astype(F32) + add).astype(BF16)
            held[1, :, cols] = total[:, :dim]
            held[2, :, cols] = total[:, dim:]
        send(1, lo, group)
        send(2, lo, group)
    for copy in copies:
        copy.wait()


def half_call(offsets, core, parts, whole, dim):
    levels, heads = offsets.shape
    tok = parts[0].shape[0]
    per = heads // 2
    turn = len(whole) > 0
    away = pl.BlockSpec(memory_space=pl.ANY)
    return pl.pallas_call(
        functools.partial(half_kernel, levels, per, dim, turn),
        grid_spec=pltpu.PrefetchScalarGridSpec(
            num_scalar_prefetch=2,
            grid=(1,),
            in_specs=[pl.BlockSpec(a.shape, lambda i, o, c: (0, 0)) for a in parts]
            + [away] * len(whole),
            out_specs=[away] * 3,
            scratch_shapes=[
                pltpu.VMEM((3, tok, per * dim), BF16),
                pltpu.SemaphoreType.DMA((1 + per,)),
            ],
        ),
        out_shape=[jax.ShapeDtypeStruct((tok, heads * dim), BF16)] * 3,
        input_output_aliases={2 + len(parts) + i: i for i in range(len(whole))},
        compiler_params=params(),
        name="add_other_half" if turn else "add_own_half",
    )(offsets, core, *parts, *whole)


def per_device(queries, keys_in, values, out_grads, offsets):
    heads = offsets.shape[1]
    dim = queries.shape[2] // heads
    core = lax.rem(lax.axis_index("seq"), 2).astype(jnp.int32).reshape(1)
    q, k, v = queries[0], keys_in[0], values[0]
    sections = lax.axis_size("section")
    grads = lax.ppermute(
        out_grads[0], "section", [(i, (i - 1) % sections) for i in range(sections)]
    )
    q_oth, k_oth, v_oth = exchange(q, 1), exchange(k, 1), exchange(v, 1)
    kept = [pltpu.with_memory_space_constraint(a, pltpu.HBM) for a in (k, v)]
    both, three = pick_call(
        pltpu.with_memory_space_constraint(offsets, pltpu.HBM), core, kept, [k_oth, v_oth], dim
    )
    x, y, d = exchange(both, 2), exchange(three, 4), exchange(three, 6)
    raw = [q, q_oth, k, k_oth, v, v_oth]
    pre = pre_call(offsets, core, raw, dim)
    y, d, grads = lax.optimization_barrier((y, d, grads, pre[1]))[:3]
    grads = [grads, exchange(pack_call(core, grads), 1)]
    exps, stats, near, selq = pre
    selg, local = grad_call(offsets, core, [exps, near], [v, v_oth], grads, dim)
    xa, xb, yab, da, db, ngrad, dqt, stats2 = far_call(
        offsets, core, [stats, selq, selg, local], [both, x, y, d], q.shape[0], dim
    )
    xa, xb, da, db = exchange(xa, 2), exchange(xb, 3), exchange(da, 6), exchange(db, 7)
    y = exchange(yab, 4)
    yy = exchange(y, 1)
    mine, other = near_call(
        offsets, core, [exps, stats2, near, ngrad, dqt], raw, grads, dim
    )
    other, xa, xb, da, db, y = lax.optimization_barrier((other, xa, xb, da, db, y))
    halves = half_call(offsets, core, [mine, xa, y, da], [], dim)
    dq, dk, dv = half_call(offsets, core, [exchange(other, 1), xb, yy, db], halves, dim)
    return dq[None], dk[None], dv[None]


def solution(mesh):
    spec = P("section", "seq", None)
    return jax.shard_map(
        per_device,
        mesh=mesh,
        in_specs=(spec, spec, spec, spec, P()),
        out_specs=(spec, spec, spec),
        check_vma=False,
    )
```

```python
import functools

import jax
import jax.numpy as jnp
from jax import lax
from jax.experimental import pallas as pl
from jax.experimental.pallas import tpu as pltpu
from jax.sharding import PartitionSpec as P

F32 = jnp.float32
BF16 = jnp.bfloat16
NEG = -1e30
VMEM_LIMIT = 32 * 1024 * 1024


def params():
    return pltpu.CompilerParams(vmem_limit_bytes=VMEM_LIMIT)


def exchange(value, bits):
    count = lax.axis_size("seq")
    return lax.ppermute(value, "seq", [(i, i ^ bits) for i in range(count)])


def dot(a, b):
    return jnp.dot(a, b, preferred_element_type=F32)


def dot_nt(a, b):
    return lax.dot_general(a, b, (((1,), (1,)), ((), ())), preferred_element_type=F32)


def pick_matrix(offs_ref, head, first, levels, tok):
    parts = []
    for level in range(first, levels + 1):
        rate = 2**level
        rows = tok // rate
        kept = lax.rem(offs_ref[level - 1, head], rate)
        row = lax.broadcasted_iota(jnp.int32, (rows, tok), 0)
        col = lax.broadcasted_iota(jnp.int32, (rows, tok), 1)
        parts.append((col == row * rate + kept).astype(F32))
    return jnp.concatenate(parts, axis=0).astype(BF16)


def place_matrix(offs_ref, head, first, levels, tok):
    parts = []
    for level in range(first, levels + 1):
        rate = 2**level
        rows = tok // rate
        kept = lax.rem(offs_ref[level - 1, head], rate)
        row = lax.broadcasted_iota(jnp.int32, (tok, rows), 0)
        col = lax.broadcasted_iota(jnp.int32, (tok, rows), 1)
        parts.append((row == col * rate + kept).astype(F32))
    return jnp.concatenate(parts, axis=1).astype(BF16)


def pack_kernel(core_ref, rows, *outs):
    lo = 0
    for out in outs:
        out[...] = rows[:, lo : lo + out.shape[1]]
        lo += out.shape[1]


def pack_call(core, rows, sizes):
    tok, width = rows.shape
    half = width // 2
    return pl.pallas_call(
        pack_kernel,
        grid_spec=pltpu.PrefetchScalarGridSpec(
            num_scalar_prefetch=1,
            grid=(1,),
            in_specs=[pl.BlockSpec((tok, half), lambda i, c: (0, 1 - c[0]))],
            out_specs=[pl.BlockSpec((tok, n), lambda i, c: (0, 0)) for n in sizes],
        ),
        out_shape=[jax.ShapeDtypeStruct((tok, n), BF16) for n in sizes],
        compiler_params=params(),
        name="pack_half",
    )(core, rows)


def pick_kernel(
    levels, per, dim, core_ref, offs, k0, v0, k1, v1, two_ref, three_ref, offs_ref, own_k, own_v, sems
):
    tok = k1.shape[0]
    n2, n3 = tok // 4, tok // 8
    each = range(per)
    mine = pl.ds(pl.multiple_of(core_ref[0] * per * dim, per * dim), per * dim)
    copies = [
        pltpu.make_async_copy(src.at[:, mine], dst, sems.at[i])
        for i, (src, dst) in enumerate(((k0, own_k), (v0, own_v)))
    ]
    table = pltpu.make_async_copy(offs, offs_ref, sems.at[2])
    table.start()
    for copy in copies:
        copy.start()
    table.wait()
    picks = [pick_matrix(offs_ref, core_ref[0] * per + h, 2, levels, tok) for h in each]

    def work(keys, values, lo):
        for h in each:
            cols = slice(h * dim, (h + 1) * dim)
            out = slice(2 * h * dim, 2 * (h + 1) * dim)
            got = dot(picks[h], side(keys[:, cols], values[:, cols])).astype(BF16)
            two_ref[lo * n2 : (lo + 1) * n2, out] = got[:n2]
            three_ref[lo * n3 : (lo + 1) * n3, out] = got[n2:]

    work(k1, v1, 1)
    for copy in copies:
        copy.wait()
    work(own_k, own_v, 0)


def pick_call(offsets, core, own, other, dim):
    tok, width = own[0].shape
    levels, heads = offsets.shape
    per = heads // 2
    spec = pl.BlockSpec((tok, per * dim), lambda i, c: (0, c[0]))

    def out(rows):
        return pl.BlockSpec((rows, 2 * per * dim), lambda i, c: (0, 0))

    rows = [tok // 2, tok // 4]
    return pl.pallas_call(
        functools.partial(pick_kernel, levels, per, dim),
        grid_spec=pltpu.PrefetchScalarGridSpec(
            num_scalar_prefetch=1,
            grid=(1,),
            in_specs=[pl.BlockSpec(memory_space=pl.ANY)] * 3 + [spec] * 2,
            out_specs=[out(r) for r in rows],
            scratch_shapes=[pltpu.SMEM((levels, heads), jnp.int32)]
            + [pltpu.VMEM((tok, per * dim), BF16)] * 2
            + [pltpu.SemaphoreType.DMA((3,))],
        ),
        out_shape=[jax.ShapeDtypeStruct((r, width), BF16) for r in rows],
        compiler_params=params(),
        name="pick_rows",
    )(core, offsets, *own, *other)


def own_spec(tok, cols, steps):
    return pl.BlockSpec((tok, cols), lambda i, o, c: (0, c[0] * steps + i))


def side(*values):
    return jnp.concatenate(values, axis=1)


def stack(*values):
    return jnp.concatenate(values, axis=0)


def split(value, terms):
    parts = []
    for _ in range(terms):
        part = value.astype(BF16)
        parts.append(part)
        value = value - part.astype(F32)
    return parts


def local_scores(pick, levels, offs_ref, head, key0, key1, ones, que0, que1):
    tok, dim = key0.shape
    pos = lax.broadcasted_iota(jnp.int32, (1, 2 * tok), 1)
    bias = jnp.where(lax.rem(pos, 2) == lax.rem(offs_ref[0, head], 2), 0.0, NEG).astype(F32)
    s0 = side(dot_nt(key0, que0), dot_nt(key1, que1)) * dim**-0.5
    s1 = dot_nt(ones, stack(que0, que1)) * dim**-0.5 + bias
    return stack(s0, s1)


def pre_kernel(
    levels, per, dim, offs_ref, core_ref, q0, q1, k0, k1, v0, v1, exp0, exp1, stats, near, selq
):
    tok = q0.shape[0]
    n1 = tok // 2
    heads = per * pl.num_programs(0)
    for h in range(per):
        head = core_ref[0] * heads + pl.program_id(0) * per + h
        pick = pick_matrix(offs_ref, head, 1, levels, tok)
        cols = slice(h * dim, (h + 1) * dim)
        wide = slice(2 * h * dim, 2 * (h + 1) * dim)
        lanes = slice(2 * h * tok, 2 * (h + 1) * tok)
        own = dot(pick[:n1], side(k0[:, cols], v0[:, cols])).astype(BF16)
        oth = dot(pick[:n1], side(k1[:, cols], v1[:, cols])).astype(BF16)
        ones = stack(own, oth)
        near[:, wide] = ones
        que0, que1 = q0[:, cols], q1[:, cols]
        far_pick = pick[n1:]
        selq[:, cols] = stack(dot(far_pick, que0), dot(far_pick, que1)).astype(BF16)
        s = local_scores(
            pick, levels, offs_ref, head, k0[:, cols], k1[:, cols], ones[:, :dim], que0, que1
        )
        top = jnp.max(s, axis=0, keepdims=True)
        e = jnp.exp(s - top)
        for half, ref in enumerate((exp0, exp1)):
            ref[:, h * tok : (h + 1) * tok] = e[:, half * tok : (half + 1) * tok].astype(BF16)
        stats[0:1, lanes] = top
        stats[1:2, lanes] = jnp.sum(e, axis=0, keepdims=True)


def pre_call(offsets, core, raw, dim):
    tok, width = raw[0].shape
    levels, heads = offsets.shape
    half = heads // 2
    per = 8
    steps = half // per
    raw_spec = own_spec(tok, per * dim, steps)
    sel = 2 * (tok // 4 + tok // 8)

    def out(rows, lanes, kind=BF16):
        return (
            pl.BlockSpec((rows, per * lanes), lambda i, o, c: (0, i)),
            jax.ShapeDtypeStruct((rows, half * lanes), kind),
        )

    outs = [out(2 * tok, tok), out(2 * tok, tok), out(8, 2 * tok, F32), out(tok, 2 * dim), out(sel, dim)]
    return pl.pallas_call(
        functools.partial(pre_kernel, levels, per, dim),
        grid_spec=pltpu.PrefetchScalarGridSpec(
            num_scalar_prefetch=2,
            grid=(steps,),
            in_specs=[raw_spec] * 6,
            out_specs=[o[0] for o in outs],
        ),
        out_shape=[o[1] for o in outs],
        compiler_params=params(),
        name="local_scores",
    )(offsets, core, *raw)


def local_delta(exps, values, ones, grads):
    tok = values.shape[0]
    p0, p1 = dot_nt(values, grads), dot_nt(ones, grads)
    both = exps[:tok].astype(F32) * p0 + exps[tok:].astype(F32) * p1
    return jnp.sum(both, axis=0, keepdims=True)


def grad_kernel(levels, per, dim, offs_ref, core_ref, exps, near, values, grads, selg, local):
    tok = values.shape[0]
    first = core_ref[0] * per
    each = range(per)
    cols = [slice(h * dim, (h + 1) * dim) for h in each]
    for h in each:
        pick = pick_matrix(offs_ref, first + h, 2, levels, tok)
        selg[:, cols[h]] = dot(pick, grads[:, cols[h]]).astype(BF16)
    for h in each:
        here = slice(h * tok, (h + 1) * tok)
        vc = slice((2 * h + 1) * dim, (2 * h + 2) * dim)
        local[0:1, here] = local_delta(
            exps[:, here], values[:, cols[h]], near[:, vc], grads[:, cols[h]]
        )


def grad_call(offsets, core, exps, near, values, grads, dim):
    tok, width = values.shape
    levels, heads = offsets.shape
    per = heads // 2
    raw_spec = own_spec(tok, per * dim, 1)

    def whole(a):
        return pl.BlockSpec(a.shape, lambda i, o, c: (0, 0))

    outs = [
        jax.ShapeDtypeStruct((tok // 4 + tok // 8, per * dim), BF16),
        jax.ShapeDtypeStruct((8, per * tok), F32),
    ]
    return pl.pallas_call(
        functools.partial(grad_kernel, levels, per, dim),
        grid_spec=pltpu.PrefetchScalarGridSpec(
            num_scalar_prefetch=2,
            grid=(1,),
            in_specs=[whole(exps), whole(near), raw_spec, raw_spec],
            out_specs=[whole(a) for a in outs],
        ),
        out_shape=outs,
        compiler_params=params(),
        name="own_delta",
    )(offsets, core, exps, near, values, grads)


def far_kernel(
    levels, per, dim, offs_ref, core_ref, stats, selq, selg0, local0, exp1, near, v1,
    own2, x2, own3, x3, y3, d3, *refs
):
    xa, xb, xab, yab, dab, ngrad, dqt, stats2 = refs[-8:]
    g1 = side(*(ref[...] for ref in refs[:-8]))
    tok = dqt.shape[0]
    n1, n2, n3 = tok // 2, tok // 4, tok // 8
    sel = n2 + n3
    scale = dim**-0.5
    heads = per * pl.num_programs(0)
    lane = lax.broadcasted_iota(jnp.int32, (1, 2 * sel), 1)
    is2 = lax.rem(lane, sel) < n2
    pos = lax.broadcasted_iota(jnp.int32, (1, 2 * tok), 1)
    first = core_ref[0] * heads + pl.program_id(0) * per
    each = range(per)
    cols = [slice(h * dim, (h + 1) * dim) for h in each]
    kc = [slice(2 * h * dim, (2 * h + 1) * dim) for h in each]
    vc = [slice((2 * h + 1) * dim, (2 * h + 2) * dim) for h in each]
    wide = [slice(2 * h * dim, 2 * (h + 1) * dim) for h in each]
    lanes = [slice(2 * h * tok, 2 * (h + 1) * tok) for h in each]

    def rows(c):
        return stack(*(ref[:, c] for ref in (own2, x2, own3, x3, y3, d3)))

    def level_pick(value):
        return jnp.where(is2, value[:tok], value[tok:])

    picks = [pick_matrix(offs_ref, first + h, 2, levels, tok) for h in each]
    selg = [
        stack(selg0[:, cols[h]], dot(picks[h], g1[:, cols[h]]).astype(BF16)) for h in each
    ]
    keys = [rows(kc[h]) for h in each]
    s = [level_pick(dot_nt(keys[h], selq[:, cols[h]])) * scale for h in each]
    p = [level_pick(dot_nt(rows(vc[h]), selg[h])) for h in each]
    local1 = [
        local_delta(exp1[:, h * tok : (h + 1) * tok], v1[:, cols[h]], near[:, vc[h]], g1[:, cols[h]])
        for h in each
    ]
    top = [jnp.max(a, axis=0, keepdims=True) for a in s]
    e = [jnp.exp(a - b) for a, b in zip(s, top)]
    size = [jnp.sum(a, axis=0, keepdims=True) for a in e]
    dhat = [jnp.sum(a * b, axis=0, keepdims=True) for a, b in zip(e, p)]
    none = jnp.zeros_like(picks[0])
    spots = [stack(side(a, none), side(none, a)) for a in picks]
    spread = []
    for h in each:
        terms = stack(*split(top[h], 3), *split(size[h], 2), *split(dhat[h], 2))
        zero = jnp.zeros_like(terms)
        apart = stack(jnp.where(is2, terms, zero), jnp.where(is2, zero, terms))
        spread.append(dot(apart, spots[h]))
    back = []
    for h in each:

        def level_stats(level, lo):
            rate = 2**level
            on = lax.rem(pos, rate) == lax.rem(offs_ref[level - 1, first + h], rate)
            t = [spread[h][lo + i : lo + i + 1] for i in range(7)]
            return jnp.where(on, t[0] + t[1] + t[2], NEG), t[3] + t[4], t[5] + t[6]

        t1, z1 = stats[0:1, lanes[h]], stats[1:2, lanes[h]]
        t2, z2, dot2 = level_stats(2, 0)
        t3, z3, dot3 = level_stats(3, 7)
        high = jnp.maximum(t1, jnp.maximum(t2, t3))
        a1, a2, a3 = jnp.exp(t1 - high), jnp.exp(t2 - high), jnp.exp(t3 - high)
        inv = 1.0 / (a1 * z1 + a2 * z2 + a3 * z3)
        f1, f2, f3 = a1 * inv, a2 * inv, a3 * inv
        delta = f1 * side(local0[0:1, h * tok : (h + 1) * tok], local1[h]) + f2 * dot2 + f3 * dot3
        stats2[0:1, lanes[h]] = f1
        stats2[1:2, lanes[h]] = delta
        terms = stack(*split(f2, 2), *split(f3, 2), *split(delta, 2))
        back.append(dot_nt(terms, spots[h]))

    def apart(value):
        zero = jnp.zeros_like(value)
        return stack(jnp.where(is2, value, zero), jnp.where(is2, zero, value)).astype(BF16)

    dsm, wm = [], []
    for h in each:
        b = back[h]
        w = e[h] * jnp.where(is2, b[0:1] + b[1:2], b[2:3] + b[3:4])
        dsm.append(apart(w * (p[h] - (b[4:5] + b[5:6]))))
        wm.append(apart(w))
    dk = [dot(dsm[h], selq[:, cols[h]]) * scale for h in each]
    dv = [dot(wm[h], selg[h]) for h in each]
    for h in each:
        dkv = side(dk[h], dv[h]).astype(BF16)
        xa[:, wide[h]] = dkv[2 * n2 : 3 * n2]
        xb[:, wide[h]] = dkv[3 * n2 : 4 * n2]
        third = [dkv[tok + i * n3 : tok + (i + 1) * n3] for i in range(8)]
        xab[:, wide[h]] = stack(third[2], third[3])
        yab[:, wide[h]] = stack(third[4], third[5])
        dab[:, wide[h]] = stack(third[6], third[7])
        ngrad[:, wide[h]] = stack(dkv[:n2], third[0], dkv[n2 : 2 * n2], third[1])
        dqt[:, h * dim : h * dim + 2 * sel] = dot(keys[h].T, dsm[h]).astype(BF16)


def far_call(offsets, core, mid, value, far, tok, dim):
    levels, heads = offsets.shape
    half = heads // 2
    per = 8
    steps = half // per
    n2, n3 = tok // 4, tok // 8

    def mid_spec(a):
        return pl.BlockSpec((a.shape[0], a.shape[1] // steps), lambda i, o, c: (0, i))

    def out(rows, lanes, kind=BF16):
        return (
            pl.BlockSpec((rows, per * lanes), lambda i, o, c: (0, i)),
            jax.ShapeDtypeStruct((rows, half * lanes), kind),
        )

    outs = [out(n2, 2 * dim)] * 2 + [out(2 * n3, 2 * dim)] * 3
    outs += [out(2 * (n2 + n3), 2 * dim), out(dim, dim), out(8, 2 * tok, F32)]
    return pl.pallas_call(
        functools.partial(far_kernel, levels, per, dim),
        grid_spec=pltpu.PrefetchScalarGridSpec(
            num_scalar_prefetch=2,
            grid=(steps,),
            in_specs=[mid_spec(a) for a in mid]
            + [own_spec(tok, per * dim, steps)]
            + [mid_spec(a) for a in far],
            out_specs=[o[0] for o in outs],
        ),
        out_shape=[o[1] for o in outs],
        compiler_params=params(),
        name="far_levels",
    )(offsets, core, *mid, value, *far)


def near_kernel(
    levels, per, dim, offs_ref, core_ref, exp0, exp1, stats2, near, ngrad, dqt,
    q0, q1, k0, k1, v0, v1, g0, *refs,
):
    mine, other = refs[-2:]
    g1 = side(*(ref[...] for ref in refs[:-2]))
    tok = q0.shape[0]
    n1 = tok // 2
    sel = tok // 4 + tok // 8
    scale = dim**-0.5
    heads = per * pl.num_programs(0)
    first = core_ref[0] * heads + pl.program_id(0) * per
    for lo in range(0, per, 4):
        each = range(lo, lo + 4)
        cols = {h: slice(h * dim, (h + 1) * dim) for h in each}
        vc = {h: slice((2 * h + 1) * dim, (2 * h + 2) * dim) for h in each}
        gra = {h: stack(g0[:, cols[h]], g1[:, cols[h]]) for h in each}
        que = {h: stack(q0[:, cols[h]], q1[:, cols[h]]) for h in each}
        wb, ds = {}, {}
        for h in each:
            lanes = slice(2 * h * tok, 2 * (h + 1) * tok)
            here = slice(h * tok, (h + 1) * tok)
            p0 = dot_nt(v0[:, cols[h]], gra[h][:tok])
            p1 = dot_nt(v1[:, cols[h]], gra[h][tok:])
            p = stack(side(p0, p1), dot_nt(near[:tok, vc[h]], gra[h]))
            w = side(exp0[:, here], exp1[:, here]).astype(F32) * stats2[0:1, lanes]
            wb[h] = w.astype(BF16)
            ds[h] = (w * (p - stats2[1:2, lanes])).astype(BF16)
        dkv1 = {
            h: side(dot(ds[h][tok:], que[h]) * scale, dot(wb[h][tok:], gra[h])).astype(BF16)
            for h in each
        }
        for ref, block, keys in ((mine, 0, k0), (other, 1, k1)):
            at = slice(block * tok, (block + 1) * tok)
            picked = slice(block * n1, (block + 1) * n1)
            grads = slice(block * sel, (block + 1) * sel)
            kv, dq = {}, {}
            for h in each:
                place = place_matrix(offs_ref, first + h, 1, levels, tok)
                wide = slice(2 * h * dim, 2 * (h + 1) * dim)
                d0, w0 = ds[h][:tok, at], wb[h][:tok, at]
                kv[h] = side(dot(d0, que[h][at]) * scale, dot(w0, gra[h][at]))
                kv[h] += dot(place, stack(dkv1[h][picked], ngrad[grads, wide]))
            for h in each:
                pick = pick_matrix(offs_ref, first + h, 2, levels, tok)
                kc = slice(2 * h * dim, (2 * h + 1) * dim)
                far = dqt[:, h * dim + block * sel : h * dim + (block + 1) * sel]
                both = stack(keys[:, cols[h]], near[:tok, kc])
                dq[h] = dot(both.T, ds[h][:, at]) + dot(far, pick)
            for h in each:
                to = 3 * h * dim
                ref[:, to : to + dim] = (dq[h] * scale).T.astype(BF16)
                ref[:, to + dim : to + 3 * dim] = kv[h].astype(BF16)


def near_call(offsets, core, mid, raw, grads, dim):
    tok, width = raw[0].shape
    levels, heads = offsets.shape
    half = heads // 2
    per = 8
    steps = half // per
    raw_spec = own_spec(tok, per * dim, steps)

    def mid_spec(a):
        return pl.BlockSpec((a.shape[0], a.shape[1] // steps), lambda i, o, c: (0, i))

    out_spec = pl.BlockSpec((tok, 3 * per * dim), lambda i, o, c: (0, i))
    return pl.pallas_call(
        functools.partial(near_kernel, levels, per, dim),
        grid_spec=pltpu.PrefetchScalarGridSpec(
            num_scalar_prefetch=2,
            grid=(steps,),
            in_specs=[mid_spec(a) for a in mid] + [raw_spec] * 7
            + [mid_spec(a) for a in grads[1:]],
            out_specs=[out_spec] * 2,
        ),
        out_shape=[jax.ShapeDtypeStruct((tok, 3 * half * dim), BF16)] * 2,
        compiler_params=params(),
        name="near_levels",
    )(offsets, core, *mid, *raw, *grads)


def sum_kernel(here, there, first, second):
    total = (here[...].astype(F32) + there[...].astype(F32)).astype(BF16)
    rows = first.shape[0]
    first[...] = total[:rows]
    second[...] = total[rows:]


def sum_call(here, there):
    rows, cols = here.shape
    return pl.pallas_call(
        sum_kernel,
        out_shape=[jax.ShapeDtypeStruct((rows // 2, cols), BF16)] * 2,
        compiler_params=params(),
        name="add_diagonal",
    )(here, there)


def half_kernel(levels, per, dim, turn, offs_ref, core_ref, base, x, y, x3, *refs):
    outs, (held, sems) = refs[-5:-2], refs[-2:]
    tok = base.shape[0]
    n2, n3 = tok // 4, tok // 8
    first = per * (1 - core_ref[0] if turn else core_ref[0])
    group = 2
    each = range(per)
    place = [place_matrix(offs_ref, first + h, 2, levels, tok) for h in each]
    mine = y[n3:] if turn else y[:n3]
    third = (x3[...].astype(F32) + mine.astype(F32)).astype(BF16)
    src = [slice(2 * h * dim, 2 * (h + 1) * dim) for h in each]
    copies = []

    def send(part, lo, n):
        cols = pl.ds(pl.multiple_of(first * dim + lo * dim, dim), n * dim)
        here = held.at[part, :, pl.ds(lo * dim, n * dim)]
        copies.append(pltpu.make_async_copy(here, outs[part].at[:, cols], sems.at[len(copies)]))
        copies[-1].start()

    for h in each:
        held[0, :, h * dim : (h + 1) * dim] = base[:, 3 * h * dim : (3 * h + 1) * dim]
    send(0, 0, per)
    for lo in range(0, per, group):
        heads = range(lo, lo + group)
        more = [dot(place[h], stack(x[:, src[h]], third[:, src[h]])) for h in heads]
        for h, add in zip(heads, more):
            cols = slice(h * dim, (h + 1) * dim)
            at = (3 * h + 1) * dim
            total = (base[:, at : at + 2 * dim].astype(F32) + add).astype(BF16)
            held[1, :, cols] = total[:, :dim]
            held[2, :, cols] = total[:, dim:]
        send(1, lo, group)
        send(2, lo, group)
    for copy in copies:
        copy.wait()


def half_call(offsets, core, parts, whole, dim):
    levels, heads = offsets.shape
    tok = parts[0].shape[0]
    per = heads // 2
    turn = len(whole) > 0
    away = pl.BlockSpec(memory_space=pl.ANY)
    return pl.pallas_call(
        functools.partial(half_kernel, levels, per, dim, turn),
        grid_spec=pltpu.PrefetchScalarGridSpec(
            num_scalar_prefetch=2,
            grid=(1,),
            in_specs=[pl.BlockSpec(a.shape, lambda i, o, c: (0, 0)) for a in parts]
            + [away] * len(whole),
            out_specs=[away] * 3,
            scratch_shapes=[
                pltpu.VMEM((3, tok, per * dim), BF16),
                pltpu.SemaphoreType.DMA((1 + per,)),
            ],
        ),
        out_shape=[jax.ShapeDtypeStruct((tok, heads * dim), BF16)] * 3,
        input_output_aliases={2 + len(parts) + i: i for i in range(len(whole))},
        compiler_params=params(),
        name="add_other_half" if turn else "add_own_half",
    )(offsets, core, *parts, *whole)


def per_device(queries, keys_in, values, out_grads, offsets):
    heads = offsets.shape[1]
    dim = queries.shape[2] // heads
    core = lax.rem(lax.axis_index("seq"), 2).astype(jnp.int32).reshape(1)
    q, k, v = queries[0], keys_in[0], values[0]
    sections = lax.axis_size("section")
    grads = lax.ppermute(
        out_grads[0], "section", [(i, (i - 1) % sections) for i in range(sections)]
    )
    q_oth, k_oth, v_oth = exchange(q, 1), exchange(k, 1), exchange(v, 1)
    kept = [pltpu.with_memory_space_constraint(a, pltpu.HBM) for a in (k, v)]
    two, three = pick_call(
        pltpu.with_memory_space_constraint(offsets, pltpu.HBM), core, kept, [k_oth, v_oth], dim
    )
    x3, y3, x2 = exchange(three, 2), exchange(three, 4), exchange(two, 2)
    x3, y3 = lax.optimization_barrier((x3, y3))
    d3 = exchange(x3, 4)
    raw = [q, q_oth, k, k_oth, v, v_oth]
    pre = pre_call(offsets, core, raw, dim)
    exp0, exp1, stats, near, selq = pre
    grads = lax.optimization_barrier((grads, stats))[0]
    sel = grad_call(offsets, core, exp0, near, v, grads, dim)
    half = heads // 2
    cuts = [half * i // 3 for i in range(4)]
    sizes = [(hi - lo) * dim for lo, hi in zip(cuts, cuts[1:])]
    other = [exchange(piece, 1) for piece in pack_call(core, grads, sizes)]
    other = lax.optimization_barrier((*other, sel[1]))[:-1]
    xa, xb, xab, yab, dab, ngrad, dqt, stats2 = far_call(
        offsets, core, [stats, selq, *sel, exp1, near], v_oth,
        [two, x2, three, x3, y3, d3, *other], q.shape[0], dim,
    )
    thirds = sum_call(xab, exchange(dab, 4))
    xa, xb, y = exchange(xa, 2), exchange(xb, 3), exchange(yab, 4)
    xa3, xb3 = exchange(thirds[0], 2), exchange(thirds[1], 3)
    yy = exchange(y, 1)
    mine, other = near_call(
        offsets, core, [exp0, exp1, stats2, near, ngrad, dqt], raw, [grads, *other], dim
    )
    other, xa, xb, xa3, xb3, y = lax.optimization_barrier((other, xa, xb, xa3, xb3, y))
    halves = half_call(offsets, core, [mine, xa, y, xa3], [], dim)
    dq, dk, dv = half_call(offsets, core, [exchange(other, 1), xb, yy, xb3], halves, dim)
    return dq[None], dk[None], dv[None]


def solution(mesh):
    spec = P("section", "seq", None)
    return jax.shard_map(
        per_device,
        mesh=mesh,
        in_specs=(spec, spec, spec, spec, P()),
        out_specs=(spec, spec, spec),
        check_vma=False,
    )
```

```python
import functools

import jax
import jax.numpy as jnp
from jax import lax
from jax.experimental import pallas as pl
from jax.experimental.pallas import tpu as pltpu
from jax.sharding import PartitionSpec as P

F32 = jnp.float32
BF16 = jnp.bfloat16
NEG = -1e30
VMEM_LIMIT = 32 * 1024 * 1024


def params():
    return pltpu.CompilerParams(vmem_limit_bytes=VMEM_LIMIT)


def exchange(value, bits):
    count = lax.axis_size("seq")
    return lax.ppermute(value, "seq", [(i, i ^ bits) for i in range(count)])


def dot(a, b):
    return jnp.dot(a, b, preferred_element_type=F32)


def dot_nt(a, b):
    return lax.dot_general(a, b, (((1,), (1,)), ((), ())), preferred_element_type=F32)


def pick_matrix(offs_ref, head, first, levels, tok):
    parts = []
    for level in range(first, levels + 1):
        rate = 2**level
        rows = tok // rate
        kept = lax.rem(offs_ref[level - 1, head], rate)
        row = lax.broadcasted_iota(jnp.int32, (rows, tok), 0)
        col = lax.broadcasted_iota(jnp.int32, (rows, tok), 1)
        parts.append((col == row * rate + kept).astype(F32))
    return jnp.concatenate(parts, axis=0).astype(BF16)


def place_matrix(offs_ref, head, first, levels, tok):
    parts = []
    for level in range(first, levels + 1):
        rate = 2**level
        rows = tok // rate
        kept = lax.rem(offs_ref[level - 1, head], rate)
        row = lax.broadcasted_iota(jnp.int32, (tok, rows), 0)
        col = lax.broadcasted_iota(jnp.int32, (tok, rows), 1)
        parts.append((row == col * rate + kept).astype(F32))
    return jnp.concatenate(parts, axis=1).astype(BF16)


def pack_kernel(core_ref, rows, *outs):
    lo = 0
    for out in outs:
        out[...] = rows[:, lo : lo + out.shape[1]]
        lo += out.shape[1]


def pack_call(core, rows, sizes):
    tok, width = rows.shape
    half = width // 2
    return pl.pallas_call(
        pack_kernel,
        grid_spec=pltpu.PrefetchScalarGridSpec(
            num_scalar_prefetch=1,
            grid=(1,),
            in_specs=[pl.BlockSpec((tok, half), lambda i, c: (0, 1 - c[0]))],
            out_specs=[pl.BlockSpec((tok, n), lambda i, c: (0, 0)) for n in sizes],
        ),
        out_shape=[jax.ShapeDtypeStruct((tok, n), BF16) for n in sizes],
        compiler_params=params(),
        name="pack_half",
    )(core, rows)


def pick_kernel(
    levels, per, dim, core_ref, offs, k0, v0, k1, v1, two_ref, three_ref, offs_ref, own_k, own_v, sems
):
    tok = k1.shape[0]
    n2, n3 = tok // 4, tok // 8
    each = range(per)
    mine = pl.ds(pl.multiple_of(core_ref[0] * per * dim, per * dim), per * dim)
    copies = [
        pltpu.make_async_copy(src.at[:, mine], dst, sems.at[i])
        for i, (src, dst) in enumerate(((k0, own_k), (v0, own_v)))
    ]
    table = pltpu.make_async_copy(offs, offs_ref, sems.at[2])
    table.start()
    for copy in copies:
        copy.start()
    table.wait()
    picks = [pick_matrix(offs_ref, core_ref[0] * per + h, 2, levels, tok) for h in each]

    def work(keys, values, lo):
        for h in each:
            cols = slice(h * dim, (h + 1) * dim)
            out = slice(2 * h * dim, 2 * (h + 1) * dim)
            got = dot(picks[h], side(keys[:, cols], values[:, cols])).astype(BF16)
            two_ref[lo * n2 : (lo + 1) * n2, out] = got[:n2]
            three_ref[lo * n3 : (lo + 1) * n3, out] = got[n2:]

    work(k1, v1, 1)
    for copy in copies:
        copy.wait()
    work(own_k, own_v, 0)


def pick_call(offsets, core, own, other, dim):
    tok, width = own[0].shape
    levels, heads = offsets.shape
    per = heads // 2
    spec = pl.BlockSpec((tok, per * dim), lambda i, c: (0, c[0]))

    def out(rows):
        return pl.BlockSpec((rows, 2 * per * dim), lambda i, c: (0, 0))

    rows = [tok // 2, tok // 4]
    return pl.pallas_call(
        functools.partial(pick_kernel, levels, per, dim),
        grid_spec=pltpu.PrefetchScalarGridSpec(
            num_scalar_prefetch=1,
            grid=(1,),
            in_specs=[pl.BlockSpec(memory_space=pl.ANY)] * 3 + [spec] * 2,
            out_specs=[out(r) for r in rows],
            scratch_shapes=[pltpu.SMEM((levels, heads), jnp.int32)]
            + [pltpu.VMEM((tok, per * dim), BF16)] * 2
            + [pltpu.SemaphoreType.DMA((3,))],
        ),
        out_shape=[jax.ShapeDtypeStruct((r, width), BF16) for r in rows],
        compiler_params=params(),
        name="pick_rows",
    )(core, offsets, *own, *other)


def own_spec(tok, cols, steps):
    return pl.BlockSpec((tok, cols), lambda i, o, c: (0, c[0] * steps + i))


def side(*values):
    return jnp.concatenate(values, axis=1)


def stack(*values):
    return jnp.concatenate(values, axis=0)


def split(value, terms):
    parts = []
    for _ in range(terms):
        part = value.astype(BF16)
        parts.append(part)
        value = value - part.astype(F32)
    return parts


def local_scores(pick, levels, offs_ref, head, key0, key1, ones, que0, que1):
    tok, dim = key0.shape
    pos = lax.broadcasted_iota(jnp.int32, (1, 2 * tok), 1)
    bias = jnp.where(lax.rem(pos, 2) == lax.rem(offs_ref[0, head], 2), 0.0, NEG).astype(F32)
    s0 = side(dot_nt(key0, que0), dot_nt(key1, que1)) * dim**-0.5
    s1 = dot_nt(ones, stack(que0, que1)) * dim**-0.5 + bias
    return stack(s0, s1)


def pre_kernel(
    levels, per, dim, offs_ref, core_ref, q0, q1, k0, k1, v0, v1, exp0, exp1, stats, near, selq
):
    tok = q0.shape[0]
    n1 = tok // 2
    heads = per * pl.num_programs(0)
    for h in range(per):
        head = core_ref[0] * heads + pl.program_id(0) * per + h
        pick = pick_matrix(offs_ref, head, 1, levels, tok)
        cols = slice(h * dim, (h + 1) * dim)
        wide = slice(2 * h * dim, 2 * (h + 1) * dim)
        lanes = slice(2 * h * tok, 2 * (h + 1) * tok)
        own = dot(pick[:n1], side(k0[:, cols], v0[:, cols])).astype(BF16)
        oth = dot(pick[:n1], side(k1[:, cols], v1[:, cols])).astype(BF16)
        ones = stack(own, oth)
        near[:, wide] = ones
        que0, que1 = q0[:, cols], q1[:, cols]
        far_pick = pick[n1:]
        selq[:, cols] = stack(dot(far_pick, que0), dot(far_pick, que1)).astype(BF16)
        s = local_scores(
            pick, levels, offs_ref, head, k0[:, cols], k1[:, cols], ones[:, :dim], que0, que1
        )
        top = jnp.max(s, axis=0, keepdims=True)
        e = jnp.exp(s - top)
        for half, ref in enumerate((exp0, exp1)):
            ref[:, h * tok : (h + 1) * tok] = e[:, half * tok : (half + 1) * tok].astype(BF16)
        stats[0:1, lanes] = top
        stats[1:2, lanes] = jnp.sum(e, axis=0, keepdims=True)


def pre_call(offsets, core, raw, dim):
    tok, width = raw[0].shape
    levels, heads = offsets.shape
    half = heads // 2
    per = 8
    steps = half // per
    raw_spec = own_spec(tok, per * dim, steps)
    sel = 2 * (tok // 4 + tok // 8)

    def out(rows, lanes, kind=BF16):
        return (
            pl.BlockSpec((rows, per * lanes), lambda i, o, c: (0, i)),
            jax.ShapeDtypeStruct((rows, half * lanes), kind),
        )

    outs = [out(2 * tok, tok), out(2 * tok, tok), out(8, 2 * tok, F32), out(tok, 2 * dim), out(sel, dim)]
    return pl.pallas_call(
        functools.partial(pre_kernel, levels, per, dim),
        grid_spec=pltpu.PrefetchScalarGridSpec(
            num_scalar_prefetch=2,
            grid=(steps,),
            in_specs=[raw_spec] * 6,
            out_specs=[o[0] for o in outs],
        ),
        out_shape=[o[1] for o in outs],
        compiler_params=params(),
        name="local_scores",
    )(offsets, core, *raw)


def local_delta(exps, values, ones, grads):
    tok = values.shape[0]
    p0, p1 = dot_nt(values, grads), dot_nt(ones, grads)
    both = exps[:tok].astype(F32) * p0 + exps[tok:].astype(F32) * p1
    return jnp.sum(both, axis=0, keepdims=True)


def grad_kernel(levels, per, dim, offs_ref, core_ref, exps, near, values, grads, selg, local):
    tok = values.shape[0]
    first = core_ref[0] * per
    each = range(per)
    cols = [slice(h * dim, (h + 1) * dim) for h in each]
    for h in each:
        pick = pick_matrix(offs_ref, first + h, 2, levels, tok)
        selg[:, cols[h]] = dot(pick, grads[:, cols[h]]).astype(BF16)
    for h in each:
        here = slice(h * tok, (h + 1) * tok)
        vc = slice((2 * h + 1) * dim, (2 * h + 2) * dim)
        local[0:1, here] = local_delta(
            exps[:, here], values[:, cols[h]], near[:, vc], grads[:, cols[h]]
        )


def grad_call(offsets, core, exps, near, values, grads, dim):
    tok, width = values.shape
    levels, heads = offsets.shape
    per = heads // 2
    raw_spec = own_spec(tok, per * dim, 1)

    def whole(a):
        return pl.BlockSpec(a.shape, lambda i, o, c: (0, 0))

    outs = [
        jax.ShapeDtypeStruct((tok // 4 + tok // 8, per * dim), BF16),
        jax.ShapeDtypeStruct((8, per * tok), F32),
    ]
    return pl.pallas_call(
        functools.partial(grad_kernel, levels, per, dim),
        grid_spec=pltpu.PrefetchScalarGridSpec(
            num_scalar_prefetch=2,
            grid=(1,),
            in_specs=[whole(exps), whole(near), raw_spec, raw_spec],
            out_specs=[whole(a) for a in outs],
        ),
        out_shape=outs,
        compiler_params=params(),
        name="own_delta",
    )(offsets, core, exps, near, values, grads)


def far_kernel(
    levels, per, dim, offs_ref, core_ref, stats, selq, selg0, local0, exp1, near, v1,
    own2, x2, own3, x3, y3, d3, *refs
):
    xa, xb, xab, yab, dab, ngrad, dqt, stats2 = refs[-8:]
    g1 = side(*(ref[...] for ref in refs[:-8]))
    tok = dqt.shape[0]
    n1, n2, n3 = tok // 2, tok // 4, tok // 8
    sel = n2 + n3
    scale = dim**-0.5
    heads = per * pl.num_programs(0)
    lane = lax.broadcasted_iota(jnp.int32, (1, 2 * sel), 1)
    is2 = lax.rem(lane, sel) < n2
    pos = lax.broadcasted_iota(jnp.int32, (1, 2 * tok), 1)
    first = core_ref[0] * heads + pl.program_id(0) * per
    each = range(per)
    cols = [slice(h * dim, (h + 1) * dim) for h in each]
    kc = [slice(2 * h * dim, (2 * h + 1) * dim) for h in each]
    vc = [slice((2 * h + 1) * dim, (2 * h + 2) * dim) for h in each]
    wide = [slice(2 * h * dim, 2 * (h + 1) * dim) for h in each]
    lanes = [slice(2 * h * tok, 2 * (h + 1) * tok) for h in each]

    def rows(c):
        return stack(*(ref[:, c] for ref in (own2, x2, own3, x3, y3, d3)))

    def level_pick(value):
        return jnp.where(is2, value[:tok], value[tok:])

    picks = [pick_matrix(offs_ref, first + h, 2, levels, tok) for h in each]
    selg = [
        stack(selg0[:, cols[h]], dot(picks[h], g1[:, cols[h]]).astype(BF16)) for h in each
    ]
    keys = [rows(kc[h]) for h in each]
    s = [level_pick(dot_nt(keys[h], selq[:, cols[h]])) * scale for h in each]
    p = [level_pick(dot_nt(rows(vc[h]), selg[h])) for h in each]
    local1 = [
        local_delta(exp1[:, h * tok : (h + 1) * tok], v1[:, cols[h]], near[:, vc[h]], g1[:, cols[h]])
        for h in each
    ]
    top = [jnp.max(a, axis=0, keepdims=True) for a in s]
    e = [jnp.exp(a - b) for a, b in zip(s, top)]
    size = [jnp.sum(a, axis=0, keepdims=True) for a in e]
    dhat = [jnp.sum(a * b, axis=0, keepdims=True) for a, b in zip(e, p)]
    none = jnp.zeros_like(picks[0])
    spots = [stack(side(a, none), side(none, a)) for a in picks]
    spread = []
    for h in each:
        terms = stack(*split(top[h], 3), *split(size[h], 2), *split(dhat[h], 3))
        zero = jnp.zeros_like(terms)
        apart = stack(jnp.where(is2, terms, zero), jnp.where(is2, zero, terms))
        spread.append(dot(apart, spots[h]))
    back = []
    for h in each:

        def level_stats(level, lo):
            rate = 2**level
            on = lax.rem(pos, rate) == lax.rem(offs_ref[level - 1, first + h], rate)
            t = [spread[h][lo + i : lo + i + 1] for i in range(8)]
            return jnp.where(on, t[0] + t[1] + t[2], NEG), t[3] + t[4], t[5] + t[6] + t[7]

        t1, z1 = stats[0:1, lanes[h]], stats[1:2, lanes[h]]
        t2, z2, dot2 = level_stats(2, 0)
        t3, z3, dot3 = level_stats(3, 8)
        high = jnp.maximum(t1, jnp.maximum(t2, t3))
        a1, a2, a3 = jnp.exp(t1 - high), jnp.exp(t2 - high), jnp.exp(t3 - high)
        inv = 1.0 / (a1 * z1 + a2 * z2 + a3 * z3)
        f1, f2, f3 = a1 * inv, a2 * inv, a3 * inv
        delta = f1 * side(local0[0:1, h * tok : (h + 1) * tok], local1[h]) + f2 * dot2 + f3 * dot3
        stats2[0:1, lanes[h]] = f1
        stats2[1:2, lanes[h]] = delta
        terms = stack(*split(f2, 2), *split(f3, 2), *split(delta, 3))
        back.append(dot_nt(terms, spots[h]))

    def apart(value):
        zero = jnp.zeros_like(value)
        return stack(jnp.where(is2, value, zero), jnp.where(is2, zero, value)).astype(BF16)

    dsm, wm = [], []
    for h in each:
        b = back[h]
        w = e[h] * jnp.where(is2, b[0:1] + b[1:2], b[2:3] + b[3:4])
        dsm.append(apart(w * (p[h] - (b[4:5] + b[5:6] + b[6:7]))))
        wm.append(apart(w))
    dk = [dot(dsm[h], selq[:, cols[h]]) * scale for h in each]
    dv = [dot(wm[h], selg[h]) for h in each]
    for h in each:
        dkv = side(dk[h], dv[h]).astype(BF16)
        xa[:, wide[h]] = dkv[2 * n2 : 3 * n2]
        xb[:, wide[h]] = dkv[3 * n2 : 4 * n2]
        third = [dkv[tok + i * n3 : tok + (i + 1) * n3] for i in range(8)]
        xab[:, wide[h]] = stack(third[2], third[3])
        yab[:, wide[h]] = stack(third[4], third[5])
        dab[:, wide[h]] = stack(third[6], third[7])
        ngrad[:, wide[h]] = stack(dkv[:n2], third[0], dkv[n2 : 2 * n2], third[1])
        dqt[:, h * dim : h * dim + 2 * sel] = dot(keys[h].T, dsm[h]).astype(BF16)


def far_call(offsets, core, mid, value, far, tok, dim):
    levels, heads = offsets.shape
    half = heads // 2
    per = 8
    steps = half // per
    n2, n3 = tok // 4, tok // 8

    def mid_spec(a):
        return pl.BlockSpec((a.shape[0], a.shape[1] // steps), lambda i, o, c: (0, i))

    def out(rows, lanes, kind=BF16):
        return (
            pl.BlockSpec((rows, per * lanes), lambda i, o, c: (0, i)),
            jax.ShapeDtypeStruct((rows, half * lanes), kind),
        )

    outs = [out(n2, 2 * dim)] * 2 + [out(2 * n3, 2 * dim)] * 3
    outs += [out(2 * (n2 + n3), 2 * dim), out(dim, dim), out(8, 2 * tok, F32)]
    return pl.pallas_call(
        functools.partial(far_kernel, levels, per, dim),
        grid_spec=pltpu.PrefetchScalarGridSpec(
            num_scalar_prefetch=2,
            grid=(steps,),
            in_specs=[mid_spec(a) for a in mid]
            + [own_spec(tok, per * dim, steps)]
            + [mid_spec(a) for a in far],
            out_specs=[o[0] for o in outs],
        ),
        out_shape=[o[1] for o in outs],
        compiler_params=params(),
        name="far_levels",
    )(offsets, core, *mid, value, *far)


def near_kernel(
    levels, per, dim, offs_ref, core_ref, exp0, exp1, stats2, near, ngrad, dqt,
    q0, q1, k0, k1, v0, v1, g0, *refs,
):
    mine, *others = refs[-3:]
    g1 = side(*(ref[...] for ref in refs[:-3]))
    tok = q0.shape[0]
    n1 = tok // 2
    sel = tok // 4 + tok // 8
    scale = dim**-0.5
    heads = per * pl.num_programs(0)
    first = core_ref[0] * heads + pl.program_id(0) * per
    for lo in range(0, per, 4):
        each = range(lo, lo + 4)
        cols = {h: slice(h * dim, (h + 1) * dim) for h in each}
        vc = {h: slice((2 * h + 1) * dim, (2 * h + 2) * dim) for h in each}
        gra = {h: stack(g0[:, cols[h]], g1[:, cols[h]]) for h in each}
        que = {h: stack(q0[:, cols[h]], q1[:, cols[h]]) for h in each}
        wb, ds = {}, {}
        for h in each:
            lanes = slice(2 * h * tok, 2 * (h + 1) * tok)
            here = slice(h * tok, (h + 1) * tok)
            p0 = dot_nt(v0[:, cols[h]], gra[h][:tok])
            p1 = dot_nt(v1[:, cols[h]], gra[h][tok:])
            p = stack(side(p0, p1), dot_nt(near[:tok, vc[h]], gra[h]))
            w = side(exp0[:, here], exp1[:, here]).astype(F32) * stats2[0:1, lanes]
            wb[h] = w.astype(BF16)
            ds[h] = (w * (p - stats2[1:2, lanes])).astype(BF16)
        dkv1 = {
            h: side(dot(ds[h][tok:], que[h]) * scale, dot(wb[h][tok:], gra[h])).astype(BF16)
            for h in each
        }
        for block, keys in enumerate((k0, k1)):
            at = slice(block * tok, (block + 1) * tok)
            picked = slice(block * n1, (block + 1) * n1)
            grads = slice(block * sel, (block + 1) * sel)
            kv, dq = {}, {}
            for h in each:
                place = place_matrix(offs_ref, first + h, 1, levels, tok)
                wide = slice(2 * h * dim, 2 * (h + 1) * dim)
                d0, w0 = ds[h][:tok, at], wb[h][:tok, at]
                kv[h] = side(dot(d0, que[h][at]) * scale, dot(w0, gra[h][at]))
                kv[h] += dot(place, stack(dkv1[h][picked], ngrad[grads, wide]))
            for h in each:
                pick = pick_matrix(offs_ref, first + h, 2, levels, tok)
                kc = slice(2 * h * dim, (2 * h + 1) * dim)
                far = dqt[:, h * dim + block * sel : h * dim + (block + 1) * sel]
                both = stack(keys[:, cols[h]], near[:tok, kc])
                dq[h] = dot(both.T, ds[h][:, at]) + dot(far, pick)
            for h in each:
                ref, to = (others[h // (per // 2)], h % (per // 2)) if block else (mine, h)
                to *= 3 * dim
                ref[:, to : to + dim] = (dq[h] * scale).T.astype(BF16)
                ref[:, to + dim : to + 3 * dim] = kv[h].astype(BF16)


def near_call(offsets, core, mid, raw, grads, dim):
    tok, width = raw[0].shape
    levels, heads = offsets.shape
    half = heads // 2
    per = 8
    steps = half // per
    raw_spec = own_spec(tok, per * dim, steps)

    def mid_spec(a):
        return pl.BlockSpec((a.shape[0], a.shape[1] // steps), lambda i, o, c: (0, i))

    widths = [3 * per * dim, 3 * per * dim // 2, 3 * per * dim // 2]
    return pl.pallas_call(
        functools.partial(near_kernel, levels, per, dim),
        grid_spec=pltpu.PrefetchScalarGridSpec(
            num_scalar_prefetch=2,
            grid=(steps,),
            in_specs=[mid_spec(a) for a in mid] + [raw_spec] * 7
            + [mid_spec(a) for a in grads[1:]],
            out_specs=[pl.BlockSpec((tok, w), lambda i, o, c: (0, 0)) for w in widths],
        ),
        out_shape=[jax.ShapeDtypeStruct((tok, w), BF16) for w in widths],
        compiler_params=params(),
        name="near_levels",
    )(offsets, core, *mid, *raw, *grads)


def sum_kernel(here, there, first, second):
    total = (here[...].astype(F32) + there[...].astype(F32)).astype(BF16)
    rows = first.shape[0]
    first[...] = total[:rows]
    second[...] = total[rows:]


def sum_call(here, there):
    rows, cols = here.shape
    return pl.pallas_call(
        sum_kernel,
        out_shape=[jax.ShapeDtypeStruct((rows // 2, cols), BF16)] * 2,
        compiler_params=params(),
        name="add_diagonal",
    )(here, there)


def add_far(levels, dim, offs_ref, first, bases, x, third, group):
    tok = bases[0].shape[0]
    per = sum(base.shape[1] for base in bases) // (3 * dim)
    in_base = per // len(bases)
    for lo in range(0, per, group):
        each = range(lo, lo + group)
        src = {h: slice(2 * h * dim, 2 * (h + 1) * dim) for h in each}
        place = {h: place_matrix(offs_ref, first + h, 2, levels, tok) for h in each}
        more = {h: dot(place[h], stack(x[:, src[h]], third[:, src[h]])) for h in each}
        for h in each:
            base, at = bases[h // in_base], (3 * (h % in_base) + 1) * dim
            yield h, (base[:, at : at + 2 * dim].astype(F32) + more[h]).astype(BF16)


def own_kernel(levels, per, dim, offs_ref, core_ref, base, x, y, x3, dq, dk, dv):
    n3 = x3.shape[0]
    third = (x3[...].astype(F32) + y[:n3].astype(F32)).astype(BF16)
    for h in range(per):
        dq[:, h * dim : (h + 1) * dim] = base[:, 3 * h * dim : (3 * h + 1) * dim]
    for h, total in add_far(levels, dim, offs_ref, core_ref[0] * per, [base], x, third, per):
        cols = slice(h * dim, (h + 1) * dim)
        dk[:, cols] = total[:, :dim]
        dv[:, cols] = total[:, dim:]


def own_call(offsets, core, parts, dim):
    levels, heads = offsets.shape
    tok = parts[0].shape[0]
    per = heads // 2
    return pl.pallas_call(
        functools.partial(own_kernel, levels, per, dim),
        grid_spec=pltpu.PrefetchScalarGridSpec(
            num_scalar_prefetch=2,
            grid=(1,),
            in_specs=[pl.BlockSpec(a.shape, lambda i, o, c: (0, 0)) for a in parts],
            out_specs=[pl.BlockSpec((tok, per * dim), lambda i, o, c: (0, 0))] * 3,
        ),
        out_shape=[jax.ShapeDtypeStruct((tok, per * dim), BF16)] * 3,
        compiler_params=params(),
        name="add_own_half",
    )(offsets, core, *parts)


def final_kernel(
    levels, per, dim, offs_ref, core_ref, own_q, own_k, own_v, base0, base1, x, y, x3,
    dq, dk, dv, held, sems,
):
    outs = dq, dk, dv
    n3 = x3.shape[0]
    copies = []

    def send(part, here, core, lo, n):
        cols = pl.ds(pl.multiple_of((core * per + lo) * dim, dim), n * dim)
        copies.append(pltpu.make_async_copy(here, outs[part].at[:, cols], sems.at[len(copies)]))
        copies[-1].start()

    for part, ref in enumerate((own_q, own_k, own_v)):
        send(part, ref, core_ref[0], 0, per)
    far_core = 1 - core_ref[0]
    half = per // 2
    for h in range(per):
        base = base1 if h >= half else base0
        at = 3 * (h % half) * dim
        held[0, :, h * dim : (h + 1) * dim] = base[:, at : at + dim]
    send(0, held.at[0], far_core, 0, per)
    third = (x3[...].astype(F32) + y[n3:].astype(F32)).astype(BF16)
    bases = [base0, base1]
    for h, total in add_far(levels, dim, offs_ref, far_core * per, bases, x, third, 4):
        cols = slice(h * dim, (h + 1) * dim)
        held[1, :, cols] = total[:, :dim]
        held[2, :, cols] = total[:, dim:]
        if (h + 1) % 4 == 0:
            for part in (1, 2):
                lo = h + 1 - 4
                send(part, held.at[part, :, pl.ds(lo * dim, 4 * dim)], far_core, lo, 4)
    for copy in copies:
        copy.wait()


def final_call(offsets, core, own, parts, dim):
    levels, heads = offsets.shape
    tok = parts[0].shape[0]
    per = heads // 2
    away = pl.BlockSpec(memory_space=pl.ANY)
    return pl.pallas_call(
        functools.partial(final_kernel, levels, per, dim),
        grid_spec=pltpu.PrefetchScalarGridSpec(
            num_scalar_prefetch=2,
            grid=(1,),
            in_specs=[pl.BlockSpec(a.shape, lambda i, o, c: (0, 0)) for a in own + parts],
            out_specs=[away] * 3,
            scratch_shapes=[
                pltpu.VMEM((3, tok, per * dim), BF16),
                pltpu.SemaphoreType.DMA((4 + 2 * (per // 4),)),
            ],
        ),
        out_shape=[jax.ShapeDtypeStruct((tok, heads * dim), BF16)] * 3,
        compiler_params=params(),
        name="add_other_half",
    )(offsets, core, *own, *parts)


def per_device(queries, keys_in, values, out_grads, offsets):
    heads = offsets.shape[1]
    dim = queries.shape[2] // heads
    core = lax.rem(lax.axis_index("seq"), 2).astype(jnp.int32).reshape(1)
    q, k, v = queries[0], keys_in[0], values[0]
    sections = lax.axis_size("section")
    grads = lax.ppermute(
        out_grads[0], "section", [(i, (i - 1) % sections) for i in range(sections)]
    )
    q_oth, k_oth, v_oth = exchange(q, 1), exchange(k, 1), exchange(v, 1)
    kept = [pltpu.with_memory_space_constraint(a, pltpu.HBM) for a in (k, v)]
    two, three = pick_call(
        pltpu.with_memory_space_constraint(offsets, pltpu.HBM), core, kept, [k_oth, v_oth], dim
    )
    x3, y3, x2 = exchange(three, 2), exchange(three, 4), exchange(two, 2)
    x3, y3 = lax.optimization_barrier((x3, y3))
    d3 = exchange(x3, 4)
    raw = [q, q_oth, k, k_oth, v, v_oth]
    pre = pre_call(offsets, core, raw, dim)
    exp0, exp1, stats, near, selq = pre
    grads = lax.optimization_barrier((grads, stats))[0]
    sel = grad_call(offsets, core, exp0, near, v, grads, dim)
    half = heads // 2
    cuts = [half * i // 3 for i in range(4)]
    sizes = [(hi - lo) * dim for lo, hi in zip(cuts, cuts[1:])]
    other = [exchange(piece, 1) for piece in pack_call(core, grads, sizes)]
    other = lax.optimization_barrier((*other, sel[1]))[:-1]
    xa, xb, xab, yab, dab, ngrad, dqt, stats2 = far_call(
        offsets, core, [stats, selq, *sel, exp1, near], v_oth,
        [two, x2, three, x3, y3, d3, *other], q.shape[0], dim,
    )
    thirds = sum_call(xab, exchange(dab, 4))
    xa, xb, y = exchange(xa, 2), exchange(xb, 3), exchange(yab, 4)
    xa3, xb3 = exchange(thirds[0], 2), exchange(thirds[1], 3)
    yy = exchange(y, 1)
    mine, first, second = near_call(
        offsets, core, [exp0, exp1, stats2, near, ngrad, dqt], raw, [grads, *other], dim
    )
    first = exchange(first, 1)
    second, xa, xb, xa3, xb3, y = lax.optimization_barrier((second, xa, xb, xa3, xb3, y))
    own = list(own_call(offsets, core, [mine, xa, y, xa3], dim))
    dq, dk, dv = final_call(
        offsets, core, own, [first, exchange(second, 1), xb, yy, xb3], dim
    )
    return dq[None], dk[None], dv[None]


def solution(mesh):
    spec = P("section", "seq", None)
    return jax.shard_map(
        per_device,
        mesh=mesh,
        in_specs=(spec, spec, spec, spec, P()),
        out_specs=(spec, spec, spec),
        check_vma=False,
    )
```

```python
import functools

import jax
import jax.numpy as jnp
from jax import lax
from jax.experimental import pallas as pl
from jax.experimental.pallas import tpu as pltpu
from jax.sharding import PartitionSpec as P

F32 = jnp.float32
BF16 = jnp.bfloat16
NEG = -1e30
VMEM_LIMIT = 32 * 1024 * 1024
PIECES = 4


def params():
    return pltpu.CompilerParams(vmem_limit_bytes=VMEM_LIMIT)


def exchange(value, bits):
    count = lax.axis_size("seq")
    return lax.ppermute(value, "seq", [(i, i ^ bits) for i in range(count)])


def dot(a, b):
    return jnp.dot(a, b, preferred_element_type=F32)


def dot_nt(a, b):
    return lax.dot_general(a, b, (((1,), (1,)), ((), ())), preferred_element_type=F32)


def pick_matrix(offs_ref, head, first, levels, tok):
    parts = []
    for level in range(first, levels + 1):
        rate = 2**level
        rows = tok // rate
        kept = lax.rem(offs_ref[level - 1, head], rate)
        row = lax.broadcasted_iota(jnp.int32, (rows, tok), 0)
        col = lax.broadcasted_iota(jnp.int32, (rows, tok), 1)
        parts.append((col == row * rate + kept).astype(F32))
    return jnp.concatenate(parts, axis=0).astype(BF16)


def place_matrix(offs_ref, head, first, levels, tok):
    parts = []
    for level in range(first, levels + 1):
        rate = 2**level
        rows = tok // rate
        kept = lax.rem(offs_ref[level - 1, head], rate)
        row = lax.broadcasted_iota(jnp.int32, (tok, rows), 0)
        col = lax.broadcasted_iota(jnp.int32, (tok, rows), 1)
        parts.append((row == col * rate + kept).astype(F32))
    return jnp.concatenate(parts, axis=1).astype(BF16)


def pack_kernel(core_ref, rows, *outs):
    lo = 0
    for out in outs:
        out[...] = rows[:, lo : lo + out.shape[1]]
        lo += out.shape[1]


def pack_call(core, rows, sizes):
    tok, width = rows.shape
    half = width // 2
    return pl.pallas_call(
        pack_kernel,
        grid_spec=pltpu.PrefetchScalarGridSpec(
            num_scalar_prefetch=1,
            grid=(1,),
            in_specs=[pl.BlockSpec((tok, half), lambda i, c: (0, 1 - c[0]))],
            out_specs=[pl.BlockSpec((tok, n), lambda i, c: (0, 0)) for n in sizes],
        ),
        out_shape=[jax.ShapeDtypeStruct((tok, n), BF16) for n in sizes],
        compiler_params=params(),
        name="pack_half",
    )(core, rows)


def pick_kernel(
    levels, per, dim, core_ref, offs, k0, v0, k1, v1, two_ref, three_ref, offs_ref, own_k, own_v, sems
):
    tok = k1.shape[0]
    n2, n3 = tok // 4, tok // 8
    each = range(per)
    mine = pl.ds(pl.multiple_of(core_ref[0] * per * dim, per * dim), per * dim)
    copies = [
        pltpu.make_async_copy(src.at[:, mine], dst, sems.at[i])
        for i, (src, dst) in enumerate(((k0, own_k), (v0, own_v)))
    ]
    table = pltpu.make_async_copy(offs, offs_ref, sems.at[2])
    table.start()
    for copy in copies:
        copy.start()
    table.wait()
    picks = [pick_matrix(offs_ref, core_ref[0] * per + h, 2, levels, tok) for h in each]

    def work(keys, values, lo):
        for h in each:
            cols = slice(h * dim, (h + 1) * dim)
            out = slice(2 * h * dim, 2 * (h + 1) * dim)
            got = dot(picks[h], side(keys[:, cols], values[:, cols])).astype(BF16)
            two_ref[lo * n2 : (lo + 1) * n2, out] = got[:n2]
            three_ref[lo * n3 : (lo + 1) * n3, out] = got[n2:]

    work(k1, v1, 1)
    for copy in copies:
        copy.wait()
    work(own_k, own_v, 0)


def pick_call(offsets, core, own, other, dim):
    tok, width = own[0].shape
    levels, heads = offsets.shape
    per = heads // 2
    spec = pl.BlockSpec((tok, per * dim), lambda i, c: (0, c[0]))

    def out(rows):
        return pl.BlockSpec((rows, 2 * per * dim), lambda i, c: (0, 0))

    rows = [tok // 2, tok // 4]
    return pl.pallas_call(
        functools.partial(pick_kernel, levels, per, dim),
        grid_spec=pltpu.PrefetchScalarGridSpec(
            num_scalar_prefetch=1,
            grid=(1,),
            in_specs=[pl.BlockSpec(memory_space=pl.ANY)] * 3 + [spec] * 2,
            out_specs=[out(r) for r in rows],
            scratch_shapes=[pltpu.SMEM((levels, heads), jnp.int32)]
            + [pltpu.VMEM((tok, per * dim), BF16)] * 2
            + [pltpu.SemaphoreType.DMA((3,))],
        ),
        out_shape=[jax.ShapeDtypeStruct((r, width), BF16) for r in rows],
        compiler_params=params(),
        name="pick_rows",
    )(core, offsets, *own, *other)


def own_spec(tok, cols, steps):
    return pl.BlockSpec((tok, cols), lambda i, o, c: (0, c[0] * steps + i))


def side(*values):
    return jnp.concatenate(values, axis=1)


def stack(*values):
    return jnp.concatenate(values, axis=0)


def split(value, terms):
    parts = []
    for _ in range(terms):
        part = value.astype(BF16)
        parts.append(part)
        value = value - part.astype(F32)
    return parts


def local_scores(pick, levels, offs_ref, head, key0, key1, ones, que0, que1):
    tok, dim = key0.shape
    pos = lax.broadcasted_iota(jnp.int32, (1, 2 * tok), 1)
    bias = jnp.where(lax.rem(pos, 2) == lax.rem(offs_ref[0, head], 2), 0.0, NEG).astype(F32)
    s0 = side(dot_nt(key0, que0), dot_nt(key1, que1)) * dim**-0.5
    s1 = dot_nt(ones, stack(que0, que1)) * dim**-0.5 + bias
    return stack(s0, s1)


def pre_kernel(
    levels, per, dim, offs_ref, core_ref, q0, q1, k0, k1, v0, v1, exp0, exp1, stats, near, selq
):
    tok = q0.shape[0]
    n1 = tok // 2
    heads = per * pl.num_programs(0)
    for h in range(per):
        head = core_ref[0] * heads + pl.program_id(0) * per + h
        pick = pick_matrix(offs_ref, head, 1, levels, tok)
        cols = slice(h * dim, (h + 1) * dim)
        wide = slice(2 * h * dim, 2 * (h + 1) * dim)
        lanes = slice(2 * h * tok, 2 * (h + 1) * tok)
        own = dot(pick[:n1], side(k0[:, cols], v0[:, cols])).astype(BF16)
        oth = dot(pick[:n1], side(k1[:, cols], v1[:, cols])).astype(BF16)
        ones = stack(own, oth)
        near[:, wide] = ones
        que0, que1 = q0[:, cols], q1[:, cols]
        far_pick = pick[n1:]
        selq[:, cols] = stack(dot(far_pick, que0), dot(far_pick, que1)).astype(BF16)
        s = local_scores(
            pick, levels, offs_ref, head, k0[:, cols], k1[:, cols], ones[:, :dim], que0, que1
        )
        top = jnp.max(s, axis=0, keepdims=True)
        e = jnp.exp(s - top)
        for half, ref in enumerate((exp0, exp1)):
            ref[:, h * tok : (h + 1) * tok] = e[:, half * tok : (half + 1) * tok].astype(BF16)
        stats[0:1, lanes] = top
        stats[1:2, lanes] = jnp.sum(e, axis=0, keepdims=True)


def pre_call(offsets, core, raw, dim):
    tok, width = raw[0].shape
    levels, heads = offsets.shape
    half = heads // 2
    per = 8
    steps = half // per
    raw_spec = own_spec(tok, per * dim, steps)
    sel = 2 * (tok // 4 + tok // 8)

    def out(rows, lanes, kind=BF16):
        return (
            pl.BlockSpec((rows, per * lanes), lambda i, o, c: (0, i)),
            jax.ShapeDtypeStruct((rows, half * lanes), kind),
        )

    outs = [out(2 * tok, tok), out(2 * tok, tok), out(8, 2 * tok, F32), out(tok, 2 * dim), out(sel, dim)]
    return pl.pallas_call(
        functools.partial(pre_kernel, levels, per, dim),
        grid_spec=pltpu.PrefetchScalarGridSpec(
            num_scalar_prefetch=2,
            grid=(steps,),
            in_specs=[raw_spec] * 6,
            out_specs=[o[0] for o in outs],
        ),
        out_shape=[o[1] for o in outs],
        compiler_params=params(),
        name="local_scores",
    )(offsets, core, *raw)


def local_delta(exps, values, ones, grads):
    tok = values.shape[0]
    p0, p1 = dot_nt(values, grads), dot_nt(ones, grads)
    both = exps[:tok].astype(F32) * p0 + exps[tok:].astype(F32) * p1
    return jnp.sum(both, axis=0, keepdims=True)


def grad_kernel(levels, per, dim, offs_ref, core_ref, exps, near, values, grads, selg, local):
    tok = values.shape[0]
    first = core_ref[0] * per
    each = range(per)
    cols = [slice(h * dim, (h + 1) * dim) for h in each]
    for h in each:
        pick = pick_matrix(offs_ref, first + h, 2, levels, tok)
        selg[:, cols[h]] = dot(pick, grads[:, cols[h]]).astype(BF16)
    for h in each:
        here = slice(h * tok, (h + 1) * tok)
        vc = slice((2 * h + 1) * dim, (2 * h + 2) * dim)
        local[0:1, here] = local_delta(
            exps[:, here], values[:, cols[h]], near[:, vc], grads[:, cols[h]]
        )


def grad_call(offsets, core, exps, near, values, grads, dim):
    tok, width = values.shape
    levels, heads = offsets.shape
    per = heads // 2
    raw_spec = own_spec(tok, per * dim, 1)

    def whole(a):
        return pl.BlockSpec(a.shape, lambda i, o, c: (0, 0))

    outs = [
        jax.ShapeDtypeStruct((tok // 4 + tok // 8, per * dim), BF16),
        jax.ShapeDtypeStruct((8, per * tok), F32),
    ]
    return pl.pallas_call(
        functools.partial(grad_kernel, levels, per, dim),
        grid_spec=pltpu.PrefetchScalarGridSpec(
            num_scalar_prefetch=2,
            grid=(1,),
            in_specs=[whole(exps), whole(near), raw_spec, raw_spec],
            out_specs=[whole(a) for a in outs],
        ),
        out_shape=outs,
        compiler_params=params(),
        name="own_delta",
    )(offsets, core, exps, near, values, grads)


def far_kernel(
    levels, per, dim, offs_ref, core_ref, stats, selq, selg0, local0, exp1, near, v1,
    own2, x2, own3, x3, y3, d3, *refs
):
    xa, xb, xab, yab, dab, ngrad, dqt, stats2 = refs[-8:]
    g1 = side(*(ref[...] for ref in refs[:-8]))
    tok = dqt.shape[0]
    n1, n2, n3 = tok // 2, tok // 4, tok // 8
    sel = n2 + n3
    scale = dim**-0.5
    heads = per * pl.num_programs(0)
    lane = lax.broadcasted_iota(jnp.int32, (1, 2 * sel), 1)
    is2 = lax.rem(lane, sel) < n2
    pos = lax.broadcasted_iota(jnp.int32, (1, 2 * tok), 1)
    first = core_ref[0] * heads + pl.program_id(0) * per
    each = range(per)
    cols = [slice(h * dim, (h + 1) * dim) for h in each]
    kc = [slice(2 * h * dim, (2 * h + 1) * dim) for h in each]
    vc = [slice((2 * h + 1) * dim, (2 * h + 2) * dim) for h in each]
    wide = [slice(2 * h * dim, 2 * (h + 1) * dim) for h in each]
    lanes = [slice(2 * h * tok, 2 * (h + 1) * tok) for h in each]

    def rows(c):
        return stack(*(ref[:, c] for ref in (own2, x2, own3, x3, y3, d3)))

    def level_pick(value):
        return jnp.where(is2, value[:tok], value[tok:])

    picks = [pick_matrix(offs_ref, first + h, 2, levels, tok) for h in each]
    selg = [
        stack(selg0[:, cols[h]], dot(picks[h], g1[:, cols[h]]).astype(BF16)) for h in each
    ]
    keys = [rows(kc[h]) for h in each]
    s = [level_pick(dot_nt(keys[h], selq[:, cols[h]])) * scale for h in each]
    p = [level_pick(dot_nt(rows(vc[h]), selg[h])) for h in each]
    local1 = [
        local_delta(exp1[:, h * tok : (h + 1) * tok], v1[:, cols[h]], near[:, vc[h]], g1[:, cols[h]])
        for h in each
    ]
    top = [jnp.max(a, axis=0, keepdims=True) for a in s]
    e = [jnp.exp(a - b) for a, b in zip(s, top)]
    size = [jnp.sum(a, axis=0, keepdims=True) for a in e]
    dhat = [jnp.sum(a * b, axis=0, keepdims=True) for a, b in zip(e, p)]
    none = jnp.zeros_like(picks[0])
    spots = [stack(side(a, none), side(none, a)) for a in picks]
    spread = []
    for h in each:
        terms = stack(*split(top[h], 3), *split(size[h], 2), *split(dhat[h], 3))
        zero = jnp.zeros_like(terms)
        apart = stack(jnp.where(is2, terms, zero), jnp.where(is2, zero, terms))
        spread.append(dot(apart, spots[h]))
    back = []
    for h in each:

        def level_stats(level, lo):
            rate = 2**level
            on = lax.rem(pos, rate) == lax.rem(offs_ref[level - 1, first + h], rate)
            t = [spread[h][lo + i : lo + i + 1] for i in range(8)]
            return jnp.where(on, t[0] + t[1] + t[2], NEG), t[3] + t[4], t[5] + t[6] + t[7]

        t1, z1 = stats[0:1, lanes[h]], stats[1:2, lanes[h]]
        t2, z2, dot2 = level_stats(2, 0)
        t3, z3, dot3 = level_stats(3, 8)
        high = jnp.maximum(t1, jnp.maximum(t2, t3))
        a1, a2, a3 = jnp.exp(t1 - high), jnp.exp(t2 - high), jnp.exp(t3 - high)
        inv = 1.0 / (a1 * z1 + a2 * z2 + a3 * z3)
        f1, f2, f3 = a1 * inv, a2 * inv, a3 * inv
        delta = f1 * side(local0[0:1, h * tok : (h + 1) * tok], local1[h]) + f2 * dot2 + f3 * dot3
        stats2[0:1, lanes[h]] = f1
        stats2[1:2, lanes[h]] = delta
        terms = stack(*split(f2, 2), *split(f3, 2), *split(delta, 3))
        back.append(dot_nt(terms, spots[h]))

    def apart(value):
        zero = jnp.zeros_like(value)
        return stack(jnp.where(is2, value, zero), jnp.where(is2, zero, value)).astype(BF16)

    dsm, wm = [], []
    for h in each:
        b = back[h]
        w = e[h] * jnp.where(is2, b[0:1] + b[1:2], b[2:3] + b[3:4])
        dsm.append(apart(w * (p[h] - (b[4:5] + b[5:6] + b[6:7]))))
        wm.append(apart(w))
    dk = [dot(dsm[h], selq[:, cols[h]]) * scale for h in each]
    dv = [dot(wm[h], selg[h]) for h in each]
    for h in each:
        dkv = side(dk[h], dv[h]).astype(BF16)
        xa[:, wide[h]] = dkv[2 * n2 : 3 * n2]
        xb[:, wide[h]] = dkv[3 * n2 : 4 * n2]
        third = [dkv[tok + i * n3 : tok + (i + 1) * n3] for i in range(8)]
        xab[:, wide[h]] = stack(third[2], third[3])
        yab[:, wide[h]] = stack(third[4], third[5])
        dab[:, wide[h]] = stack(third[6], third[7])
        ngrad[:, wide[h]] = stack(dkv[:n2], third[0], dkv[n2 : 2 * n2], third[1])
        dqt[:, h * dim : h * dim + 2 * sel] = dot(keys[h].T, dsm[h]).astype(BF16)


def far_call(offsets, core, mid, value, far, tok, dim):
    levels, heads = offsets.shape
    half = heads // 2
    per = 8
    steps = half // per
    n2, n3 = tok // 4, tok // 8

    def mid_spec(a):
        return pl.BlockSpec((a.shape[0], a.shape[1] // steps), lambda i, o, c: (0, i))

    def out(rows, lanes, kind=BF16):
        return (
            pl.BlockSpec((rows, per * lanes), lambda i, o, c: (0, i)),
            jax.ShapeDtypeStruct((rows, half * lanes), kind),
        )

    outs = [out(n2, 2 * dim)] * 2 + [out(2 * n3, 2 * dim)] * 3
    outs += [out(2 * (n2 + n3), 2 * dim), out(dim, dim), out(8, 2 * tok, F32)]
    return pl.pallas_call(
        functools.partial(far_kernel, levels, per, dim),
        grid_spec=pltpu.PrefetchScalarGridSpec(
            num_scalar_prefetch=2,
            grid=(steps,),
            in_specs=[mid_spec(a) for a in mid]
            + [own_spec(tok, per * dim, steps)]
            + [mid_spec(a) for a in far],
            out_specs=[o[0] for o in outs],
        ),
        out_shape=[o[1] for o in outs],
        compiler_params=params(),
        name="far_levels",
    )(offsets, core, *mid, value, *far)


def near_kernel(
    levels, per, dim, offs_ref, core_ref, exp0, exp1, stats2, near, ngrad, dqt,
    q0, q1, k0, k1, v0, v1, g0, *refs,
):
    mine, *others = refs[-1 - PIECES :]
    g1 = side(*(ref[...] for ref in refs[: -1 - PIECES]))
    tok = q0.shape[0]
    n1 = tok // 2
    sel = tok // 4 + tok // 8
    scale = dim**-0.5
    heads = per * pl.num_programs(0)
    first = core_ref[0] * heads + pl.program_id(0) * per
    for lo in range(0, per, 4):
        each = range(lo, lo + 4)
        cols = {h: slice(h * dim, (h + 1) * dim) for h in each}
        vc = {h: slice((2 * h + 1) * dim, (2 * h + 2) * dim) for h in each}
        gra = {h: stack(g0[:, cols[h]], g1[:, cols[h]]) for h in each}
        que = {h: stack(q0[:, cols[h]], q1[:, cols[h]]) for h in each}
        wb, ds = {}, {}
        for h in each:
            lanes = slice(2 * h * tok, 2 * (h + 1) * tok)
            here = slice(h * tok, (h + 1) * tok)
            p0 = dot_nt(v0[:, cols[h]], gra[h][:tok])
            p1 = dot_nt(v1[:, cols[h]], gra[h][tok:])
            p = stack(side(p0, p1), dot_nt(near[:tok, vc[h]], gra[h]))
            w = side(exp0[:, here], exp1[:, here]).astype(F32) * stats2[0:1, lanes]
            wb[h] = w.astype(BF16)
            ds[h] = (w * (p - stats2[1:2, lanes])).astype(BF16)
        dkv1 = {
            h: side(dot(ds[h][tok:], que[h]) * scale, dot(wb[h][tok:], gra[h])).astype(BF16)
            for h in each
        }
        for block, keys in enumerate((k0, k1)):
            at = slice(block * tok, (block + 1) * tok)
            picked = slice(block * n1, (block + 1) * n1)
            grads = slice(block * sel, (block + 1) * sel)
            kv, dq = {}, {}
            for h in each:
                place = place_matrix(offs_ref, first + h, 1, levels, tok)
                wide = slice(2 * h * dim, 2 * (h + 1) * dim)
                d0, w0 = ds[h][:tok, at], wb[h][:tok, at]
                kv[h] = side(dot(d0, que[h][at]) * scale, dot(w0, gra[h][at]))
                kv[h] += dot(place, stack(dkv1[h][picked], ngrad[grads, wide]))
            for h in each:
                pick = pick_matrix(offs_ref, first + h, 2, levels, tok)
                kc = slice(2 * h * dim, (2 * h + 1) * dim)
                far = dqt[:, h * dim + block * sel : h * dim + (block + 1) * sel]
                both = stack(keys[:, cols[h]], near[:tok, kc])
                dq[h] = dot(both.T, ds[h][:, at]) + dot(far, pick)
            for h in each:
                part = per // PIECES
                ref, to = (others[h // part], h % part) if block else (mine, h)
                to *= 3 * dim
                ref[:, to : to + dim] = (dq[h] * scale).T.astype(BF16)
                ref[:, to + dim : to + 3 * dim] = kv[h].astype(BF16)


def near_call(offsets, core, mid, raw, grads, dim):
    tok, width = raw[0].shape
    levels, heads = offsets.shape
    half = heads // 2
    per = 8
    steps = half // per
    raw_spec = own_spec(tok, per * dim, steps)

    def mid_spec(a):
        return pl.BlockSpec((a.shape[0], a.shape[1] // steps), lambda i, o, c: (0, i))

    widths = [3 * per * dim] + [3 * per * dim // PIECES] * PIECES
    return pl.pallas_call(
        functools.partial(near_kernel, levels, per, dim),
        grid_spec=pltpu.PrefetchScalarGridSpec(
            num_scalar_prefetch=2,
            grid=(steps,),
            in_specs=[mid_spec(a) for a in mid] + [raw_spec] * 7
            + [mid_spec(a) for a in grads[1:]],
            out_specs=[pl.BlockSpec((tok, w), lambda i, o, c: (0, 0)) for w in widths],
        ),
        out_shape=[jax.ShapeDtypeStruct((tok, w), BF16) for w in widths],
        compiler_params=params(),
        name="near_levels",
    )(offsets, core, *mid, *raw, *grads)


def sum_kernel(here, there, first, second):
    total = (here[...].astype(F32) + there[...].astype(F32)).astype(BF16)
    rows = first.shape[0]
    first[...] = total[:rows]
    second[...] = total[rows:]


def sum_call(here, there):
    rows, cols = here.shape
    return pl.pallas_call(
        sum_kernel,
        out_shape=[jax.ShapeDtypeStruct((rows // 2, cols), BF16)] * 2,
        compiler_params=params(),
        name="add_diagonal",
    )(here, there)


def add_far(levels, dim, offs_ref, first, bases, x, third, group):
    tok = bases[0].shape[0]
    per = sum(base.shape[1] for base in bases) // (3 * dim)
    in_base = per // len(bases)
    for lo in range(0, per, group):
        each = range(lo, lo + group)
        src = {h: slice(2 * h * dim, 2 * (h + 1) * dim) for h in each}
        place = {h: place_matrix(offs_ref, first + h, 2, levels, tok) for h in each}
        more = {h: dot(place[h], stack(x[:, src[h]], third[:, src[h]])) for h in each}
        for h in each:
            base, at = bases[h // in_base], (3 * (h % in_base) + 1) * dim
            yield h, (base[:, at : at + 2 * dim].astype(F32) + more[h]).astype(BF16)


def own_kernel(levels, per, dim, offs_ref, core_ref, base, x, y, x3, dq, dk, dv):
    n3 = x3.shape[0]
    third = (x3[...].astype(F32) + y[:n3].astype(F32)).astype(BF16)
    for h in range(per):
        dq[:, h * dim : (h + 1) * dim] = base[:, 3 * h * dim : (3 * h + 1) * dim]
    for h, total in add_far(levels, dim, offs_ref, core_ref[0] * per, [base], x, third, per):
        cols = slice(h * dim, (h + 1) * dim)
        dk[:, cols] = total[:, :dim]
        dv[:, cols] = total[:, dim:]


def own_call(offsets, core, parts, dim):
    levels, heads = offsets.shape
    tok = parts[0].shape[0]
    per = heads // 2
    return pl.pallas_call(
        functools.partial(own_kernel, levels, per, dim),
        grid_spec=pltpu.PrefetchScalarGridSpec(
            num_scalar_prefetch=2,
            grid=(1,),
            in_specs=[pl.BlockSpec(a.shape, lambda i, o, c: (0, 0)) for a in parts],
            out_specs=[pl.BlockSpec((tok, per * dim), lambda i, o, c: (0, 0))] * 3,
        ),
        out_shape=[jax.ShapeDtypeStruct((tok, per * dim), BF16)] * 3,
        compiler_params=params(),
        name="add_own_half",
    )(offsets, core, *parts)


def final_kernel(
    levels, per, dim, offs_ref, core_ref, own_q, own_k, own_v, x, y, x3, *refs
):
    bases, outs, (held, sems) = refs[:PIECES], refs[PIECES : PIECES + 3], refs[-2:]
    n3 = x3.shape[0]
    copies = []

    def send(part, here, core, lo, n):
        cols = pl.ds(pl.multiple_of((core * per + lo) * dim, dim), n * dim)
        copies.append(pltpu.make_async_copy(here, outs[part].at[:, cols], sems.at[len(copies)]))
        copies[-1].start()

    for part, ref in enumerate((own_q, own_k, own_v)):
        send(part, ref, core_ref[0], 0, per)
    far_core = 1 - core_ref[0]
    each = per // PIECES
    for h in range(per):
        at = 3 * (h % each) * dim
        held[0, :, h * dim : (h + 1) * dim] = bases[h // each][:, at : at + dim]
    send(0, held.at[0], far_core, 0, per)
    third = (x3[...].astype(F32) + y[n3:].astype(F32)).astype(BF16)
    for h, total in add_far(levels, dim, offs_ref, far_core * per, bases, x, third, 4):
        cols = slice(h * dim, (h + 1) * dim)
        held[1, :, cols] = total[:, :dim]
        held[2, :, cols] = total[:, dim:]
        if (h + 1) % 4 == 0:
            for part in (1, 2):
                lo = h + 1 - 4
                send(part, held.at[part, :, pl.ds(lo * dim, 4 * dim)], far_core, lo, 4)
    for copy in copies:
        copy.wait()


def final_call(offsets, core, own, parts, dim):
    levels, heads = offsets.shape
    tok = own[0].shape[0]
    per = heads // 2
    away = pl.BlockSpec(memory_space=pl.ANY)
    return pl.pallas_call(
        functools.partial(final_kernel, levels, per, dim),
        grid_spec=pltpu.PrefetchScalarGridSpec(
            num_scalar_prefetch=2,
            grid=(1,),
            in_specs=[pl.BlockSpec(a.shape, lambda i, o, c: (0, 0)) for a in own + parts],
            out_specs=[away] * 3,
            scratch_shapes=[
                pltpu.VMEM((3, tok, per * dim), BF16),
                pltpu.SemaphoreType.DMA((4 + 2 * (per // 4),)),
            ],
        ),
        out_shape=[jax.ShapeDtypeStruct((tok, heads * dim), BF16)] * 3,
        compiler_params=params(),
        name="add_other_half",
    )(offsets, core, *own, *parts)


def per_device(queries, keys_in, values, out_grads, offsets):
    heads = offsets.shape[1]
    dim = queries.shape[2] // heads
    core = lax.rem(lax.axis_index("seq"), 2).astype(jnp.int32).reshape(1)
    q, k, v = queries[0], keys_in[0], values[0]
    sections = lax.axis_size("section")
    grads = lax.ppermute(
        out_grads[0], "section", [(i, (i - 1) % sections) for i in range(sections)]
    )
    q_oth, k_oth, v_oth = exchange(q, 1), exchange(k, 1), exchange(v, 1)
    kept = [pltpu.with_memory_space_constraint(a, pltpu.HBM) for a in (k, v)]
    two, three = pick_call(
        pltpu.with_memory_space_constraint(offsets, pltpu.HBM), core, kept, [k_oth, v_oth], dim
    )
    x3, y3, x2 = exchange(three, 2), exchange(three, 4), exchange(two, 2)
    d3 = exchange(x3, 4)
    raw = [q, q_oth, k, k_oth, v, v_oth]
    pre = pre_call(offsets, core, raw, dim)
    exp0, exp1, stats, near, selq = pre
    y3, grads = lax.optimization_barrier((y3, grads, stats))[:2]
    sel = grad_call(offsets, core, exp0, near, v, grads, dim)
    half = heads // 2
    cuts = [half * i // 3 for i in range(4)]
    sizes = [(hi - lo) * dim for lo, hi in zip(cuts, cuts[1:])]
    other = [exchange(piece, 1) for piece in pack_call(core, grads, sizes)]
    other = lax.optimization_barrier((*other, sel[1]))[:-1]
    xa, xb, xab, yab, dab, ngrad, dqt, stats2 = far_call(
        offsets, core, [stats, selq, *sel, exp1, near], v_oth,
        [two, x2, three, x3, y3, d3, *other], q.shape[0], dim,
    )
    thirds = sum_call(xab, exchange(dab, 4))
    xa, xb, y = exchange(xa, 2), exchange(xb, 3), exchange(yab, 4)
    xa3, xb3 = exchange(thirds[0], 2), exchange(thirds[1], 3)
    yy = exchange(y, 1)
    mine, *others = near_call(
        offsets, core, [exp0, exp1, stats2, near, ngrad, dqt], raw, [grads, *other], dim
    )
    last, xa, xb, xa3, xb3, y = lax.optimization_barrier((others[-1], xa, xb, xa3, xb3, y))
    bases = [exchange(piece, 1) for piece in (*others[:-1], last)]
    own = list(own_call(offsets, core, [mine, xa, y, xa3], dim))
    dq, dk, dv = final_call(offsets, core, own, [xb, yy, xb3, *bases], dim)
    return dq[None], dk[None], dv[None]


def solution(mesh):
    spec = P("section", "seq", None)
    return jax.shard_map(
        per_device,
        mesh=mesh,
        in_specs=(spec, spec, spec, spec, P()),
        out_specs=(spec, spec, spec),
        check_vma=False,
    )
```

```python
import functools

import jax
import jax.numpy as jnp
from jax import lax
from jax.experimental import pallas as pl
from jax.experimental.pallas import tpu as pltpu
from jax.sharding import PartitionSpec as P

F32 = jnp.float32
BF16 = jnp.bfloat16
NEG = -1e30
VMEM_LIMIT = 32 * 1024 * 1024
PIECES = 4


def params():
    return pltpu.CompilerParams(vmem_limit_bytes=VMEM_LIMIT)


def exchange(value, bits):
    count = lax.axis_size("seq")
    return lax.ppermute(value, "seq", [(i, i ^ bits) for i in range(count)])


def dot(a, b):
    return jnp.dot(a, b, preferred_element_type=F32)


def dot_nt(a, b):
    return lax.dot_general(a, b, (((1,), (1,)), ((), ())), preferred_element_type=F32)


def pick_matrix(offs_ref, head, first, levels, tok):
    parts = []
    for level in range(first, levels + 1):
        rate = 2**level
        rows = tok // rate
        kept = lax.rem(offs_ref[level - 1, head], rate)
        row = lax.broadcasted_iota(jnp.int32, (rows, tok), 0)
        col = lax.broadcasted_iota(jnp.int32, (rows, tok), 1)
        parts.append((col == row * rate + kept).astype(F32))
    return jnp.concatenate(parts, axis=0).astype(BF16)


def place_matrix(offs_ref, head, first, levels, tok):
    total = sum(tok // 2**level for level in range(first, levels + 1))
    col = lax.broadcasted_iota(jnp.int32, (1, total), 1)
    target, lo = jnp.zeros_like(col), 0
    for level in range(first, levels + 1):
        rate = 2**level
        kept = lax.rem(offs_ref[level - 1, head], rate)
        target = jnp.where(col >= lo, (col - lo) * rate + kept, target)
        lo += tok // rate
    row = lax.broadcasted_iota(jnp.int32, (tok, total), 0)
    return (row == target).astype(F32).astype(BF16)


def pack_kernel(core_ref, rows, *outs):
    lo = 0
    for out in outs:
        out[...] = rows[:, lo : lo + out.shape[1]]
        lo += out.shape[1]


def pack_call(core, rows, sizes):
    tok, width = rows.shape
    half = width // 2
    return pl.pallas_call(
        pack_kernel,
        grid_spec=pltpu.PrefetchScalarGridSpec(
            num_scalar_prefetch=1,
            grid=(1,),
            in_specs=[pl.BlockSpec((tok, half), lambda i, c: (0, 1 - c[0]))],
            out_specs=[pl.BlockSpec((tok, n), lambda i, c: (0, 0)) for n in sizes],
        ),
        out_shape=[jax.ShapeDtypeStruct((tok, n), BF16) for n in sizes],
        compiler_params=params(),
        name="pack_half",
    )(core, rows)


def pick_kernel(
    levels, per, dim, core_ref, offs, k0, v0, k1, v1, two_ref, three_ref, offs_ref, own_k, own_v, sems
):
    tok = k1.shape[0]
    n2, n3 = tok // 4, tok // 8
    each = range(per)
    mine = pl.ds(pl.multiple_of(core_ref[0] * per * dim, per * dim), per * dim)
    copies = [
        pltpu.make_async_copy(src.at[:, mine], dst, sems.at[i])
        for i, (src, dst) in enumerate(((k0, own_k), (v0, own_v)))
    ]
    table = pltpu.make_async_copy(offs, offs_ref, sems.at[2])
    table.start()
    for copy in copies:
        copy.start()
    table.wait()
    picks = [pick_matrix(offs_ref, core_ref[0] * per + h, 2, levels, tok) for h in each]

    def work(keys, values, lo):
        for h in each:
            cols = slice(h * dim, (h + 1) * dim)
            out = slice(2 * h * dim, 2 * (h + 1) * dim)
            got = dot(picks[h], side(keys[:, cols], values[:, cols])).astype(BF16)
            two_ref[lo * n2 : (lo + 1) * n2, out] = got[:n2]
            three_ref[lo * n3 : (lo + 1) * n3, out] = got[n2:]

    work(k1, v1, 1)
    for copy in copies:
        copy.wait()
    work(own_k, own_v, 0)


def pick_call(offsets, core, own, other, dim):
    tok, width = own[0].shape
    levels, heads = offsets.shape
    per = heads // 2
    spec = pl.BlockSpec((tok, per * dim), lambda i, c: (0, c[0]))

    def out(rows):
        return pl.BlockSpec((rows, 2 * per * dim), lambda i, c: (0, 0))

    rows = [tok // 2, tok // 4]
    return pl.pallas_call(
        functools.partial(pick_kernel, levels, per, dim),
        grid_spec=pltpu.PrefetchScalarGridSpec(
            num_scalar_prefetch=1,
            grid=(1,),
            in_specs=[pl.BlockSpec(memory_space=pl.ANY)] * 3 + [spec] * 2,
            out_specs=[out(r) for r in rows],
            scratch_shapes=[pltpu.SMEM((levels, heads), jnp.int32)]
            + [pltpu.VMEM((tok, per * dim), BF16)] * 2
            + [pltpu.SemaphoreType.DMA((3,))],
        ),
        out_shape=[jax.ShapeDtypeStruct((r, width), BF16) for r in rows],
        compiler_params=params(),
        name="pick_rows",
    )(core, offsets, *own, *other)


def own_spec(tok, cols, steps):
    return pl.BlockSpec((tok, cols), lambda i, o, c: (0, c[0] * steps + i))


def side(*values):
    return jnp.concatenate(values, axis=1)


def stack(*values):
    return jnp.concatenate(values, axis=0)


def split(value, terms):
    parts = []
    for _ in range(terms):
        part = value.astype(BF16)
        parts.append(part)
        value = value - part.astype(F32)
    return parts


def local_scores(pick, levels, offs_ref, head, key0, key1, ones, que0, que1):
    tok, dim = key0.shape
    pos = lax.broadcasted_iota(jnp.int32, (1, 2 * tok), 1)
    bias = jnp.where(lax.rem(pos, 2) == lax.rem(offs_ref[0, head], 2), 0.0, NEG).astype(F32)
    s0 = side(dot_nt(key0, que0), dot_nt(key1, que1)) * dim**-0.5
    s1 = dot_nt(ones, stack(que0, que1)) * dim**-0.5 + bias
    return stack(s0, s1)


def pre_kernel(
    levels, per, dim, offs_ref, core_ref, q0, q1, k0, k1, v0, v1, exp0, exp1, stats, near, selq
):
    tok = q0.shape[0]
    n1 = tok // 2
    heads = per * pl.num_programs(0)
    for h in range(per):
        head = core_ref[0] * heads + pl.program_id(0) * per + h
        pick = pick_matrix(offs_ref, head, 1, levels, tok)
        cols = slice(h * dim, (h + 1) * dim)
        wide = slice(2 * h * dim, 2 * (h + 1) * dim)
        lanes = slice(2 * h * tok, 2 * (h + 1) * tok)
        own = dot(pick[:n1], side(k0[:, cols], v0[:, cols])).astype(BF16)
        oth = dot(pick[:n1], side(k1[:, cols], v1[:, cols])).astype(BF16)
        ones = stack(own, oth)
        near[:, wide] = ones
        que0, que1 = q0[:, cols], q1[:, cols]
        far_pick = pick[n1:]
        selq[:, cols] = stack(dot(far_pick, que0), dot(far_pick, que1)).astype(BF16)
        s = local_scores(
            pick, levels, offs_ref, head, k0[:, cols], k1[:, cols], ones[:, :dim], que0, que1
        )
        top = jnp.max(s, axis=0, keepdims=True)
        e = jnp.exp(s - top)
        for half, ref in enumerate((exp0, exp1)):
            ref[:, h * tok : (h + 1) * tok] = e[:, half * tok : (half + 1) * tok].astype(BF16)
        stats[0:1, lanes] = top
        stats[1:2, lanes] = jnp.sum(e, axis=0, keepdims=True)


def pre_call(offsets, core, raw, dim):
    tok, width = raw[0].shape
    levels, heads = offsets.shape
    half = heads // 2
    per = 8
    steps = half // per
    raw_spec = own_spec(tok, per * dim, steps)
    sel = 2 * (tok // 4 + tok // 8)

    def out(rows, lanes, kind=BF16):
        return (
            pl.BlockSpec((rows, per * lanes), lambda i, o, c: (0, i)),
            jax.ShapeDtypeStruct((rows, half * lanes), kind),
        )

    outs = [out(2 * tok, tok), out(2 * tok, tok), out(8, 2 * tok, F32), out(tok, 2 * dim), out(sel, dim)]
    return pl.pallas_call(
        functools.partial(pre_kernel, levels, per, dim),
        grid_spec=pltpu.PrefetchScalarGridSpec(
            num_scalar_prefetch=2,
            grid=(steps,),
            in_specs=[raw_spec] * 6,
            out_specs=[o[0] for o in outs],
        ),
        out_shape=[o[1] for o in outs],
        compiler_params=params(),
        name="local_scores",
    )(offsets, core, *raw)


def local_delta(exps, values, ones, grads):
    tok = values.shape[0]
    p0, p1 = dot_nt(values, grads), dot_nt(ones, grads)
    both = exps[:tok].astype(F32) * p0 + exps[tok:].astype(F32) * p1
    return jnp.sum(both, axis=0, keepdims=True)


def grad_kernel(levels, per, dim, offs_ref, core_ref, exps, near, values, grads, selg, local):
    tok = values.shape[0]
    first = core_ref[0] * per
    each = range(per)
    cols = [slice(h * dim, (h + 1) * dim) for h in each]
    for h in each:
        pick = pick_matrix(offs_ref, first + h, 2, levels, tok)
        selg[:, cols[h]] = dot(pick, grads[:, cols[h]]).astype(BF16)
    for h in each:
        here = slice(h * tok, (h + 1) * tok)
        vc = slice((2 * h + 1) * dim, (2 * h + 2) * dim)
        local[0:1, here] = local_delta(
            exps[:, here], values[:, cols[h]], near[:, vc], grads[:, cols[h]]
        )


def grad_call(offsets, core, exps, near, values, grads, dim):
    tok, width = values.shape
    levels, heads = offsets.shape
    per = heads // 2
    raw_spec = own_spec(tok, per * dim, 1)

    def whole(a):
        return pl.BlockSpec(a.shape, lambda i, o, c: (0, 0))

    outs = [
        jax.ShapeDtypeStruct((tok // 4 + tok // 8, per * dim), BF16),
        jax.ShapeDtypeStruct((8, per * tok), F32),
    ]
    return pl.pallas_call(
        functools.partial(grad_kernel, levels, per, dim),
        grid_spec=pltpu.PrefetchScalarGridSpec(
            num_scalar_prefetch=2,
            grid=(1,),
            in_specs=[whole(exps), whole(near), raw_spec, raw_spec],
            out_specs=[whole(a) for a in outs],
        ),
        out_shape=outs,
        compiler_params=params(),
        name="own_delta",
    )(offsets, core, exps, near, values, grads)


def far_kernel(
    levels, per, dim, offs_ref, core_ref, stats, selq, selg0, local0, exp1, near, v1,
    own2, x2, own3, x3, y3, d3, *refs
):
    xa, xb, xab, yab, dab, ngrad, dqt, stats2 = refs[-8:]
    g1 = side(*(ref[...] for ref in refs[:-8]))
    tok = dqt.shape[0]
    n1, n2, n3 = tok // 2, tok // 4, tok // 8
    sel = n2 + n3
    scale = dim**-0.5
    heads = per * pl.num_programs(0)
    lane = lax.broadcasted_iota(jnp.int32, (1, 2 * sel), 1)
    is2 = lax.rem(lane, sel) < n2
    pos = lax.broadcasted_iota(jnp.int32, (1, 2 * tok), 1)
    first = core_ref[0] * heads + pl.program_id(0) * per
    each = range(per)
    cols = [slice(h * dim, (h + 1) * dim) for h in each]
    kc = [slice(2 * h * dim, (2 * h + 1) * dim) for h in each]
    vc = [slice((2 * h + 1) * dim, (2 * h + 2) * dim) for h in each]
    wide = [slice(2 * h * dim, 2 * (h + 1) * dim) for h in each]
    lanes = [slice(2 * h * tok, 2 * (h + 1) * tok) for h in each]

    def rows(c):
        return stack(*(ref[:, c] for ref in (own2, x2, own3, x3, y3, d3)))

    def level_pick(value):
        return jnp.where(is2, value[:tok], value[tok:])

    picks = [pick_matrix(offs_ref, first + h, 2, levels, tok) for h in each]
    selg = [
        stack(selg0[:, cols[h]], dot(picks[h], g1[:, cols[h]]).astype(BF16)) for h in each
    ]
    keys = [rows(kc[h]) for h in each]
    s = [level_pick(dot_nt(keys[h], selq[:, cols[h]])) * scale for h in each]
    p = [level_pick(dot_nt(rows(vc[h]), selg[h])) for h in each]
    local1 = [
        local_delta(exp1[:, h * tok : (h + 1) * tok], v1[:, cols[h]], near[:, vc[h]], g1[:, cols[h]])
        for h in each
    ]
    top = [jnp.max(a, axis=0, keepdims=True) for a in s]
    e = [jnp.exp(a - b) for a, b in zip(s, top)]
    size = [jnp.sum(a, axis=0, keepdims=True) for a in e]
    dhat = [jnp.sum(a * b, axis=0, keepdims=True) for a, b in zip(e, p)]
    none = jnp.zeros_like(picks[0])
    spots = [stack(side(a, none), side(none, a)) for a in picks]
    spread = []
    for h in each:
        terms = stack(*split(top[h], 3), *split(size[h], 2), *split(dhat[h], 3))
        zero = jnp.zeros_like(terms)
        apart = stack(jnp.where(is2, terms, zero), jnp.where(is2, zero, terms))
        spread.append(dot(apart, spots[h]))
    back = []
    for h in each:

        def level_stats(level, lo):
            rate = 2**level
            on = lax.rem(pos, rate) == lax.rem(offs_ref[level - 1, first + h], rate)
            t = [spread[h][lo + i : lo + i + 1] for i in range(8)]
            return jnp.where(on, t[0] + t[1] + t[2], NEG), t[3] + t[4], t[5] + t[6] + t[7]

        t1, z1 = stats[0:1, lanes[h]], stats[1:2, lanes[h]]
        t2, z2, dot2 = level_stats(2, 0)
        t3, z3, dot3 = level_stats(3, 8)
        high = jnp.maximum(t1, jnp.maximum(t2, t3))
        a1, a2, a3 = jnp.exp(t1 - high), jnp.exp(t2 - high), jnp.exp(t3 - high)
        inv = 1.0 / (a1 * z1 + a2 * z2 + a3 * z3)
        f1, f2, f3 = a1 * inv, a2 * inv, a3 * inv
        delta = f1 * side(local0[0:1, h * tok : (h + 1) * tok], local1[h]) + f2 * dot2 + f3 * dot3
        stats2[0:1, lanes[h]] = f1
        stats2[1:2, lanes[h]] = delta
        terms = stack(*split(f2, 2), *split(f3, 2), *split(delta, 3))
        back.append(dot_nt(terms, spots[h]))

    def apart(value):
        zero = jnp.zeros_like(value)
        return stack(jnp.where(is2, value, zero), jnp.where(is2, zero, value)).astype(BF16)

    dsm, wm = [], []
    for h in each:
        b = back[h]
        w = e[h] * jnp.where(is2, b[0:1] + b[1:2], b[2:3] + b[3:4])
        dsm.append(apart(w * (p[h] - (b[4:5] + b[5:6] + b[6:7]))))
        wm.append(apart(w))
    dk = [dot(dsm[h], selq[:, cols[h]]) * scale for h in each]
    dv = [dot(wm[h], selg[h]) for h in each]
    for h in each:
        dkv = side(dk[h], dv[h]).astype(BF16)
        xa[:, wide[h]] = dkv[2 * n2 : 3 * n2]
        xb[:, wide[h]] = dkv[3 * n2 : 4 * n2]
        third = [dkv[tok + i * n3 : tok + (i + 1) * n3] for i in range(8)]
        xab[:, wide[h]] = stack(third[2], third[3])
        yab[:, wide[h]] = stack(third[4], third[5])
        dab[:, wide[h]] = stack(third[6], third[7])
        ngrad[:, wide[h]] = stack(dkv[:n2], third[0], dkv[n2 : 2 * n2], third[1])
        dqt[:, h * dim : h * dim + 2 * sel] = dot(keys[h].T, dsm[h]).astype(BF16)


def far_call(offsets, core, mid, value, far, tok, dim):
    levels, heads = offsets.shape
    half = heads // 2
    per = 8
    steps = half // per
    n2, n3 = tok // 4, tok // 8

    def mid_spec(a):
        return pl.BlockSpec((a.shape[0], a.shape[1] // steps), lambda i, o, c: (0, i))

    def out(rows, lanes, kind=BF16):
        return (
            pl.BlockSpec((rows, per * lanes), lambda i, o, c: (0, i)),
            jax.ShapeDtypeStruct((rows, half * lanes), kind),
        )

    outs = [out(n2, 2 * dim)] * 2 + [out(2 * n3, 2 * dim)] * 3
    outs += [out(2 * (n2 + n3), 2 * dim), out(dim, dim), out(8, 2 * tok, F32)]
    return pl.pallas_call(
        functools.partial(far_kernel, levels, per, dim),
        grid_spec=pltpu.PrefetchScalarGridSpec(
            num_scalar_prefetch=2,
            grid=(steps,),
            in_specs=[mid_spec(a) for a in mid]
            + [own_spec(tok, per * dim, steps)]
            + [mid_spec(a) for a in far],
            out_specs=[o[0] for o in outs],
        ),
        out_shape=[o[1] for o in outs],
        compiler_params=params(),
        name="far_levels",
    )(offsets, core, *mid, value, *far)


def near_kernel(
    levels, per, dim, offs_ref, core_ref, exp0, exp1, stats2, near, ngrad, dqt,
    q0, q1, k0, k1, v0, v1, g0, *refs,
):
    mine, *others = refs[-1 - PIECES :]
    g1 = side(*(ref[...] for ref in refs[: -1 - PIECES]))
    tok = q0.shape[0]
    n1 = tok // 2
    sel = tok // 4 + tok // 8
    scale = dim**-0.5
    heads = per * pl.num_programs(0)
    first = core_ref[0] * heads + pl.program_id(0) * per
    for lo in range(0, per, 4):
        each = range(lo, lo + 4)
        cols = {h: slice(h * dim, (h + 1) * dim) for h in each}
        vc = {h: slice((2 * h + 1) * dim, (2 * h + 2) * dim) for h in each}
        gra = {h: stack(g0[:, cols[h]], g1[:, cols[h]]) for h in each}
        que = {h: stack(q0[:, cols[h]], q1[:, cols[h]]) for h in each}
        wb, ds = {}, {}
        for h in each:
            lanes = slice(2 * h * tok, 2 * (h + 1) * tok)
            here = slice(h * tok, (h + 1) * tok)
            p0 = dot_nt(v0[:, cols[h]], gra[h][:tok])
            p1 = dot_nt(v1[:, cols[h]], gra[h][tok:])
            p = stack(side(p0, p1), dot_nt(near[:tok, vc[h]], gra[h]))
            w = side(exp0[:, here], exp1[:, here]).astype(F32) * stats2[0:1, lanes]
            wb[h] = w.astype(BF16)
            ds[h] = (w * (p - stats2[1:2, lanes])).astype(BF16)
        dkv1 = {
            h: side(dot(ds[h][tok:], que[h]) * scale, dot(wb[h][tok:], gra[h])).astype(BF16)
            for h in each
        }
        for block, keys in enumerate((k0, k1)):
            at = slice(block * tok, (block + 1) * tok)
            picked = slice(block * n1, (block + 1) * n1)
            grads = slice(block * sel, (block + 1) * sel)
            kv, dq = {}, {}
            for h in each:
                place = place_matrix(offs_ref, first + h, 1, levels, tok)
                wide = slice(2 * h * dim, 2 * (h + 1) * dim)
                d0, w0 = ds[h][:tok, at], wb[h][:tok, at]
                kv[h] = side(dot(d0, que[h][at]) * scale, dot(w0, gra[h][at]))
                kv[h] += dot(place, stack(dkv1[h][picked], ngrad[grads, wide]))
            for h in each:
                pick = pick_matrix(offs_ref, first + h, 2, levels, tok)
                kc = slice(2 * h * dim, (2 * h + 1) * dim)
                far = dqt[:, h * dim + block * sel : h * dim + (block + 1) * sel]
                both = stack(keys[:, cols[h]], near[:tok, kc])
                dq[h] = dot(both.T, ds[h][:, at]) + dot(far, pick)
            for h in each:
                part = per // PIECES
                ref, to = (others[h // part], h % part) if block else (mine, h)
                to *= 3 * dim
                ref[:, to : to + dim] = (dq[h] * scale).T.astype(BF16)
                ref[:, to + dim : to + 3 * dim] = kv[h].astype(BF16)


def near_call(offsets, core, mid, raw, grads, dim):
    tok, width = raw[0].shape
    levels, heads = offsets.shape
    half = heads // 2
    per = 8
    steps = half // per
    raw_spec = own_spec(tok, per * dim, steps)

    def mid_spec(a):
        return pl.BlockSpec((a.shape[0], a.shape[1] // steps), lambda i, o, c: (0, i))

    widths = [3 * per * dim] + [3 * per * dim // PIECES] * PIECES
    return pl.pallas_call(
        functools.partial(near_kernel, levels, per, dim),
        grid_spec=pltpu.PrefetchScalarGridSpec(
            num_scalar_prefetch=2,
            grid=(steps,),
            in_specs=[mid_spec(a) for a in mid] + [raw_spec] * 7
            + [mid_spec(a) for a in grads[1:]],
            out_specs=[pl.BlockSpec((tok, w), lambda i, o, c: (0, 0)) for w in widths],
        ),
        out_shape=[jax.ShapeDtypeStruct((tok, w), BF16) for w in widths],
        compiler_params=params(),
        name="near_levels",
    )(offsets, core, *mid, *raw, *grads)


def sum_kernel(here, there, first, second):
    total = (here[...].astype(F32) + there[...].astype(F32)).astype(BF16)
    rows = first.shape[0]
    first[...] = total[:rows]
    second[...] = total[rows:]


def sum_call(here, there):
    rows, cols = here.shape
    return pl.pallas_call(
        sum_kernel,
        out_shape=[jax.ShapeDtypeStruct((rows // 2, cols), BF16)] * 2,
        compiler_params=params(),
        name="add_diagonal",
    )(here, there)


def add_far(levels, dim, offs_ref, first, bases, x, third, group):
    tok = bases[0].shape[0]
    per = sum(base.shape[1] for base in bases) // (3 * dim)
    in_base = per // len(bases)
    for lo in range(0, per, group):
        each = range(lo, lo + group)
        src = {h: slice(2 * h * dim, 2 * (h + 1) * dim) for h in each}
        place = {h: place_matrix(offs_ref, first + h, 2, levels, tok) for h in each}
        more = {h: dot(place[h], stack(x[:, src[h]], third[:, src[h]])) for h in each}
        for h in each:
            base, at = bases[h // in_base], (3 * (h % in_base) + 1) * dim
            yield h, (base[:, at : at + 2 * dim].astype(F32) + more[h]).astype(BF16)


def own_kernel(levels, per, dim, offs_ref, core_ref, base, x, y, x3, dq, dk, dv):
    n3 = x3.shape[0]
    third = (x3[...].astype(F32) + y[:n3].astype(F32)).astype(BF16)
    for h in range(per):
        dq[:, h * dim : (h + 1) * dim] = base[:, 3 * h * dim : (3 * h + 1) * dim]
    for h, total in add_far(levels, dim, offs_ref, core_ref[0] * per, [base], x, third, per):
        cols = slice(h * dim, (h + 1) * dim)
        dk[:, cols] = total[:, :dim]
        dv[:, cols] = total[:, dim:]


def own_call(offsets, core, parts, dim):
    levels, heads = offsets.shape
    tok = parts[0].shape[0]
    per = heads // 2
    return pl.pallas_call(
        functools.partial(own_kernel, levels, per, dim),
        grid_spec=pltpu.PrefetchScalarGridSpec(
            num_scalar_prefetch=2,
            grid=(1,),
            in_specs=[pl.BlockSpec(a.shape, lambda i, o, c: (0, 0)) for a in parts],
            out_specs=[pl.BlockSpec((tok, per * dim), lambda i, o, c: (0, 0))] * 3,
        ),
        out_shape=[jax.ShapeDtypeStruct((tok, per * dim), BF16)] * 3,
        compiler_params=params(),
        name="add_own_half",
    )(offsets, core, *parts)


def final_kernel(
    levels, per, dim, offs_ref, core_ref, own_q, own_k, own_v, x, y, x3, *refs
):
    bases, outs, (held, sems) = refs[:PIECES], refs[PIECES : PIECES + 3], refs[-2:]
    n3 = x3.shape[0]
    copies = []

    def send(part, here, core, lo, n):
        cols = pl.ds(pl.multiple_of((core * per + lo) * dim, dim), n * dim)
        copies.append(pltpu.make_async_copy(here, outs[part].at[:, cols], sems.at[len(copies)]))
        copies[-1].start()

    for part, ref in enumerate((own_q, own_k, own_v)):
        send(part, ref, core_ref[0], 0, per)
    far_core = 1 - core_ref[0]
    each = per // PIECES
    for h in range(per):
        at = 3 * (h % each) * dim
        held[0, :, h * dim : (h + 1) * dim] = bases[h // each][:, at : at + dim]
    send(0, held.at[0], far_core, 0, per)
    third = (x3[...].astype(F32) + y[n3:].astype(F32)).astype(BF16)
    for h, total in add_far(levels, dim, offs_ref, far_core * per, bases, x, third, 4):
        cols = slice(h * dim, (h + 1) * dim)
        held[1, :, cols] = total[:, :dim]
        held[2, :, cols] = total[:, dim:]
        if (h + 1) % 4 == 0:
            for part in (1, 2):
                lo = h + 1 - 4
                send(part, held.at[part, :, pl.ds(lo * dim, 4 * dim)], far_core, lo, 4)
    for copy in copies:
        copy.wait()


def final_call(offsets, core, own, parts, dim):
    levels, heads = offsets.shape
    tok = own[0].shape[0]
    per = heads // 2
    away = pl.BlockSpec(memory_space=pl.ANY)
    return pl.pallas_call(
        functools.partial(final_kernel, levels, per, dim),
        grid_spec=pltpu.PrefetchScalarGridSpec(
            num_scalar_prefetch=2,
            grid=(1,),
            in_specs=[pl.BlockSpec(a.shape, lambda i, o, c: (0, 0)) for a in own + parts],
            out_specs=[away] * 3,
            scratch_shapes=[
                pltpu.VMEM((3, tok, per * dim), BF16),
                pltpu.SemaphoreType.DMA((4 + 2 * (per // 4),)),
            ],
        ),
        out_shape=[jax.ShapeDtypeStruct((tok, heads * dim), BF16)] * 3,
        compiler_params=params(),
        name="add_other_half",
    )(offsets, core, *own, *parts)


def per_device(queries, keys_in, values, out_grads, offsets):
    heads = offsets.shape[1]
    dim = queries.shape[2] // heads
    core = lax.rem(lax.axis_index("seq"), 2).astype(jnp.int32).reshape(1)
    q, k, v = queries[0], keys_in[0], values[0]
    sections = lax.axis_size("section")
    grads = lax.ppermute(
        out_grads[0], "section", [(i, (i - 1) % sections) for i in range(sections)]
    )
    q_oth, k_oth, v_oth = exchange(q, 1), exchange(k, 1), exchange(v, 1)
    kept = [pltpu.with_memory_space_constraint(a, pltpu.HBM) for a in (k, v)]
    two, three = pick_call(
        pltpu.with_memory_space_constraint(offsets, pltpu.HBM), core, kept, [k_oth, v_oth], dim
    )
    x3, y3, x2 = exchange(three, 2), exchange(three, 4), exchange(two, 2)
    d3 = exchange(x3, 4)
    raw = [q, q_oth, k, k_oth, v, v_oth]
    pre = pre_call(offsets, core, raw, dim)
    exp0, exp1, stats, near, selq = pre
    y3, grads = lax.optimization_barrier((y3, grads, stats))[:2]
    sel = grad_call(offsets, core, exp0, near, v, grads, dim)
    half = heads // 2
    cuts = [half * i // 3 for i in range(4)]
    sizes = [(hi - lo) * dim for lo, hi in zip(cuts, cuts[1:])]
    other = [exchange(piece, 1) for piece in pack_call(core, grads, sizes)]
    other = lax.optimization_barrier((*other, sel[1]))[:-1]
    xa, xb, xab, yab, dab, ngrad, dqt, stats2 = far_call(
        offsets, core, [stats, selq, *sel, exp1, near], v_oth,
        [two, x2, three, x3, y3, d3, *other], q.shape[0], dim,
    )
    thirds = sum_call(xab, exchange(dab, 4))
    xa, xb, y = exchange(xa, 2), exchange(xb, 3), exchange(yab, 4)
    xa3, xb3 = exchange(thirds[0], 2), exchange(thirds[1], 3)
    yy = exchange(y, 1)
    mine, *others = near_call(
        offsets, core, [exp0, exp1, stats2, near, ngrad, dqt], raw, [grads, *other], dim
    )
    last, xa, xb, xa3, xb3, y = lax.optimization_barrier((others[-1], xa, xb, xa3, xb3, y))
    bases = [exchange(piece, 1) for piece in (*others[:-1], last)]
    own = list(own_call(offsets, core, [mine, xa, y, xa3], dim))
    dq, dk, dv = final_call(offsets, core, own, [xb, yy, xb3, *bases], dim)
    return dq[None], dk[None], dv[None]


def solution(mesh):
    spec = P("section", "seq", None)
    return jax.shard_map(
        per_device,
        mesh=mesh,
        in_specs=(spec, spec, spec, spec, P()),
        out_specs=(spec, spec, spec),
        check_vma=False,
    )
```

```python
import functools

import jax
import jax.numpy as jnp
from jax import lax
from jax.experimental import pallas as pl
from jax.experimental.pallas import tpu as pltpu
from jax.sharding import PartitionSpec as P

F32 = jnp.float32
BF16 = jnp.bfloat16
NEG = -1e30
VMEM_LIMIT = 32 * 1024 * 1024
PIECES = 4


def params():
    return pltpu.CompilerParams(vmem_limit_bytes=VMEM_LIMIT)


def exchange(value, bits):
    count = lax.axis_size("seq")
    return lax.ppermute(value, "seq", [(i, i ^ bits) for i in range(count)])


def dot(a, b):
    return jnp.dot(a, b, preferred_element_type=F32)


def dot_nt(a, b):
    return lax.dot_general(a, b, (((1,), (1,)), ((), ())), preferred_element_type=F32)


def pick_matrix(offs_ref, head, first, levels, tok):
    parts = []
    for level in range(first, levels + 1):
        rate = 2**level
        rows = tok // rate
        kept = lax.rem(offs_ref[level - 1, head], rate)
        row = lax.broadcasted_iota(jnp.int32, (rows, tok), 0)
        col = lax.broadcasted_iota(jnp.int32, (rows, tok), 1)
        parts.append((col == row * rate + kept).astype(F32))
    return jnp.concatenate(parts, axis=0).astype(BF16)


def place_matrix(offs_ref, head, first, levels, tok):
    total = sum(tok // 2**level for level in range(first, levels + 1))
    col = lax.broadcasted_iota(jnp.int32, (1, total), 1)
    target, lo = jnp.zeros_like(col), 0
    for level in range(first, levels + 1):
        rate = 2**level
        kept = lax.rem(offs_ref[level - 1, head], rate)
        target = jnp.where(col >= lo, (col - lo) * rate + kept, target)
        lo += tok // rate
    row = lax.broadcasted_iota(jnp.int32, (tok, total), 0)
    return (row == target).astype(F32).astype(BF16)


def pack_kernel(core_ref, rows, *outs):
    lo = 0
    for out in outs:
        out[...] = rows[:, lo : lo + out.shape[1]]
        lo += out.shape[1]


def pack_call(core, rows, sizes):
    tok, width = rows.shape
    half = width // 2
    return pl.pallas_call(
        pack_kernel,
        grid_spec=pltpu.PrefetchScalarGridSpec(
            num_scalar_prefetch=1,
            grid=(1,),
            in_specs=[pl.BlockSpec((tok, half), lambda i, c: (0, 1 - c[0]))],
            out_specs=[pl.BlockSpec((tok, n), lambda i, c: (0, 0)) for n in sizes],
        ),
        out_shape=[jax.ShapeDtypeStruct((tok, n), BF16) for n in sizes],
        compiler_params=params(),
        name="pack_half",
    )(core, rows)


def pick_kernel(
    levels, per, dim, core_ref, offs, k0, v0, k1, v1, two_ref, three_ref, offs_ref, own_k, own_v, sems
):
    tok = k1.shape[0]
    n2, n3 = tok // 4, tok // 8
    each = range(per)
    mine = pl.ds(pl.multiple_of(core_ref[0] * per * dim, per * dim), per * dim)
    copies = [
        pltpu.make_async_copy(src.at[:, mine], dst, sems.at[i])
        for i, (src, dst) in enumerate(((k0, own_k), (v0, own_v)))
    ]
    table = pltpu.make_async_copy(offs, offs_ref, sems.at[2])
    table.start()
    for copy in copies:
        copy.start()
    table.wait()
    picks = [pick_matrix(offs_ref, core_ref[0] * per + h, 2, levels, tok) for h in each]

    def work(keys, values, lo):
        for h in each:
            cols = slice(h * dim, (h + 1) * dim)
            out = slice(2 * h * dim, 2 * (h + 1) * dim)
            got = dot(picks[h], side(keys[:, cols], values[:, cols])).astype(BF16)
            two_ref[lo * n2 : (lo + 1) * n2, out] = got[:n2]
            three_ref[lo * n3 : (lo + 1) * n3, out] = got[n2:]

    work(k1, v1, 1)
    for copy in copies:
        copy.wait()
    work(own_k, own_v, 0)


def pick_call(offsets, core, own, other, dim):
    tok, width = own[0].shape
    levels, heads = offsets.shape
    per = heads // 2
    spec = pl.BlockSpec((tok, per * dim), lambda i, c: (0, c[0]))

    def out(rows):
        return pl.BlockSpec((rows, 2 * per * dim), lambda i, c: (0, 0))

    rows = [tok // 2, tok // 4]
    return pl.pallas_call(
        functools.partial(pick_kernel, levels, per, dim),
        grid_spec=pltpu.PrefetchScalarGridSpec(
            num_scalar_prefetch=1,
            grid=(1,),
            in_specs=[pl.BlockSpec(memory_space=pl.ANY)] * 3 + [spec] * 2,
            out_specs=[out(r) for r in rows],
            scratch_shapes=[pltpu.SMEM((levels, heads), jnp.int32)]
            + [pltpu.VMEM((tok, per * dim), BF16)] * 2
            + [pltpu.SemaphoreType.DMA((3,))],
        ),
        out_shape=[jax.ShapeDtypeStruct((r, width), BF16) for r in rows],
        compiler_params=params(),
        name="pick_rows",
    )(core, offsets, *own, *other)


def own_spec(tok, cols, steps):
    return pl.BlockSpec((tok, cols), lambda i, o, c: (0, c[0] * steps + i))


def side(*values):
    return jnp.concatenate(values, axis=1)


def stack(*values):
    return jnp.concatenate(values, axis=0)


def split(value, terms):
    parts = []
    for _ in range(terms):
        part = value.astype(BF16)
        parts.append(part)
        value = value - part.astype(F32)
    return parts


def local_scores(pick, levels, offs_ref, head, key0, key1, ones, que0, que1):
    tok, dim = key0.shape
    pos = lax.broadcasted_iota(jnp.int32, (1, 2 * tok), 1)
    bias = jnp.where(lax.rem(pos, 2) == lax.rem(offs_ref[0, head], 2), 0.0, NEG).astype(F32)
    s0 = side(dot_nt(key0, que0), dot_nt(key1, que1)) * dim**-0.5
    s1 = dot_nt(ones, stack(que0, que1)) * dim**-0.5 + bias
    return stack(s0, s1)


def pre_kernel(
    levels, per, dim, offs_ref, core_ref, q0, q1, k0, k1, v0, v1, exp0, exp1, stats, near, selq
):
    tok = q0.shape[0]
    n1 = tok // 2
    heads = per * pl.num_programs(0)
    for h in range(per):
        head = core_ref[0] * heads + pl.program_id(0) * per + h
        pick = pick_matrix(offs_ref, head, 1, levels, tok)
        cols = slice(h * dim, (h + 1) * dim)
        wide = slice(2 * h * dim, 2 * (h + 1) * dim)
        lanes = slice(2 * h * tok, 2 * (h + 1) * tok)
        own = dot(pick[:n1], side(k0[:, cols], v0[:, cols])).astype(BF16)
        oth = dot(pick[:n1], side(k1[:, cols], v1[:, cols])).astype(BF16)
        ones = stack(own, oth)
        near[:, wide] = ones
        que0, que1 = q0[:, cols], q1[:, cols]
        far_pick = pick[n1:]
        selq[:, cols] = stack(dot(far_pick, que0), dot(far_pick, que1)).astype(BF16)
        s = local_scores(
            pick, levels, offs_ref, head, k0[:, cols], k1[:, cols], ones[:, :dim], que0, que1
        )
        top = jnp.max(s, axis=0, keepdims=True)
        e = jnp.exp(s - top)
        for half, ref in enumerate((exp0, exp1)):
            ref[:, h * tok : (h + 1) * tok] = e[:, half * tok : (half + 1) * tok].astype(BF16)
        stats[0:1, lanes] = top
        stats[1:2, lanes] = jnp.sum(e, axis=0, keepdims=True)


def pre_call(offsets, core, raw, dim):
    tok, width = raw[0].shape
    levels, heads = offsets.shape
    half = heads // 2
    per = 8
    steps = half // per
    raw_spec = own_spec(tok, per * dim, steps)
    sel = 2 * (tok // 4 + tok // 8)

    def out(rows, lanes, kind=BF16):
        return (
            pl.BlockSpec((rows, per * lanes), lambda i, o, c: (0, i)),
            jax.ShapeDtypeStruct((rows, half * lanes), kind),
        )

    outs = [out(2 * tok, tok), out(2 * tok, tok), out(8, 2 * tok, F32), out(tok, 2 * dim), out(sel, dim)]
    return pl.pallas_call(
        functools.partial(pre_kernel, levels, per, dim),
        grid_spec=pltpu.PrefetchScalarGridSpec(
            num_scalar_prefetch=2,
            grid=(steps,),
            in_specs=[raw_spec] * 6,
            out_specs=[o[0] for o in outs],
        ),
        out_shape=[o[1] for o in outs],
        compiler_params=params(),
        name="local_scores",
    )(offsets, core, *raw)


def local_delta(exps, values, ones, grads):
    tok = values.shape[0]
    p0, p1 = dot_nt(values, grads), dot_nt(ones, grads)
    both = exps[:tok].astype(F32) * p0 + exps[tok:].astype(F32) * p1
    return jnp.sum(both, axis=0, keepdims=True)


def grad_kernel(levels, per, dim, offs_ref, core_ref, exps, near, values, grads, selg, local):
    tok = values.shape[0]
    first = core_ref[0] * per
    each = range(per)
    cols = [slice(h * dim, (h + 1) * dim) for h in each]
    picks = [pick_matrix(offs_ref, first + h, 2, levels, tok) for h in each]
    rows = [dot(picks[h], grads[:, cols[h]]).astype(BF16) for h in each]
    vc = [slice((2 * h + 1) * dim, (2 * h + 2) * dim) for h in each]
    p0 = [dot_nt(values[:, cols[h]], grads[:, cols[h]]) for h in each]
    p1 = [dot_nt(near[:, vc[h]], grads[:, cols[h]]) for h in each]
    for h in each:
        here = slice(h * tok, (h + 1) * tok)
        selg[:, cols[h]] = rows[h]
        both = exps[:tok, here].astype(F32) * p0[h] + exps[tok:, here].astype(F32) * p1[h]
        local[0:1, here] = jnp.sum(both, axis=0, keepdims=True)


def grad_call(offsets, core, exps, near, values, grads, dim):
    tok, width = values.shape
    levels, heads = offsets.shape
    per = heads // 2
    raw_spec = own_spec(tok, per * dim, 1)

    def whole(a):
        return pl.BlockSpec(a.shape, lambda i, o, c: (0, 0))

    outs = [
        jax.ShapeDtypeStruct((tok // 4 + tok // 8, per * dim), BF16),
        jax.ShapeDtypeStruct((8, per * tok), F32),
    ]
    return pl.pallas_call(
        functools.partial(grad_kernel, levels, per, dim),
        grid_spec=pltpu.PrefetchScalarGridSpec(
            num_scalar_prefetch=2,
            grid=(1,),
            in_specs=[whole(exps), whole(near), raw_spec, raw_spec],
            out_specs=[whole(a) for a in outs],
        ),
        out_shape=outs,
        compiler_params=params(),
        name="own_delta",
    )(offsets, core, exps, near, values, grads)


def far_kernel(
    levels, per, dim, offs_ref, core_ref, stats, selq, selg0, local0, exp1, near, v1,
    own2, x2, own3, x3, y3, d3, *refs
):
    xa, xb, xab, yab, dab, dsms, wms, selg1, stats2 = refs[-9:]
    g1 = side(*(ref[...] for ref in refs[:-9]))
    tok = g1.shape[0]
    n1, n2, n3 = tok // 2, tok // 4, tok // 8
    sel = n2 + n3
    scale = dim**-0.5
    heads = per * pl.num_programs(0)
    lane = lax.broadcasted_iota(jnp.int32, (1, 2 * sel), 1)
    is2 = lax.rem(lane, sel) < n2
    pos = lax.broadcasted_iota(jnp.int32, (1, 2 * tok), 1)
    first = core_ref[0] * heads + pl.program_id(0) * per
    each = range(per)
    cols = [slice(h * dim, (h + 1) * dim) for h in each]
    kc = [slice(2 * h * dim, (2 * h + 1) * dim) for h in each]
    vc = [slice((2 * h + 1) * dim, (2 * h + 2) * dim) for h in each]
    wide = [slice(2 * h * dim, 2 * (h + 1) * dim) for h in each]
    lanes = [slice(2 * h * tok, 2 * (h + 1) * tok) for h in each]

    def rows(c):
        return stack(*(ref[:, c] for ref in (own2, x2, own3, x3, y3, d3)))

    def level_pick(value):
        return jnp.where(is2, value[:tok], value[tok:])

    picks = [pick_matrix(offs_ref, first + h, 2, levels, tok) for h in each]
    selg = [
        stack(selg0[:, cols[h]], dot(picks[h], g1[:, cols[h]]).astype(BF16)) for h in each
    ]
    keys = [rows(kc[h]) for h in each]
    s = [level_pick(dot_nt(keys[h], selq[:, cols[h]])) * scale for h in each]
    p = [level_pick(dot_nt(rows(vc[h]), selg[h])) for h in each]
    local1 = [
        local_delta(exp1[:, h * tok : (h + 1) * tok], v1[:, cols[h]], near[:, vc[h]], g1[:, cols[h]])
        for h in each
    ]
    top = [jnp.max(a, axis=0, keepdims=True) for a in s]
    e = [jnp.exp(a - b) for a, b in zip(s, top)]
    size = [jnp.sum(a, axis=0, keepdims=True) for a in e]
    dhat = [jnp.sum(a * b, axis=0, keepdims=True) for a, b in zip(e, p)]
    none = jnp.zeros_like(picks[0])
    spots = [stack(side(a, none), side(none, a)) for a in picks]
    spread = []
    for h in each:
        terms = stack(*split(top[h], 3), *split(size[h], 2), *split(dhat[h], 3))
        zero = jnp.zeros_like(terms)
        apart = stack(jnp.where(is2, terms, zero), jnp.where(is2, zero, terms))
        spread.append(dot(apart, spots[h]))
    back = []
    for h in each:

        def level_stats(level, lo):
            rate = 2**level
            on = lax.rem(pos, rate) == lax.rem(offs_ref[level - 1, first + h], rate)
            t = [spread[h][lo + i : lo + i + 1] for i in range(8)]
            return jnp.where(on, t[0] + t[1] + t[2], NEG), t[3] + t[4], t[5] + t[6] + t[7]

        t1, z1 = stats[0:1, lanes[h]], stats[1:2, lanes[h]]
        t2, z2, dot2 = level_stats(2, 0)
        t3, z3, dot3 = level_stats(3, 8)
        high = jnp.maximum(t1, jnp.maximum(t2, t3))
        a1, a2, a3 = jnp.exp(t1 - high), jnp.exp(t2 - high), jnp.exp(t3 - high)
        inv = 1.0 / (a1 * z1 + a2 * z2 + a3 * z3)
        f1, f2, f3 = a1 * inv, a2 * inv, a3 * inv
        delta = f1 * side(local0[0:1, h * tok : (h + 1) * tok], local1[h]) + f2 * dot2 + f3 * dot3
        stats2[0:1, lanes[h]] = f1
        stats2[1:2, lanes[h]] = delta
        terms = stack(*split(f2, 2), *split(f3, 2), *split(delta, 3))
        back.append(dot_nt(terms, spots[h]))

    def apart(value):
        zero = jnp.zeros_like(value)
        return stack(jnp.where(is2, value, zero), jnp.where(is2, zero, value)).astype(BF16)

    dsm, wm = [], []
    for h in each:
        b = back[h]
        w = e[h] * jnp.where(is2, b[0:1] + b[1:2], b[2:3] + b[3:4])
        dsm.append(apart(w * (p[h] - (b[4:5] + b[5:6] + b[6:7]))))
        wm.append(apart(w))
    def away(value):
        return stack(value[2 * n2 : tok], value[tok + 2 * n3 :])

    dk = [dot(away(dsm[h]), selq[:, cols[h]]) * scale for h in each]
    dv = [dot(away(wm[h]), selg[h]) for h in each]
    for h in each:
        dkv = side(dk[h], dv[h]).astype(BF16)
        xa[:, wide[h]] = dkv[:n2]
        xb[:, wide[h]] = dkv[n2 : 2 * n2]
        for i, ref in enumerate((xab, yab, dab)):
            lo = 2 * n2 + 2 * i * n3
            ref[:, wide[h]] = dkv[lo : lo + 2 * n3]
        dsms[:, h * dim : h * dim + 2 * sel] = dsm[h]
        wms[:, h * dim : h * dim + 2 * sel] = wm[h]
        selg1[:, cols[h]] = selg[h][sel:]


def far_call(offsets, core, mid, value, far, tok, dim):
    levels, heads = offsets.shape
    half = heads // 2
    per = 8
    steps = half // per
    n2, n3 = tok // 4, tok // 8

    def mid_spec(a):
        return pl.BlockSpec((a.shape[0], a.shape[1] // steps), lambda i, o, c: (0, i))

    def out(rows, lanes, kind=BF16):
        return (
            pl.BlockSpec((rows, per * lanes), lambda i, o, c: (0, i)),
            jax.ShapeDtypeStruct((rows, half * lanes), kind),
        )

    outs = [out(n2, 2 * dim)] * 2 + [out(2 * n3, 2 * dim)] * 3
    outs += [out(2 * tok, dim)] * 2 + [out(n2 + n3, dim), out(8, 2 * tok, F32)]
    return pl.pallas_call(
        functools.partial(far_kernel, levels, per, dim),
        grid_spec=pltpu.PrefetchScalarGridSpec(
            num_scalar_prefetch=2,
            grid=(steps,),
            in_specs=[mid_spec(a) for a in mid]
            + [own_spec(tok, per * dim, steps)]
            + [mid_spec(a) for a in far],
            out_specs=[o[0] for o in outs],
        ),
        out_shape=[o[1] for o in outs],
        compiler_params=params(),
        name="far_levels",
    )(offsets, core, *mid, value, *far)


def near_kernel(
    levels, per, dim, offs_ref, core_ref, exp0, exp1, stats2, near, dsms, wms, selq, selg0, selg1,
    own2, x2, own3, x3, y3, d3,
    q0, q1, k0, k1, v0, v1, g0, *refs,
):
    mine, *others = refs[-1 - PIECES :]
    g1 = side(*(ref[...] for ref in refs[: -1 - PIECES]))
    tok = q0.shape[0]
    n1 = tok // 2
    n2, n3 = tok // 4, tok // 8
    sel = n2 + n3
    scale = dim**-0.5
    heads = per * pl.num_programs(0)
    first = core_ref[0] * heads + pl.program_id(0) * per
    for lo in range(0, per, 4):
        each = range(lo, lo + 4)
        cols = {h: slice(h * dim, (h + 1) * dim) for h in each}
        vc = {h: slice((2 * h + 1) * dim, (2 * h + 2) * dim) for h in each}
        gra = {h: stack(g0[:, cols[h]], g1[:, cols[h]]) for h in each}
        que = {h: stack(q0[:, cols[h]], q1[:, cols[h]]) for h in each}
        wb, ds = {}, {}
        for h in each:
            lanes = slice(2 * h * tok, 2 * (h + 1) * tok)
            here = slice(h * tok, (h + 1) * tok)
            p0 = dot_nt(v0[:, cols[h]], gra[h][:tok])
            p1 = dot_nt(v1[:, cols[h]], gra[h][tok:])
            p = stack(side(p0, p1), dot_nt(near[:tok, vc[h]], gra[h]))
            w = side(exp0[:, here], exp1[:, here]).astype(F32) * stats2[0:1, lanes]
            wb[h] = w.astype(BF16)
            ds[h] = (w * (p - stats2[1:2, lanes])).astype(BF16)
        dkv1 = {
            h: side(dot(ds[h][tok:], que[h]) * scale, dot(wb[h][tok:], gra[h])).astype(BF16)
            for h in each
        }
        ngrad, dqt = {}, {}

        def here_rows(value):
            return stack(
                value[:n2], value[tok : tok + n3], value[n2 : 2 * n2], value[tok + n3 : tok + 2 * n3]
            )

        for h in each:
            used = slice(h * dim, h * dim + 2 * sel)
            dsm, wm = dsms[:, used], wms[:, used]
            gsel = stack(selg0[:, cols[h]], selg1[:, cols[h]])
            dk = dot(here_rows(dsm), selq[:, cols[h]]) * scale
            ngrad[h] = side(dk, dot(here_rows(wm), gsel)).astype(BF16)
            kc = slice(2 * h * dim, (2 * h + 1) * dim)
            keys = stack(*(ref[:, kc] for ref in (own2, x2, own3, x3, y3, d3)))
            dqt[h] = dot(keys.T, dsm).astype(BF16)
        for block, keys in enumerate((k0, k1)):
            at = slice(block * tok, (block + 1) * tok)
            picked = slice(block * n1, (block + 1) * n1)
            grads = slice(block * sel, (block + 1) * sel)
            kv, dq = {}, {}
            for h in each:
                place = place_matrix(offs_ref, first + h, 1, levels, tok)
                d0, w0 = ds[h][:tok, at], wb[h][:tok, at]
                kv[h] = side(dot(d0, que[h][at]) * scale, dot(w0, gra[h][at]))
                kv[h] += dot(place, stack(dkv1[h][picked], ngrad[h][grads]))
            for h in each:
                pick = pick_matrix(offs_ref, first + h, 2, levels, tok)
                kc = slice(2 * h * dim, (2 * h + 1) * dim)
                far = dqt[h][:, block * sel : (block + 1) * sel]
                both = stack(keys[:, cols[h]], near[:tok, kc])
                dq[h] = dot(both.T, ds[h][:, at]) + dot(far, pick)
            for h in each:
                part = per // PIECES
                ref, to = (others[h // part], h % part) if block else (mine, h)
                to *= 3 * dim
                ref[:, to : to + dim] = (dq[h] * scale).T.astype(BF16)
                ref[:, to + dim : to + 3 * dim] = kv[h].astype(BF16)


def near_call(offsets, core, mid, raw, grads, dim):
    tok, width = raw[0].shape
    levels, heads = offsets.shape
    half = heads // 2
    per = 8
    steps = half // per
    raw_spec = own_spec(tok, per * dim, steps)

    def mid_spec(a):
        return pl.BlockSpec((a.shape[0], a.shape[1] // steps), lambda i, o, c: (0, i))

    widths = [3 * per * dim] + [3 * per * dim // PIECES] * PIECES
    return pl.pallas_call(
        functools.partial(near_kernel, levels, per, dim),
        grid_spec=pltpu.PrefetchScalarGridSpec(
            num_scalar_prefetch=2,
            grid=(steps,),
            in_specs=[mid_spec(a) for a in mid] + [raw_spec] * 7
            + [mid_spec(a) for a in grads[1:]],
            out_specs=[pl.BlockSpec((tok, w), lambda i, o, c: (0, 0)) for w in widths],
        ),
        out_shape=[jax.ShapeDtypeStruct((tok, w), BF16) for w in widths],
        compiler_params=params(),
        name="near_levels",
    )(offsets, core, *mid, *raw, *grads)


def sum_kernel(here, there, first, second):
    total = (here[...].astype(F32) + there[...].astype(F32)).astype(BF16)
    rows = first.shape[0]
    first[...] = total[:rows]
    second[...] = total[rows:]


def sum_call(here, there):
    rows, cols = here.shape
    return pl.pallas_call(
        sum_kernel,
        out_shape=[jax.ShapeDtypeStruct((rows // 2, cols), BF16)] * 2,
        compiler_params=params(),
        name="add_diagonal",
    )(here, there)


def add_far(dim, place, bases, x, third, group):
    per = sum(base.shape[1] for base in bases) // (3 * dim)
    in_base = per // len(bases)
    for lo in range(0, per, group):
        each = range(lo, lo + group)
        src = {h: slice(2 * h * dim, 2 * (h + 1) * dim) for h in each}
        more = {h: dot(place(h), stack(x[:, src[h]], third[:, src[h]])) for h in each}
        for h in each:
            base, at = bases[h // in_base], (3 * (h % in_base) + 1) * dim
            yield h, (base[:, at : at + 2 * dim].astype(F32) + more[h]).astype(BF16)


def own_kernel(levels, per, dim, offs_ref, core_ref, base, x, y, x3, dq, dk, dv, places):
    n3 = x3.shape[0]
    third = (x3[...].astype(F32) + y[:n3].astype(F32)).astype(BF16)
    for h in range(per):
        dq[:, h * dim : (h + 1) * dim] = base[:, 3 * h * dim : (3 * h + 1) * dim]
    tok, sel = base.shape[0], 3 * n3
    far_core = 1 - core_ref[0]
    for h in range(per):
        place = place_matrix(offs_ref, far_core * per + h, 2, levels, tok)
        places[:, h * dim : h * dim + sel] = place

    def here(h):
        return place_matrix(offs_ref, core_ref[0] * per + h, 2, levels, tok)

    for h, total in add_far(dim, here, [base], x, third, per):
        cols = slice(h * dim, (h + 1) * dim)
        dk[:, cols] = total[:, :dim]
        dv[:, cols] = total[:, dim:]


def own_call(offsets, core, parts, dim):
    levels, heads = offsets.shape
    tok = parts[0].shape[0]
    per = heads // 2
    return pl.pallas_call(
        functools.partial(own_kernel, levels, per, dim),
        grid_spec=pltpu.PrefetchScalarGridSpec(
            num_scalar_prefetch=2,
            grid=(1,),
            in_specs=[pl.BlockSpec(a.shape, lambda i, o, c: (0, 0)) for a in parts],
            out_specs=[pl.BlockSpec((tok, per * dim), lambda i, o, c: (0, 0))] * 4,
        ),
        out_shape=[jax.ShapeDtypeStruct((tok, per * dim), BF16)] * 4,
        compiler_params=params(),
        name="add_own_half",
    )(offsets, core, *parts)


def final_kernel(
    levels, per, dim, offs_ref, core_ref, own_q, own_k, own_v, places, x, y, x3, *refs
):
    bases, outs, (held, sems) = refs[:PIECES], refs[PIECES : PIECES + 3], refs[-2:]
    n3 = x3.shape[0]
    copies = []

    def send(part, here, core, lo, n):
        cols = pl.ds(pl.multiple_of((core * per + lo) * dim, dim), n * dim)
        copies.append(pltpu.make_async_copy(here, outs[part].at[:, cols], sems.at[len(copies)]))
        copies[-1].start()

    for part, ref in enumerate((own_q, own_k, own_v)):
        send(part, ref, core_ref[0], 0, per)
    far_core = 1 - core_ref[0]
    each = per // PIECES
    for h in range(per):
        at = 3 * (h % each) * dim
        held[0, :, h * dim : (h + 1) * dim] = bases[h // each][:, at : at + dim]
    send(0, held.at[0], far_core, 0, per)
    third = (x3[...].astype(F32) + y[n3:].astype(F32)).astype(BF16)

    def place(h):
        return places[:, h * dim : h * dim + 3 * n3]

    for h, total in add_far(dim, place, bases, x, third, 4):
        cols = slice(h * dim, (h + 1) * dim)
        held[1, :, cols] = total[:, :dim]
        held[2, :, cols] = total[:, dim:]
        if (h + 1) % 4 == 0:
            for part in (1, 2):
                lo = h + 1 - 4
                send(part, held.at[part, :, pl.ds(lo * dim, 4 * dim)], far_core, lo, 4)
    for copy in copies:
        copy.wait()


def final_call(offsets, core, own, parts, dim):
    levels, heads = offsets.shape
    tok = own[0].shape[0]
    per = heads // 2
    away = pl.BlockSpec(memory_space=pl.ANY)
    return pl.pallas_call(
        functools.partial(final_kernel, levels, per, dim),
        grid_spec=pltpu.PrefetchScalarGridSpec(
            num_scalar_prefetch=2,
            grid=(1,),
            in_specs=[pl.BlockSpec(a.shape, lambda i, o, c: (0, 0)) for a in own + parts],
            out_specs=[away] * 3,
            scratch_shapes=[
                pltpu.VMEM((3, tok, per * dim), BF16),
                pltpu.SemaphoreType.DMA((4 + 2 * (per // 4),)),
            ],
        ),
        out_shape=[jax.ShapeDtypeStruct((tok, heads * dim), BF16)] * 3,
        compiler_params=params(),
        name="add_other_half",
    )(offsets, core, *own, *parts)


def per_device(queries, keys_in, values, out_grads, offsets):
    heads = offsets.shape[1]
    dim = queries.shape[2] // heads
    core = lax.rem(lax.axis_index("seq"), 2).astype(jnp.int32).reshape(1)
    q, k, v = queries[0], keys_in[0], values[0]
    sections = lax.axis_size("section")
    grads = lax.ppermute(
        out_grads[0], "section", [(i, (i - 1) % sections) for i in range(sections)]
    )
    q_oth, k_oth, v_oth = exchange(q, 1), exchange(k, 1), exchange(v, 1)
    kept = [pltpu.with_memory_space_constraint(a, pltpu.HBM) for a in (k, v)]
    two, three = pick_call(
        pltpu.with_memory_space_constraint(offsets, pltpu.HBM), core, kept, [k_oth, v_oth], dim
    )
    x3, y3, x2 = exchange(three, 2), exchange(three, 4), exchange(two, 2)
    d3 = exchange(x3, 4)
    raw = [q, q_oth, k, k_oth, v, v_oth]
    pre = pre_call(offsets, core, raw, dim)
    exp0, exp1, stats, near, selq = pre
    y3, grads = lax.optimization_barrier((y3, grads, stats))[:2]
    sel = grad_call(offsets, core, exp0, near, v, grads, dim)
    half = heads // 2
    cuts = [half * i // 3 for i in range(4)]
    sizes = [(hi - lo) * dim for lo, hi in zip(cuts, cuts[1:])]
    other = [exchange(piece, 1) for piece in pack_call(core, grads, sizes)]
    other = lax.optimization_barrier((*other, sel[1]))[:-1]
    xa, xb, xab, yab, dab, dsms, wms, selg1, stats2 = far_call(
        offsets, core, [stats, selq, *sel, exp1, near], v_oth,
        [two, x2, three, x3, y3, d3, *other], q.shape[0], dim,
    )
    thirds = sum_call(xab, exchange(dab, 4))
    xa, xb, y = exchange(xa, 2), exchange(xb, 3), exchange(yab, 4)
    xa3, xb3 = exchange(thirds[0], 2), exchange(thirds[1], 3)
    yy = exchange(y, 1)
    mine, *others = near_call(
        offsets, core, [exp0, exp1, stats2, near, dsms, wms, selq, sel[0], selg1, two, x2, three, x3, y3, d3], raw, [grads, *other], dim
    )
    last, xa, xb, xa3, xb3, y = lax.optimization_barrier((others[-1], xa, xb, xa3, xb3, y))
    bases = [exchange(piece, 1) for piece in (*others[:-1], last)]
    own = list(own_call(offsets, core, [mine, xa, y, xa3], dim))
    dq, dk, dv = final_call(offsets, core, own, [xb, yy, xb3, *bases], dim)
    return dq[None], dk[None], dv[None]


def solution(mesh):
    spec = P("section", "seq", None)
    return jax.shard_map(
        per_device,
        mesh=mesh,
        in_specs=(spec, spec, spec, spec, P()),
        out_specs=(spec, spec, spec),
        check_vma=False,
    )
```

```python
import functools

import jax
import jax.numpy as jnp
from jax import lax
from jax.experimental import pallas as pl
from jax.experimental.pallas import tpu as pltpu
from jax.sharding import PartitionSpec as P

F32 = jnp.float32
BF16 = jnp.bfloat16
NEG = -1e30
VMEM_LIMIT = 32 * 1024 * 1024
PIECES = 4


def params():
    return pltpu.CompilerParams(vmem_limit_bytes=VMEM_LIMIT)


def exchange(value, bits):
    count = lax.axis_size("seq")
    return lax.ppermute(value, "seq", [(i, i ^ bits) for i in range(count)])


def dot(a, b):
    return jnp.dot(a, b, preferred_element_type=F32)


def dot_nt(a, b):
    return lax.dot_general(a, b, (((1,), (1,)), ((), ())), preferred_element_type=F32)


def pick_matrix(offs_ref, head, first, levels, tok):
    parts = []
    for level in range(first, levels + 1):
        rate = 2**level
        rows = tok // rate
        kept = lax.rem(offs_ref[level - 1, head], rate)
        row = lax.broadcasted_iota(jnp.int32, (rows, tok), 0)
        col = lax.broadcasted_iota(jnp.int32, (rows, tok), 1)
        parts.append((col == row * rate + kept).astype(F32))
    return jnp.concatenate(parts, axis=0).astype(BF16)


def place_matrix(offs_ref, head, first, levels, tok):
    total = sum(tok // 2**level for level in range(first, levels + 1))
    col = lax.broadcasted_iota(jnp.int32, (1, total), 1)
    target, lo = jnp.zeros_like(col), 0
    for level in range(first, levels + 1):
        rate = 2**level
        kept = lax.rem(offs_ref[level - 1, head], rate)
        target = jnp.where(col >= lo, (col - lo) * rate + kept, target)
        lo += tok // rate
    row = lax.broadcasted_iota(jnp.int32, (tok, total), 0)
    return (row == target).astype(F32).astype(BF16)


def pack_kernel(core_ref, rows, *outs):
    lo = 0
    for out in outs:
        out[...] = rows[:, lo : lo + out.shape[1]]
        lo += out.shape[1]


def pack_call(core, rows, sizes):
    tok, width = rows.shape
    half = width // 2
    return pl.pallas_call(
        pack_kernel,
        grid_spec=pltpu.PrefetchScalarGridSpec(
            num_scalar_prefetch=1,
            grid=(1,),
            in_specs=[pl.BlockSpec((tok, half), lambda i, c: (0, 1 - c[0]))],
            out_specs=[pl.BlockSpec((tok, n), lambda i, c: (0, 0)) for n in sizes],
        ),
        out_shape=[jax.ShapeDtypeStruct((tok, n), BF16) for n in sizes],
        compiler_params=params(),
        name="pack_half",
    )(core, rows)


def pick_kernel(
    levels, per, dim, core_ref, offs, k0, v0, k1, v1, two_ref, three_ref, offs_ref, own_k, own_v, sems
):
    tok = k1.shape[0]
    n2, n3 = tok // 4, tok // 8
    each = range(per)
    mine = pl.ds(pl.multiple_of(core_ref[0] * per * dim, per * dim), per * dim)
    copies = [
        pltpu.make_async_copy(src.at[:, mine], dst, sems.at[i])
        for i, (src, dst) in enumerate(((k0, own_k), (v0, own_v)))
    ]
    table = pltpu.make_async_copy(offs, offs_ref, sems.at[2])
    table.start()
    for copy in copies:
        copy.start()
    table.wait()
    picks = [pick_matrix(offs_ref, core_ref[0] * per + h, 2, levels, tok) for h in each]

    def work(keys, values, lo):
        for h in each:
            cols = slice(h * dim, (h + 1) * dim)
            out = slice(2 * h * dim, 2 * (h + 1) * dim)
            got = dot(picks[h], side(keys[:, cols], values[:, cols])).astype(BF16)
            two_ref[lo * n2 : (lo + 1) * n2, out] = got[:n2]
            three_ref[lo * n3 : (lo + 1) * n3, out] = got[n2:]

    work(k1, v1, 1)
    for copy in copies:
        copy.wait()
    work(own_k, own_v, 0)


def pick_call(offsets, core, own, other, dim):
    tok, width = own[0].shape
    levels, heads = offsets.shape
    per = heads // 2
    spec = pl.BlockSpec((tok, per * dim), lambda i, c: (0, c[0]))

    def out(rows):
        return pl.BlockSpec((rows, 2 * per * dim), lambda i, c: (0, 0))

    rows = [tok // 2, tok // 4]
    return pl.pallas_call(
        functools.partial(pick_kernel, levels, per, dim),
        grid_spec=pltpu.PrefetchScalarGridSpec(
            num_scalar_prefetch=1,
            grid=(1,),
            in_specs=[pl.BlockSpec(memory_space=pl.ANY)] * 3 + [spec] * 2,
            out_specs=[out(r) for r in rows],
            scratch_shapes=[pltpu.SMEM((levels, heads), jnp.int32)]
            + [pltpu.VMEM((tok, per * dim), BF16)] * 2
            + [pltpu.SemaphoreType.DMA((3,))],
        ),
        out_shape=[jax.ShapeDtypeStruct((r, width), BF16) for r in rows],
        compiler_params=params(),
        name="pick_rows",
    )(core, offsets, *own, *other)


def own_spec(tok, cols, steps):
    return pl.BlockSpec((tok, cols), lambda i, o, c: (0, c[0] * steps + i))


def side(*values):
    return jnp.concatenate(values, axis=1)


def stack(*values):
    return jnp.concatenate(values, axis=0)


def split(value, terms):
    parts = []
    for _ in range(terms):
        part = value.astype(BF16)
        parts.append(part)
        value = value - part.astype(F32)
    return parts


def local_scores(pick, levels, offs_ref, head, key0, key1, ones, que0, que1):
    tok, dim = key0.shape
    pos = lax.broadcasted_iota(jnp.int32, (1, 2 * tok), 1)
    bias = jnp.where(lax.rem(pos, 2) == lax.rem(offs_ref[0, head], 2), 0.0, NEG).astype(F32)
    s0 = side(dot_nt(key0, que0), dot_nt(key1, que1)) * dim**-0.5
    s1 = dot_nt(ones, stack(que0, que1)) * dim**-0.5 + bias
    return stack(s0, s1)


def pre_kernel(
    levels, per, dim, offs_ref, core_ref, q0, q1, k0, k1, v0, v1, exp0, exp1, stats, near, selq
):
    tok = q0.shape[0]
    n1 = tok // 2
    heads = per * pl.num_programs(0)
    for h in range(per):
        head = core_ref[0] * heads + pl.program_id(0) * per + h
        pick = pick_matrix(offs_ref, head, 1, levels, tok)
        cols = slice(h * dim, (h + 1) * dim)
        wide = slice(2 * h * dim, 2 * (h + 1) * dim)
        lanes = slice(2 * h * tok, 2 * (h + 1) * tok)
        own = dot(pick[:n1], side(k0[:, cols], v0[:, cols])).astype(BF16)
        oth = dot(pick[:n1], side(k1[:, cols], v1[:, cols])).astype(BF16)
        ones = stack(own, oth)
        near[:, wide] = ones
        que0, que1 = q0[:, cols], q1[:, cols]
        far_pick = pick[n1:]
        selq[:, cols] = stack(dot(far_pick, que0), dot(far_pick, que1)).astype(BF16)
        s = local_scores(
            pick, levels, offs_ref, head, k0[:, cols], k1[:, cols], ones[:, :dim], que0, que1
        )
        top = jnp.max(s, axis=0, keepdims=True)
        e = jnp.exp(s - top)
        for half, ref in enumerate((exp0, exp1)):
            ref[:, h * tok : (h + 1) * tok] = e[:, half * tok : (half + 1) * tok].astype(BF16)
        stats[0:1, lanes] = top
        stats[1:2, lanes] = jnp.sum(e, axis=0, keepdims=True)


def pre_call(offsets, core, raw, dim):
    tok, width = raw[0].shape
    levels, heads = offsets.shape
    half = heads // 2
    per = 8
    steps = half // per
    raw_spec = own_spec(tok, per * dim, steps)
    sel = 2 * (tok // 4 + tok // 8)

    def out(rows, lanes, kind=BF16):
        return (
            pl.BlockSpec((rows, per * lanes), lambda i, o, c: (0, i)),
            jax.ShapeDtypeStruct((rows, half * lanes), kind),
        )

    outs = [out(2 * tok, tok), out(2 * tok, tok), out(8, 2 * tok, F32), out(tok, 2 * dim), out(sel, dim)]
    return pl.pallas_call(
        functools.partial(pre_kernel, levels, per, dim),
        grid_spec=pltpu.PrefetchScalarGridSpec(
            num_scalar_prefetch=2,
            grid=(steps,),
            in_specs=[raw_spec] * 6,
            out_specs=[o[0] for o in outs],
        ),
        out_shape=[o[1] for o in outs],
        compiler_params=params(),
        name="local_scores",
    )(offsets, core, *raw)


def local_delta(exps, values, ones, grads):
    tok = values.shape[0]
    p0, p1 = dot_nt(values, grads), dot_nt(ones, grads)
    both = exps[:tok].astype(F32) * p0 + exps[tok:].astype(F32) * p1
    return jnp.sum(both, axis=0, keepdims=True)


def grad_kernel(levels, per, dim, offs_ref, core_ref, exps, near, values, grads, selg, local):
    tok = values.shape[0]
    first = core_ref[0] * per
    each = range(per)
    cols = [slice(h * dim, (h + 1) * dim) for h in each]
    picks = [pick_matrix(offs_ref, first + h, 2, levels, tok) for h in each]
    rows = [dot(picks[h], grads[:, cols[h]]).astype(BF16) for h in each]
    vc = [slice((2 * h + 1) * dim, (2 * h + 2) * dim) for h in each]
    p0 = [dot_nt(values[:, cols[h]], grads[:, cols[h]]) for h in each]
    p1 = [dot_nt(near[:, vc[h]], grads[:, cols[h]]) for h in each]
    for h in each:
        here = slice(h * tok, (h + 1) * tok)
        selg[:, cols[h]] = rows[h]
        both = exps[:tok, here].astype(F32) * p0[h] + exps[tok:, here].astype(F32) * p1[h]
        local[0:1, here] = jnp.sum(both, axis=0, keepdims=True)


def grad_call(offsets, core, exps, near, values, grads, dim):
    tok, width = values.shape
    levels, heads = offsets.shape
    per = heads // 2
    raw_spec = own_spec(tok, per * dim, 1)

    def whole(a):
        return pl.BlockSpec(a.shape, lambda i, o, c: (0, 0))

    outs = [
        jax.ShapeDtypeStruct((tok // 4 + tok // 8, per * dim), BF16),
        jax.ShapeDtypeStruct((8, per * tok), F32),
    ]
    return pl.pallas_call(
        functools.partial(grad_kernel, levels, per, dim),
        grid_spec=pltpu.PrefetchScalarGridSpec(
            num_scalar_prefetch=2,
            grid=(1,),
            in_specs=[whole(exps), whole(near), raw_spec, raw_spec],
            out_specs=[whole(a) for a in outs],
        ),
        out_shape=outs,
        compiler_params=params(),
        name="own_delta",
    )(offsets, core, exps, near, values, grads)


def far_kernel(
    levels, per, dim, offs_ref, core_ref, stats, selq, selg0, local0, exp1, near, v1,
    own2, x2, own3, x3, y3, d3, *refs
):
    xa, xb, xab, yab, dab, dsms, wms, selg1, stats2 = refs[-9:]
    g1 = side(*(ref[...] for ref in refs[:-9]))
    tok = g1.shape[0]
    n1, n2, n3 = tok // 2, tok // 4, tok // 8
    sel = n2 + n3
    scale = dim**-0.5
    heads = per * pl.num_programs(0)
    lane = lax.broadcasted_iota(jnp.int32, (1, 2 * sel), 1)
    is2 = lax.rem(lane, sel) < n2
    pos = lax.broadcasted_iota(jnp.int32, (1, 2 * tok), 1)
    first = core_ref[0] * heads + pl.program_id(0) * per
    each = range(per)
    cols = [slice(h * dim, (h + 1) * dim) for h in each]
    kc = [slice(2 * h * dim, (2 * h + 1) * dim) for h in each]
    vc = [slice((2 * h + 1) * dim, (2 * h + 2) * dim) for h in each]
    wide = [slice(2 * h * dim, 2 * (h + 1) * dim) for h in each]
    lanes = [slice(2 * h * tok, 2 * (h + 1) * tok) for h in each]

    def rows(c):
        return stack(*(ref[:, c] for ref in (own2, x2, own3, x3, y3, d3)))

    def level_pick(value):
        return jnp.where(is2, value[:tok], value[tok:])

    picks = [pick_matrix(offs_ref, first + h, 2, levels, tok) for h in each]
    selg = [
        stack(selg0[:, cols[h]], dot(picks[h], g1[:, cols[h]]).astype(BF16)) for h in each
    ]
    keys = [rows(kc[h]) for h in each]
    s = [level_pick(dot_nt(keys[h], selq[:, cols[h]])) * scale for h in each]
    p = [level_pick(dot_nt(rows(vc[h]), selg[h])) for h in each]
    local1 = [
        local_delta(exp1[:, h * tok : (h + 1) * tok], v1[:, cols[h]], near[:, vc[h]], g1[:, cols[h]])
        for h in each
    ]
    top = [jnp.max(a, axis=0, keepdims=True) for a in s]
    e = [jnp.exp(a - b) for a, b in zip(s, top)]
    size = [jnp.sum(a, axis=0, keepdims=True) for a in e]
    dhat = [jnp.sum(a * b, axis=0, keepdims=True) for a, b in zip(e, p)]
    none = jnp.zeros_like(picks[0])
    spots = [stack(side(a, none), side(none, a)) for a in picks]
    spread = []
    for h in each:
        terms = stack(*split(top[h], 3), *split(size[h], 2), *split(dhat[h], 3))
        zero = jnp.zeros_like(terms)
        apart = stack(jnp.where(is2, terms, zero), jnp.where(is2, zero, terms))
        spread.append(dot(apart, spots[h]))
    back = []
    for h in each:

        def level_stats(level, lo):
            rate = 2**level
            on = lax.rem(pos, rate) == lax.rem(offs_ref[level - 1, first + h], rate)
            t = [spread[h][lo + i : lo + i + 1] for i in range(8)]
            return jnp.where(on, t[0] + t[1] + t[2], NEG), t[3] + t[4], t[5] + t[6] + t[7]

        t1, z1 = stats[0:1, lanes[h]], stats[1:2, lanes[h]]
        t2, z2, dot2 = level_stats(2, 0)
        t3, z3, dot3 = level_stats(3, 8)
        high = jnp.maximum(t1, jnp.maximum(t2, t3))
        a1, a2, a3 = jnp.exp(t1 - high), jnp.exp(t2 - high), jnp.exp(t3 - high)
        inv = 1.0 / (a1 * z1 + a2 * z2 + a3 * z3)
        f1, f2, f3 = a1 * inv, a2 * inv, a3 * inv
        delta = f1 * side(local0[0:1, h * tok : (h + 1) * tok], local1[h]) + f2 * dot2 + f3 * dot3
        stats2[0:1, lanes[h]] = f1
        stats2[1:2, lanes[h]] = delta
        terms = stack(*split(f2, 2), *split(f3, 2), *split(delta, 3))
        back.append(dot_nt(terms, spots[h]))

    def apart(value):
        value = value.astype(BF16)
        zero = jnp.zeros_like(value)
        return stack(jnp.where(is2, value, zero), jnp.where(is2, zero, value))

    dsm, wm = [], []
    for h in each:
        b = back[h]
        w = e[h] * jnp.where(is2, b[0:1] + b[1:2], b[2:3] + b[3:4])
        dsm.append(apart(w * (p[h] - (b[4:5] + b[5:6] + b[6:7]))))
        wm.append(apart(w))
    def away(value):
        return stack(value[2 * n2 : tok], value[tok + 2 * n3 :])

    dk = [dot(away(dsm[h]), selq[:, cols[h]]) * scale for h in each]
    dv = [dot(away(wm[h]), selg[h]) for h in each]
    for h in each:
        dkv = side(dk[h], dv[h]).astype(BF16)
        xa[:, wide[h]] = dkv[:n2]
        xb[:, wide[h]] = dkv[n2 : 2 * n2]
        for i, ref in enumerate((xab, yab, dab)):
            lo = 2 * n2 + 2 * i * n3
            ref[:, wide[h]] = dkv[lo : lo + 2 * n3]
        dsms[:, h * dim : h * dim + 2 * sel] = dsm[h]
        wms[:, h * dim : h * dim + 2 * sel] = wm[h]
        selg1[:, cols[h]] = selg[h][sel:]


def far_call(offsets, core, mid, value, far, tok, dim):
    levels, heads = offsets.shape
    half = heads // 2
    per = 8
    steps = half // per
    n2, n3 = tok // 4, tok // 8

    def mid_spec(a):
        return pl.BlockSpec((a.shape[0], a.shape[1] // steps), lambda i, o, c: (0, i))

    def out(rows, lanes, kind=BF16):
        return (
            pl.BlockSpec((rows, per * lanes), lambda i, o, c: (0, i)),
            jax.ShapeDtypeStruct((rows, half * lanes), kind),
        )

    outs = [out(n2, 2 * dim)] * 2 + [out(2 * n3, 2 * dim)] * 3
    outs += [out(2 * tok, dim)] * 2 + [out(n2 + n3, dim), out(8, 2 * tok, F32)]
    return pl.pallas_call(
        functools.partial(far_kernel, levels, per, dim),
        grid_spec=pltpu.PrefetchScalarGridSpec(
            num_scalar_prefetch=2,
            grid=(steps,),
            in_specs=[mid_spec(a) for a in mid]
            + [own_spec(tok, per * dim, steps)]
            + [mid_spec(a) for a in far],
            out_specs=[o[0] for o in outs],
        ),
        out_shape=[o[1] for o in outs],
        compiler_params=params(),
        name="far_levels",
    )(offsets, core, *mid, value, *far)


def near_kernel(
    levels, per, dim, offs_ref, core_ref, exp0, exp1, stats2, near, dsms, wms, selq, selg0, selg1,
    own2, x2, own3, x3, y3, d3,
    q0, q1, k0, k1, v0, v1, g0, *refs,
):
    mine, *others = refs[-1 - PIECES :]
    g1 = side(*(ref[...] for ref in refs[: -1 - PIECES]))
    tok = q0.shape[0]
    n1 = tok // 2
    n2, n3 = tok // 4, tok // 8
    sel = n2 + n3
    scale = dim**-0.5
    heads = per * pl.num_programs(0)
    first = core_ref[0] * heads + pl.program_id(0) * per
    for lo in range(0, per, 4):
        each = range(lo, lo + 4)
        cols = {h: slice(h * dim, (h + 1) * dim) for h in each}
        vc = {h: slice((2 * h + 1) * dim, (2 * h + 2) * dim) for h in each}
        gra = {h: stack(g0[:, cols[h]], g1[:, cols[h]]) for h in each}
        que = {h: stack(q0[:, cols[h]], q1[:, cols[h]]) for h in each}
        wb, ds = {}, {}
        for h in each:
            lanes = slice(2 * h * tok, 2 * (h + 1) * tok)
            here = slice(h * tok, (h + 1) * tok)
            p0 = dot_nt(v0[:, cols[h]], gra[h][:tok])
            p1 = dot_nt(v1[:, cols[h]], gra[h][tok:])
            p = stack(side(p0, p1), dot_nt(near[:tok, vc[h]], gra[h]))
            w = side(exp0[:, here], exp1[:, here]).astype(F32) * stats2[0:1, lanes]
            wb[h] = w.astype(BF16)
            ds[h] = (w * (p - stats2[1:2, lanes])).astype(BF16)
        dkv1 = {
            h: side(dot(ds[h][tok:], que[h]) * scale, dot(wb[h][tok:], gra[h])).astype(BF16)
            for h in each
        }
        ngrad, dqt = {}, {}

        def here_rows(value):
            return stack(
                value[:n2], value[tok : tok + n3], value[n2 : 2 * n2], value[tok + n3 : tok + 2 * n3]
            )

        for h in each:
            used = slice(h * dim, h * dim + 2 * sel)
            dsm, wm = dsms[:, used], wms[:, used]
            gsel = stack(selg0[:, cols[h]], selg1[:, cols[h]])
            dk = dot(here_rows(dsm), selq[:, cols[h]]) * scale
            ngrad[h] = side(dk, dot(here_rows(wm), gsel)).astype(BF16)
            kc = slice(2 * h * dim, (2 * h + 1) * dim)
            keys = stack(*(ref[:, kc] for ref in (own2, x2, own3, x3, y3, d3)))
            dqt[h] = dot(keys.T, dsm).astype(BF16)
        for block, keys in enumerate((k0, k1)):
            at = slice(block * tok, (block + 1) * tok)
            picked = slice(block * n1, (block + 1) * n1)
            grads = slice(block * sel, (block + 1) * sel)
            kv, dq = {}, {}
            for h in each:
                place = place_matrix(offs_ref, first + h, 1, levels, tok)
                d0, w0 = ds[h][:tok, at], wb[h][:tok, at]
                kv[h] = side(dot(d0, que[h][at]) * scale, dot(w0, gra[h][at]))
                kv[h] += dot(place, stack(dkv1[h][picked], ngrad[h][grads]))
            for h in each:
                pick = pick_matrix(offs_ref, first + h, 2, levels, tok)
                kc = slice(2 * h * dim, (2 * h + 1) * dim)
                far = dqt[h][:, block * sel : (block + 1) * sel]
                both = stack(keys[:, cols[h]], near[:tok, kc])
                dq[h] = dot(both.T, ds[h][:, at]) + dot(far, pick)
            for h in each:
                part = per // PIECES
                ref, to = (others[h // part], h % part) if block else (mine, h)
                to *= 3 * dim
                ref[:, to : to + dim] = (dq[h] * scale).T.astype(BF16)
                ref[:, to + dim : to + 3 * dim] = kv[h].astype(BF16)


def near_call(offsets, core, mid, raw, grads, dim):
    tok, width = raw[0].shape
    levels, heads = offsets.shape
    half = heads // 2
    per = 8
    steps = half // per
    raw_spec = own_spec(tok, per * dim, steps)

    def mid_spec(a):
        return pl.BlockSpec((a.shape[0], a.shape[1] // steps), lambda i, o, c: (0, i))

    widths = [3 * per * dim] + [3 * per * dim // PIECES] * PIECES
    return pl.pallas_call(
        functools.partial(near_kernel, levels, per, dim),
        grid_spec=pltpu.PrefetchScalarGridSpec(
            num_scalar_prefetch=2,
            grid=(steps,),
            in_specs=[mid_spec(a) for a in mid] + [raw_spec] * 7
            + [mid_spec(a) for a in grads[1:]],
            out_specs=[pl.BlockSpec((tok, w), lambda i, o, c: (0, 0)) for w in widths],
        ),
        out_shape=[jax.ShapeDtypeStruct((tok, w), BF16) for w in widths],
        compiler_params=params(),
        name="near_levels",
    )(offsets, core, *mid, *raw, *grads)


def sum_kernel(here, there, first, second):
    total = (here[...].astype(F32) + there[...].astype(F32)).astype(BF16)
    rows = first.shape[0]
    first[...] = total[:rows]
    second[...] = total[rows:]


def sum_call(here, there):
    rows, cols = here.shape
    return pl.pallas_call(
        sum_kernel,
        out_shape=[jax.ShapeDtypeStruct((rows // 2, cols), BF16)] * 2,
        compiler_params=params(),
        name="add_diagonal",
    )(here, there)


def add_far(dim, place, bases, x, third, group):
    per = sum(base.shape[1] for base in bases) // (3 * dim)
    in_base = per // len(bases)
    for lo in range(0, per, group):
        each = range(lo, lo + group)
        src = {h: slice(2 * h * dim, 2 * (h + 1) * dim) for h in each}
        more = {h: dot(place(h), stack(x[:, src[h]], third[:, src[h]])) for h in each}
        for h in each:
            base, at = bases[h // in_base], (3 * (h % in_base) + 1) * dim
            yield h, (base[:, at : at + 2 * dim].astype(F32) + more[h]).astype(BF16)


def own_kernel(levels, per, dim, offs_ref, core_ref, base, x, y, x3, dq, dk, dv, places):
    n3 = x3.shape[0]
    third = (x3[...].astype(F32) + y[:n3].astype(F32)).astype(BF16)
    for h in range(per):
        dq[:, h * dim : (h + 1) * dim] = base[:, 3 * h * dim : (3 * h + 1) * dim]
    tok, sel = base.shape[0], 3 * n3
    far_core = 1 - core_ref[0]
    for h in range(per):
        place = place_matrix(offs_ref, far_core * per + h, 2, levels, tok)
        places[:, h * dim : h * dim + sel] = place

    def here(h):
        return place_matrix(offs_ref, core_ref[0] * per + h, 2, levels, tok)

    for h, total in add_far(dim, here, [base], x, third, per):
        cols = slice(h * dim, (h + 1) * dim)
        dk[:, cols] = total[:, :dim]
        dv[:, cols] = total[:, dim:]


def own_call(offsets, core, parts, dim):
    levels, heads = offsets.shape
    tok = parts[0].shape[0]
    per = heads // 2
    return pl.pallas_call(
        functools.partial(own_kernel, levels, per, dim),
        grid_spec=pltpu.PrefetchScalarGridSpec(
            num_scalar_prefetch=2,
            grid=(1,),
            in_specs=[pl.BlockSpec(a.shape, lambda i, o, c: (0, 0)) for a in parts],
            out_specs=[pl.BlockSpec((tok, per * dim), lambda i, o, c: (0, 0))] * 4,
        ),
        out_shape=[jax.ShapeDtypeStruct((tok, per * dim), BF16)] * 4,
        compiler_params=params(),
        name="add_own_half",
    )(offsets, core, *parts)


def final_kernel(
    levels, per, dim, offs_ref, core_ref, own_q, own_k, own_v, places, x, y, x3, *refs
):
    bases, outs, (held, sems) = refs[:PIECES], refs[PIECES : PIECES + 3], refs[-2:]
    n3 = x3.shape[0]
    copies = []

    def send(part, here, core, lo, n):
        cols = pl.ds(pl.multiple_of((core * per + lo) * dim, dim), n * dim)
        copies.append(pltpu.make_async_copy(here, outs[part].at[:, cols], sems.at[len(copies)]))
        copies[-1].start()

    for part, ref in enumerate((own_q, own_k, own_v)):
        send(part, ref, core_ref[0], 0, per)
    far_core = 1 - core_ref[0]
    each = per // PIECES
    for h in range(per):
        at = 3 * (h % each) * dim
        held[0, :, h * dim : (h + 1) * dim] = bases[h // each][:, at : at + dim]
    send(0, held.at[0], far_core, 0, per)
    third = (x3[...].astype(F32) + y[n3:].astype(F32)).astype(BF16)

    def place(h):
        return places[:, h * dim : h * dim + 3 * n3]

    for h, total in add_far(dim, place, bases, x, third, 4):
        cols = slice(h * dim, (h + 1) * dim)
        held[1, :, cols] = total[:, :dim]
        held[2, :, cols] = total[:, dim:]
        if (h + 1) % 4 == 0:
            for part in (1, 2):
                lo = h + 1 - 4
                send(part, held.at[part, :, pl.ds(lo * dim, 4 * dim)], far_core, lo, 4)
    for copy in copies:
        copy.wait()


def final_call(offsets, core, own, parts, dim):
    levels, heads = offsets.shape
    tok = own[0].shape[0]
    per = heads // 2
    away = pl.BlockSpec(memory_space=pl.ANY)
    return pl.pallas_call(
        functools.partial(final_kernel, levels, per, dim),
        grid_spec=pltpu.PrefetchScalarGridSpec(
            num_scalar_prefetch=2,
            grid=(1,),
            in_specs=[pl.BlockSpec(a.shape, lambda i, o, c: (0, 0)) for a in own + parts],
            out_specs=[away] * 3,
            scratch_shapes=[
                pltpu.VMEM((3, tok, per * dim), BF16),
                pltpu.SemaphoreType.DMA((4 + 2 * (per // 4),)),
            ],
        ),
        out_shape=[jax.ShapeDtypeStruct((tok, heads * dim), BF16)] * 3,
        compiler_params=params(),
        name="add_other_half",
    )(offsets, core, *own, *parts)


def per_device(queries, keys_in, values, out_grads, offsets):
    heads = offsets.shape[1]
    dim = queries.shape[2] // heads
    core = lax.rem(lax.axis_index("seq"), 2).astype(jnp.int32).reshape(1)
    q, k, v = queries[0], keys_in[0], values[0]
    sections = lax.axis_size("section")
    grads = lax.ppermute(
        out_grads[0], "section", [(i, (i - 1) % sections) for i in range(sections)]
    )
    q_oth, k_oth, v_oth = exchange(q, 1), exchange(k, 1), exchange(v, 1)
    kept = [pltpu.with_memory_space_constraint(a, pltpu.HBM) for a in (k, v)]
    two, three = pick_call(
        pltpu.with_memory_space_constraint(offsets, pltpu.HBM), core, kept, [k_oth, v_oth], dim
    )
    x3, y3, x2 = exchange(three, 2), exchange(three, 4), exchange(two, 2)
    d3 = exchange(x3, 4)
    raw = [q, q_oth, k, k_oth, v, v_oth]
    pre = pre_call(offsets, core, raw, dim)
    exp0, exp1, stats, near, selq = pre
    y3, grads = lax.optimization_barrier((y3, grads, stats))[:2]
    sel = grad_call(offsets, core, exp0, near, v, grads, dim)
    half = heads // 2
    cuts = [half * i // 3 for i in range(4)]
    sizes = [(hi - lo) * dim for lo, hi in zip(cuts, cuts[1:])]
    other = [exchange(piece, 1) for piece in pack_call(core, grads, sizes)]
    other = lax.optimization_barrier((*other, sel[1]))[:-1]
    xa, xb, xab, yab, dab, dsms, wms, selg1, stats2 = far_call(
        offsets, core, [stats, selq, *sel, exp1, near], v_oth,
        [two, x2, three, x3, y3, d3, *other], q.shape[0], dim,
    )
    thirds = sum_call(xab, exchange(dab, 4))
    xa, xb, y = exchange(xa, 2), exchange(xb, 3), exchange(yab, 4)
    xa3, xb3 = exchange(thirds[0], 2), exchange(thirds[1], 3)
    yy = exchange(y, 1)
    mine, *others = near_call(
        offsets, core, [exp0, exp1, stats2, near, dsms, wms, selq, sel[0], selg1, two, x2, three, x3, y3, d3], raw, [grads, *other], dim
    )
    last, xa, xb, xa3, xb3, y = lax.optimization_barrier((others[-1], xa, xb, xa3, xb3, y))
    bases = [exchange(piece, 1) for piece in (*others[:-1], last)]
    own = list(own_call(offsets, core, [mine, xa, y, xa3], dim))
    dq, dk, dv = final_call(offsets, core, own, [xb, yy, xb3, *bases], dim)
    return dq[None], dk[None], dv[None]


def solution(mesh):
    spec = P("section", "seq", None)
    return jax.shard_map(
        per_device,
        mesh=mesh,
        in_specs=(spec, spec, spec, spec, P()),
        out_specs=(spec, spec, spec),
        check_vma=False,
    )
```
